32 devices in a mesh: seq: 8 (over y, x, core), fsdp: 4 (over z).
Axes of the slice: x: 2, y: 2, z: 4, core: 2. Of those that a mesh axis runs over, the one named last changes fastest.
Arguments:
- activations: bfloat16 [4, 1024, 768], P('fsdp', 'seq'), may hold values from -6 to 6
- segments: int32 [4, 1024], P('fsdp', 'seq'), may hold values from 0 to 1, never falling along the last dimension, each value on 1 to 768 neighbouring positions
- cotangent: bfloat16 [4, 1024, 768], P('fsdp', 'seq'), may hold values from -6 to 6
- attention_gain: bfloat16 [768], P('fsdp'), may hold values from 0.5 to 1.5
- query_weight: bfloat16 [768, 768], P('fsdp'), may hold values from -0.109375 to 0.109375
- key_weight: bfloat16 [768, 768], P('fsdp'), may hold values from -0.109375 to 0.109375
- value_weight: bfloat16 [768, 768], P('fsdp'), may hold values from -0.21875 to 0.21875
- output_weight: bfloat16 [768, 768], P('fsdp'), may hold values from -1.75 to 1.75
- bias_table: bfloat16 [32, 12], P('fsdp'), may hold values from -4 to 4
- feedforward_gain: bfloat16 [768], P('fsdp'), may hold values from 0.5 to 1.5
- inner_weight: bfloat16 [768, 3072], P('fsdp'), may hold values from -0.21875 to 0.21875
- outer_weight: bfloat16 [3072, 768], P('fsdp'), may hold values from -0.109375 to 0.109375
Outputs:
- layer_output: float32 [4, 1024, 768], P('fsdp', 'seq')
- input_gradient: float32 [4, 1024, 768], P('fsdp', 'seq')
- attention_gain_grad: float32 [768], P(('seq', 'fsdp'))
- query_weight_grad: float32 [768, 768], P(('seq', 'fsdp'))
- key_weight_grad: float32 [768, 768], P(('seq', 'fsdp'))
- value_weight_grad: float32 [768, 768], P(('seq', 'fsdp'))
- output_weight_grad: float32 [768, 768], P(('seq', 'fsdp'))
- bias_table_grad: float32 [32, 12], replicated
- feedforward_gain_grad: float32 [768], P(('seq', 'fsdp'))
- inner_weight_grad: float32 [768, 3072], P(('seq', 'fsdp'))
- outer_weight_grad: float32 [3072, 768], P(('seq', 'fsdp'))
The draws below stay inside these ranges and needn't reach their ends.
Inputs may be any that keep to these rules, and one draw needn't show every extreme that they name: `segments`: along each sequence the numbers never fall; each of the 2 documents has 1 to 768 tokens.
All inputs are finite; a program needn't handle non-finite values.
Results may differ from the reference program's by a relative error of at most 0.018.
Values may be sent and summed in bfloat16 or wider, within the bound.
No kernel may reach another device: no remote copies, remote signals or barrier semaphores. Data moves between devices by JAX's collectives and lax.ppermute only.
A program may use at most 192 MiB of HBM per device.

```python
import math
import jax
import jax.numpy as jnp
import numpy as np
from jax import lax

D = 768
H = 12
DH = 64
FF = 3072
NB = 32
LEN = 1024
BATCH = 4
DOCS = 2
MOST = 768


def levels(own_key, dims, split, smallest, high):
    factor_of, own = 1.0, jax.random.fold_in(own_key, 6)
    for dim, blocks in split:
        steps = jnp.exp(jax.random.uniform(jax.random.fold_in(own, dim), (blocks,), jnp.float32, smallest / len(split), high / len(split)))
        factor_of = factor_of * jnp.repeat(steps, dims[dim] // blocks).reshape([-1 if axis == dim else 1 for axis in range(len(dims))])
    return factor_of


def profile(amount, total, bound, skew):
    portions = [(1 << 20) // math.isqrt(standing ** skew) + 1 for standing in range(2, amount + 1)]
    surplus, given = total - bound - (amount - 1), [1] * (amount - 1)
    while surplus > 0:
        movable = [i for i in range(amount - 1) if given[i] < bound]
        whole, remaining = sum([portions[i] for i in movable]), surplus
        for i in movable:
            more = min(bound - given[i], max(1, remaining * portions[i] // whole), surplus)
            given[i] = given[i] + more
            surplus = surplus - more
    return np.array([bound] + given)


def ragged_sizes(stream_key, amount, total, most, slope):
    if amount == 2:
        one = jax.random.randint(stream_key, (), max(1, total - most), min(most, total - 1) + 1)
        return jnp.stack([one, total - one])
    sizes = jnp.asarray(profile(amount, total, most, slope), jnp.int32)
    couples = (amount - 1) // 2
    giver, sink = sizes[1:1 + 2 * couples:2], sizes[2:2 + 2 * couples:2]
    margin = jnp.minimum(giver - 1, most - sink)
    moved = jax.random.randint(jax.random.fold_in(stream_key, 1), (couples,), 0, 1 << 20) % (margin + 1)
    sizes = sizes.at[1:1 + 2 * couples:2].set(giver - moved).at[2:2 + 2 * couples:2].set(sink + moved)
    return sizes[jax.random.permutation(jax.random.fold_in(stream_key, 2), amount)]


def normal_values(own_key, extent, deviation, bound, cuts=(), kind=jnp.bfloat16):
    values = jax.random.normal(own_key, extent, jnp.float32) * deviation
    if len(cuts) > 0:
        values = levels(own_key, extent, cuts, -0.22, 0.18) * values
    return jnp.clip(values, min=-bound, max=bound).astype(kind)


def setup_inputs(seed: int = 0) -> dict:
    arg_keys = jax.random.split(jax.random.key(seed), 13)
    return {
        "activations": normal_values(arg_keys[0], (BATCH, LEN, D), 1.0, 6.0, ((0, 4), (1, 8))),
        "segments": jax.vmap(lambda own: jnp.searchsorted(jnp.cumsum(ragged_sizes(own, DOCS, LEN, MOST, 1)), jnp.arange(LEN), side="right"))(jax.random.split(arg_keys[1], BATCH)).reshape((BATCH, LEN)).astype(jnp.int32),
        "cotangent": normal_values(arg_keys[2], (BATCH, LEN, D), 1.0, 6.0, ((0, 4), (1, 8))),
        "attention_gain": jnp.clip(1.0 + 0.1 * jax.random.normal(arg_keys[3], (D,), jnp.float32), 0.5, 1.5).astype(jnp.bfloat16),
        "query_weight": normal_values(arg_keys[4], (D, D), (4 * D) ** -0.5, 0.109375, ((0, 4),)),
        "key_weight": normal_values(arg_keys[5], (D, D), (4 * D) ** -0.5, 0.109375, ((0, 4),)),
        "value_weight": normal_values(arg_keys[6], (D, D), D ** -0.5, 0.21875, ((0, 4),)),
        "output_weight": normal_values(arg_keys[7], (D, D), (D // 64) ** -0.5, 1.75, ((0, 4),)),
        "bias_table": normal_values(arg_keys[8], (NB, H), 1.0, 4.0, ((0, 4),)),
        "feedforward_gain": jnp.clip(1.0 + 0.1 * jax.random.normal(arg_keys[9], (D,), jnp.float32), 0.5, 1.5).astype(jnp.bfloat16),
        "inner_weight": normal_values(arg_keys[10], (D, FF), D ** -0.5, 0.21875, ((0, 4),)),
        "outer_weight": normal_values(arg_keys[11], (FF, D), FF ** -0.5, 0.109375, ((0, 4),)),
    }


@jax.custom_vjp
def low(v):
    return lax.optimization_barrier(v.astype(jnp.bfloat16)).astype(jnp.float32)

@jax.custom_vjp
def low_back(v):
    return v

def low_keep(v):
    return (low(v), None)

def low_pass(kept, grad):
    return (grad,)

def back_keep(v):
    return (v, None)

def back_low(kept, grad):
    return (low(grad),)
low.defvjp(low_keep, low_pass)
low_back.defvjp(back_keep, back_low)
epsilon = 1e-06
limits = (12, 16, 23, 32, 46, 64, 91)
highest = lax.Precision.HIGHEST

def bucket_of(offset):
    distance = jnp.abs(offset)
    farther = jnp.zeros_like(offset) + 8
    for limit in limits:
        farther = farther + (distance >= limit).astype(jnp.int32)
    nearer = jnp.where(distance < 8, distance, farther)
    return (nearer + jnp.where(offset > 0, 16, 0)).astype(jnp.int32)

def rms_scale(value, gain):
    return value * lax.rsqrt(lax.optimization_barrier(jnp.mean(value * value, axis=-1, keepdims=True)) + epsilon) * gain

def attend_sequence(query, keys, values, marks, table):
    span = query.shape[0]
    rows = min(256, span)
    positions = jnp.arange(span, dtype=jnp.int32)

    @jax.checkpoint
    def one_block(pieces):
        query_part, marks_part, first = pieces
        query_pos = first + jnp.arange(rows, dtype=jnp.int32)
        buckets = bucket_of(positions[None, :] - query_pos[:, None])
        bias = table.T[:, buckets]
        scores = jnp.einsum('qhd,khd->hqk', query_part, keys, precision=highest) + bias
        scores = low_back(scores)
        allowed = (marks_part[:, None] == marks[None, :])[None]
        probs = jax.nn.softmax(jnp.where(allowed, scores, -1e+30), axis=-1)
        return jnp.einsum('hqk,khd->qhd', low(probs), values, precision=highest)
    count = span // rows
    starts = jnp.arange(count, dtype=jnp.int32) * rows
    blocks = lax.map(one_block, (query.reshape(count, rows, H, DH), marks.reshape(count, rows), starts))
    return blocks.reshape(span, H, DH)

def layer(inputs, gain_first, query_weight, key_weight, value_weight, output_weight, table, gain_second, inner_weight, outer_weight, segments):
    batch, span = (inputs.shape[0], inputs.shape[1])
    normed = low(rms_scale(inputs, gain_first))
    query = low(low_back(jnp.einsum('bld,de->ble', normed, query_weight, precision=highest)))
    keys = low(low_back(jnp.einsum('bld,de->ble', normed, key_weight, precision=highest)))
    values = low(low_back(jnp.einsum('bld,de->ble', normed, value_weight, precision=highest)))

    def one_sequence(pieces):
        query_seq, keys_seq, values_seq, marks = pieces
        return attend_sequence(query_seq.reshape(span, H, DH), keys_seq.reshape(span, H, DH), values_seq.reshape(span, H, DH), marks, table)
    context = lax.map(one_sequence, (query, keys, values, segments)).reshape(batch, span, D)
    context = low(low_back(context))
    attended = inputs + low_back(jnp.einsum('ble,ed->bld', context, output_weight, precision=highest))
    normed_second = low(rms_scale(attended, gain_second))
    inner = low_back(jnp.einsum('bld,df->blf', normed_second, inner_weight, precision=highest))
    active = low(low_back(jax.nn.gelu(inner, approximate=False)))
    return attended + jnp.einsum('blf,fd->bld', active, outer_weight, precision=highest)

def reference(activations, segments, cotangent, attention_gain, query_weight, key_weight, value_weight, output_weight, bias_table, feedforward_gain, inner_weight, outer_weight):
    floats = tuple((a.astype(jnp.float32) for a in (activations, attention_gain, query_weight, key_weight, value_weight, output_weight, bias_table, feedforward_gain, inner_weight, outer_weight)))
    result, pullback = jax.vjp(lambda *a: layer(*a, segments), *floats)
    grads = pullback(cotangent.astype(jnp.float32))
    return (result, grads[0], grads[1], grads[2], grads[3], grads[4], grads[5], grads[6], grads[7], grads[8], grads[9])
```

```python
import functools

import jax
import jax.numpy as jnp
from jax import lax
from jax.experimental import pallas as pl
from jax.experimental.pallas import tpu as pltpu
from jax.sharding import PartitionSpec as P

D = 768
H = 12
DH = 64
GROUPS = 4
HG = H // GROUPS
CG = HG * DH

epsilon = 1e-06
FORCE_GENERIC = False
neg_fill = -1e30
limits = (12, 16, 23, 32, 46, 64, 91)
root_half = 0.7071067811865476
inv_root_tau = 0.3989422804014327
bf16 = jnp.bfloat16
f32 = jnp.float32
NT = (((1,), (1,)), ((), ()))
TN = (((0,), (0,)), ((), ()))
NN = (((1,), (0,)), ((), ()))


def mm(a, b, dims=NN):
    return lax.dot_general(a, b, dims, preferred_element_type=f32)


def bucket_of(offset):
    distance = jnp.abs(offset)
    farther = jnp.zeros_like(offset) + 8
    for limit in limits:
        farther = farther + (distance >= limit).astype(jnp.int32)
    nearer = jnp.where(distance < 8, distance, farther)
    return nearer + jnp.where(offset > 0, 16, 0)


def call(kernel, outs, args, scalars=0, scratch=(), mib=32, cost=None):
    vmem = pl.BlockSpec(memory_space=pltpu.VMEM)
    smem = pl.BlockSpec(memory_space=pltpu.SMEM)
    return pl.pallas_call(
        kernel,
        out_shape=outs,
        in_specs=[smem] * scalars + [vmem] * (len(args) - scalars),
        out_specs=jax.tree.map(lambda _: vmem, outs),
        scratch_shapes=scratch,
        compiler_params=pltpu.CompilerParams(vmem_limit_bytes=mib << 20),
        cost_estimate=None
        if cost is None
        else pl.CostEstimate(flops=cost, bytes_accessed=1 << 20, transcendentals=0),
    )(*args)


def shape(dims, kind):
    return jax.ShapeDtypeStruct(dims, kind)


def project_kernel(T, ids, x0, x1, x2, x3, w0, w1, w2, w3, wo, normed, kv, query, gains, table, W, small):
    half, f = ids[1], ids[2]
    rows = W.shape[2]
    xs, ws = (x0, x1, x2, x3), (w0, w1, w2, w3)
    for k in range(4):
        z = f ^ k
        W[z, half] = ws[k][:rows, :]
        W[z, 1 - half] = wo[k, :rows, :]
        small[z] = ws[k][rows:, :].astype(f32)
    gain = jnp.concatenate([small[z, 0:1, 0 : D // 4] for z in range(4)], axis=1)
    gains[0:1, :] = gain
    gains[1:2, :] = jnp.concatenate([small[z, 1:2, 0 : D // 4] for z in range(4)], axis=1)
    table[...] = jnp.concatenate([small[z, 8:16, 0:128] for z in range(4)], axis=0)
    weight = W[...].reshape(D, 3 * CG)
    for i in range(2):
        parts = []
        for k in (2 * i, 2 * i + 1):
            x = xs[k][:T, :].astype(f32)
            s = lax.rsqrt(jnp.mean(x * x, axis=-1, keepdims=True) + epsilon)
            parts.append((x * s * gain).astype(bf16))
        n = jnp.concatenate(parts, axis=0)
        at = slice(2 * i * T, (2 * i + 2) * T)
        normed[at, :] = n
        out = mm(n, weight)
        blank = jnp.zeros((2 * T, DH), f32)
        for h in range(HG):
            kv[h, at, :] = out[:, 128 * h : 128 * h + 128].astype(bf16)
            q = out[:, 2 * CG + DH * h : 2 * CG + DH * (h + 1)]
            query[h, at, :] = jnp.concatenate([q, blank], axis=1).astype(bf16)


def tiles_kernel(T, ids, table, tiles):
    g = ids[0]
    lane = lax.broadcasted_iota(jnp.int32, (32, 128), 1)
    m = lax.broadcasted_iota(jnp.int32, (32, 2 * T), 1)
    label = lax.broadcasted_iota(jnp.int32, (32, 2 * T), 0)
    for h in range(HG):
        column = jnp.sum(jnp.where(lane == HG * g + h, table[...], 0.0), axis=1, keepdims=True)
        for d in range(5):
            offset = T * (d - 2) - jnp.where(m < T, m, m - 2 * T)
            hot = jnp.where(bucket_of(offset) == label, column, 0.0)
            along = jnp.sum(hot, axis=0, keepdims=True)
            wide = jnp.broadcast_to(along, (T, 2 * T))
            tiles[h, d] = pltpu.roll(wide, 0, 1, stride=1, stride_axis=0)[:, :T]


def tile_of(key_at, query_at):
    return jnp.clip(key_at - query_at, -2, 2) + 2


def mark_columns(T, count, marks, columns):
    across = jnp.concatenate([marks[...], jnp.zeros((128 - marks.shape[0], 128), f32)], axis=0).T
    for t in range(count):
        columns[t] = jnp.broadcast_to(across[:, t : t + 1], (T, 128))


def masked_scores(T, scores, base, pair, h, q_at, k_at, seg_q, columns, tiles):
    pieces = []
    for t in range(8):
        kt = base + t
        bias = jnp.concatenate([tiles[h, tile_of(k_at[kt], q_at[2 * pair + j])] for j in range(2)], axis=1)
        column = jnp.concatenate([columns[kt], columns[kt]], axis=1)
        piece = scores[t * T : (t + 1) * T] + bias
        pieces.append(jnp.where(column == seg_q, piece, neg_fill))
    return jnp.concatenate(pieces, axis=0)


def pick_keys(blocks, i, h):
    if len(blocks) == 2:
        return jnp.concatenate([blocks[0][h], blocks[1][h]], axis=0)
    return jnp.concatenate([blocks[0][2 * i, h], blocks[0][2 * i + 1, h]], axis=0)


def forward_kernel(T, nb, fast, ids, q_at, k_at, query, seg_q, seg_k, tiles, *rest):
    blocks, (context, lse, columns) = rest[:-3], rest[-3:]
    mark_columns(T, nb * 4, seg_k, columns)

    def pair_step(pair, carry):
        at = pl.ds(pl.multiple_of(pair * 2 * T, 2 * T), 2 * T)
        seg = jnp.concatenate([seg_q[pl.ds(2 * pair + j, 1), :] for j in range(2)], axis=1)
        out = []
        for h in range(HG):
            q = query[h, at, :]

            def chunk(i, state):
                peak, total, acc = state
                keys = pick_keys(blocks, i, h)
                s = masked_scores(T, mm(keys, q, NT), 8 * i, pair, h, q_at, k_at, seg, columns, tiles)
                top = jnp.maximum(peak, jnp.max(s, axis=0, keepdims=True))
                p = jnp.exp(s - top)
                fade = jnp.exp(peak - top)
                total = total * fade + jnp.sum(p, axis=0, keepdims=True)
                acc = acc * fade + mm(keys, p.astype(bf16), TN)
                return top, total, acc

            start = (
                jnp.full((1, 2 * T), neg_fill, f32),
                jnp.zeros((1, 2 * T), f32),
                jnp.zeros((128, 2 * T), f32),
            )
            if fast:
                peak, total, acc = chunk(0, start)
            else:
                peak, total, acc = lax.fori_loop(0, nb // 2, chunk, start)
            out.append(acc[DH:, :] / total)
            lse[pair, h : h + 1, :] = peak + jnp.log(total)
        joined = jnp.concatenate(out, axis=0)
        context[at, :] = joined.T.astype(bf16)
        return carry

    lax.fori_loop(0, 2, pair_step, 0)


def backward_kernel(T, nb, fast, ids, q_at, k_at, query, seg_q, seg_k, tiles, lse, g0, g1, g2, g3, *rest):
    nin = 2 if fast else 1
    blocks = rest[:nin]
    if fast:
        dquery, down, doth, sums, columns, dkv = rest[nin:]
    else:
        dquery, dkv, sums, columns = rest[nin:]
    mark_columns(T, nb * 4, seg_k, columns)
    sums[...] = jnp.zeros_like(sums)
    dkv[...] = jnp.zeros_like(dkv)

    def pair_step(pair, carry):
        at = pl.ds(pl.multiple_of(pair * 2 * T, 2 * T), 2 * T)
        seg = jnp.concatenate([seg_q[pl.ds(2 * pair + j, 1), :] for j in range(2)], axis=1)
        grad = g0[at, :].astype(f32) + g1[at, :].astype(f32) + g2[at, :].astype(f32) + g3[at, :].astype(f32)
        blank = jnp.zeros((2 * T, DH), f32)
        out = []
        for h in range(HG):
            q = query[h, at, :]
            do = jnp.concatenate([blank, grad[:, DH * h : DH * (h + 1)]], axis=1).astype(bf16)
            row = lse[pair, h : h + 1, :]

            def probs_of(i):
                keys = pick_keys(blocks, i, h)
                s = masked_scores(T, mm(keys, q, NT), 8 * i, pair, h, q_at, k_at, seg, columns, tiles)
                return keys, jnp.exp(s - row), mm(keys, do, NT)

            def finish(i, keys, p, dp, delta):
                ds = p * (dp - delta)
                for t in range(8):
                    for j in range(2):
                        index = tile_of(k_at[8 * i + t], q_at[2 * pair + j])
                        sums[h, index] += ds[t * T : (t + 1) * T, j * T : (j + 1) * T]
                ds = ds.astype(bf16)
                both = jnp.concatenate([ds, p.astype(bf16)], axis=1)
                piece = mm(both, jnp.concatenate([q, do], axis=0))
                if fast:
                    dkv[h] += piece
                else:
                    dkv[2 * i, h] += piece[: 4 * T]
                    dkv[2 * i + 1, h] += piece[4 * T :]
                return mm(keys, ds, TN)[:DH, :]

            if fast:
                keys, p, dp = probs_of(0)
                delta = jnp.sum(p * dp, axis=0, keepdims=True)
                dq = finish(0, keys, p, dp, delta)
            else:

                def first(i, delta):
                    keys, p, dp = probs_of(i)
                    return delta + jnp.sum(p * dp, axis=0, keepdims=True)

                delta = lax.fori_loop(0, nb // 2, first, jnp.zeros((1, 2 * T), f32))

                def second(i, dq):
                    keys, p, dp = probs_of(i)
                    return dq + finish(i, keys, p, dp, delta)

                dq = lax.fori_loop(0, nb // 2, second, jnp.zeros((DH, 2 * T), f32))
            out.append(dq)
        dquery[at, :] = jnp.concatenate(out, axis=0).T.astype(bf16)
        return carry

    lax.fori_loop(0, 2, pair_step, 0)
    if fast:
        for h in range(HG):
            down[h] = dkv[h, : 4 * T, :]
            doth[h] = dkv[h, 4 * T :, :].astype(bf16)


def table_kernel(T, ids, sums, out):
    g = ids[0]
    j = lax.broadcasted_iota(jnp.int32, (T, T), 0)
    i = lax.broadcasted_iota(jnp.int32, (T, T), 1)
    rows = []
    for h in range(HG):
        near = [sums[h, 1], sums[h, 2], sums[h, 3]]
        maps = [bucket_of(j - i + T * d) for d in (-1, 0, 1)]
        parts = []
        for n in range(32):
            value = jnp.zeros((1, T), f32)
            if n == 15:
                value = value + jnp.sum(sums[h, 0], axis=0, keepdims=True)
            if n == 31:
                value = value + jnp.sum(sums[h, 4], axis=0, keepdims=True)
            for d in range(3):
                if (d == 0 and n > 15) or (d == 2 and n < 16):
                    continue
                value = value + jnp.sum(jnp.where(maps[d] == n, near[d], 0.0), axis=0, keepdims=True)
            parts.append(value)
        stacked = jnp.concatenate(parts, axis=0).T
        rows.append(jnp.sum(stacked, axis=0, keepdims=True))
    pieces = []
    for a in range(GROUPS):
        for h in range(HG):
            pieces.append(jnp.where(g == a, rows[h], 0.0))
    out[...] = jnp.concatenate(pieces, axis=1)


def middle_kernel(T, ids, *refs):
    g, half, f = ids[0], ids[1], ids[2]
    xs, cots, ctxs, ws = refs[0:4], refs[4:8], refs[8:12], refs[12:16]
    other, gains = refs[16], refs[17]
    res0, sends = refs[18], refs[19:22]
    gcs = refs[22:26]
    grads, normed, active, ginner, branch, gain_grad = refs[26:32]
    WO, W1, W2, attended = refs[32:36]
    rows = ws[0].shape[0] // 3
    FH = W1.shape[3]
    for k in range(4):
        z = f ^ k
        for own in (True, False):
            at = half if own else 1 - half
            block = ws[k][...] if own else other[k]
            WO[z, at] = block[:rows]
            W1[at, z] = block[rows : 2 * rows]
            W2[at, z, :, 0 : D // 2] = block[2 * rows : 2 * rows + rows // 2]
            W2[at, z, :, D // 2 :] = block[2 * rows + rows // 2 :]
    gain = gains[1:2, :]
    gain_grad[...] = jnp.zeros_like(gain_grad)

    def out_rows(k):
        return jnp.concatenate([WO[g ^ k, 0], WO[g ^ k, 1]], axis=1)

    def step(i, carry):
        at = slice(2 * i * T, (2 * i + 2) * T)
        slots = (2 * i, 2 * i + 1)
        att = jnp.concatenate([xs[m][:T, :] for m in slots], axis=0).astype(f32)
        cot = jnp.concatenate([cots[m][...] for m in slots], axis=0)
        for k in range(4):
            ctx = jnp.concatenate([ctxs[k][(m ^ k) * T : (m ^ k) * T + T, :] for m in slots], axis=0)
            att = att + mm(ctx, out_rows(k))
        s = lax.rsqrt(jnp.mean(att * att, axis=-1, keepdims=True) + epsilon)
        n = (att * s * gain).astype(bf16)
        normed[at, :] = n
        result = None
        gn = None
        for c in range(2):
            columns = slice(c * FH, (c + 1) * FH)
            w1 = W1[c].reshape(D, FH)
            w2 = W2[c].reshape(FH, D)
            inner = mm(n, w1)
            cdf = 0.5 * (1.0 + lax.erf(inner * root_half))
            act = (inner * cdf).astype(bf16)
            slope = cdf + inner * jnp.exp(-0.5 * inner * inner) * inv_root_tau
            part = mm(act, w2)
            result = part if result is None else result + part
            ga = mm(cot, w2, NT).astype(bf16)
            gi = (ga.astype(f32) * slope).astype(bf16)
            part = mm(gi, w1, NT)
            gn = part if gn is None else gn + part
            active[at, columns] = act
            ginner[at, columns] = gi
        for index, m in enumerate(slots):
            piece = result[index * T : (index + 1) * T]
            if m == 0:
                res0[...] = att[:T] + piece
            else:
                sends[m - 1][...] = piece.astype(bf16)
        u = gn * gain
        gain_grad[...] += jnp.sum(gn * att * s, axis=0, keepdims=True)
        grad = 0.25 * cot.astype(f32) + s * u - att * (s * s * s) * jnp.mean(u * att, axis=-1, keepdims=True)
        grads[at, :] = grad
        gb = grad.astype(bf16)
        branch[at, :] = gb
        for k in range(4):
            gc = mm(gb, out_rows(k), NT).astype(bf16)
            for index, m in enumerate(slots):
                gcs[k][(m ^ k) * T : (m ^ k) * T + T, :] = gc[index * T : (index + 1) * T]
        return carry

    for i in range(2):
        step(i, 0)


def weight_kernel(T, ids, *refs):
    g, c = ids[0], ids[3]
    normed, active, ginner, branch = refs[0:4]
    cots, ctxs = refs[4:8], refs[8:12]
    keep, send, gi, go, gw = refs[12:17]
    R = D // 8
    gi[...] = mm(normed[...], ginner[...], TN).reshape(4, 2, R, D)
    cot = jnp.concatenate([r[...] for r in cots], axis=0)
    go[...] = mm(active[...], cot, TN).reshape(2, 4, R, D)
    gb = branch[...]
    for k in range(4):
        ctx = jnp.concatenate([ctxs[k][(m ^ k) * T : (m ^ k) * T + T, :] for m in range(4)], axis=0)
        gw[g ^ k] = mm(ctx, gb, TN).reshape(2, R, D)
    for a in range(4):
        keep[0, a] = gi[a, c]
        keep[1, a] = go[c, a]
        keep[2, a] = gw[a, c]
        send[0, a] = gi[a, 1 - c].astype(bf16)
        send[1, a] = go[1 - c, a].astype(bf16)
        send[2, a] = gw[a, 1 - c].astype(bf16)


def tail_kernel(T, ids, x0, x1, x2, x3, dq, down, doth, grads, gains, w0, w1, w2, w3, wo, own, s1, s2, s3, joined, gain_grad, W):
    half, f = ids[1], ids[2]
    rows = W.shape[2]
    xs, ws, sends = (x0, x1, x2, x3), (w0, w1, w2, w3), (s1, s2, s3)
    for k in range(4):
        z = f ^ k
        W[z, half] = ws[k][:rows, :]
        W[z, 1 - half] = wo[k, :rows, :]
    weight = W[...].reshape(D, 3 * CG)
    gain = gains[0:1, :]
    gain_grad[...] = jnp.zeros_like(gain_grad)
    for i in range(2):
        at = slice(2 * i * T, (2 * i + 2) * T)
        parts = [(down[h, at, :] + doth[h, at, :].astype(f32)).astype(bf16) for h in range(HG)]
        dqkv = jnp.concatenate(parts + [dq[at, :]], axis=1)
        joined[at, :] = dqkv
        gn = mm(dqkv, weight, NT)
        x = jnp.concatenate([xs[m][:T, :] for m in (2 * i, 2 * i + 1)], axis=0).astype(f32)
        s = lax.rsqrt(jnp.mean(x * x, axis=-1, keepdims=True) + epsilon)
        u = gn * gain
        gain_grad[...] += jnp.sum(gn * x * s, axis=0, keepdims=True)
        total = grads[at, :] + s * u - x * (s * s * s) * jnp.mean(u * x, axis=-1, keepdims=True)
        for index, m in enumerate((2 * i, 2 * i + 1)):
            piece = total[index * T : (index + 1) * T]
            if m == 0:
                own[...] = piece
            else:
                sends[m - 1][...] = piece.astype(bf16)


def split_rows(value):
    high = value.astype(bf16)
    return jnp.concatenate([high, (value - high.astype(f32)).astype(bf16)], axis=0)


def project_grad_kernel(T, ids, normed, joined, second, first, table, keep, send, extra, gw):
    c = ids[3]
    R = D // 8
    gw[...] = mm(normed[...], joined[...], TN).reshape(4, 2, R, 3 * CG)
    for a in range(4):
        keep[a] = gw[a, c]
        send[a * R : (a + 1) * R, :] = gw[a, 1 - c].astype(bf16)
    wide = jnp.zeros((1, 3 * CG - D // 2), f32)
    vectors = [second[:, : D // 2], second[:, D // 2 :], first[:, : D // 2], first[:, D // 2 :], table[...]]
    block = jnp.concatenate([jnp.concatenate([v, wide], axis=1) for v in vectors], axis=0)
    block = jnp.concatenate([block, jnp.zeros((3, 3 * CG), f32)], axis=0)
    extra[...] = block
    send[4 * R :, :] = split_rows(block)


def on_device(seqs, fsdps, *args):
    (
        activations,
        segments,
        cotangent,
        attention_gain,
        query_weight,
        key_weight,
        value_weight,
        output_weight,
        bias_table,
        feedforward_gain,
        inner_weight,
        outer_weight,
    ) = args
    T = activations.shape[1]
    C = seqs // GROUPS
    fast = C == 2 and not FORCE_GENERIC
    position = lax.axis_index("seq")
    f = lax.axis_index("fsdp")
    g, c = position // C, position % C
    half = c if fast else 0
    ids = jnp.stack([g, half, f, c]).astype(jnp.int32)
    R0 = query_weight.shape[0]
    RH = R0 // 2
    F0 = outer_weight.shape[0]

    def group_move(value, k):
        pairs = [(a * C + b, (a ^ k) * C + b) for a in range(GROUPS) for b in range(C)]
        return lax.ppermute(value, "seq", pairs)

    def plane_move(value, k):
        return lax.ppermute(value, "fsdp", [(i, i ^ k) for i in range(fsdps)])

    def core_move(value):
        return lax.ppermute(value, "seq", [(i, i ^ 1) for i in range(seqs)])

    def from_group(value):
        return [value] + [group_move(value, k) for k in (1, 2, 3)]

    def from_planes(value):
        return [value] + [plane_move(value, k) for k in (1, 2, 3)]

    def both_halves(pack_of):
        if fast:
            own = from_planes(pack_of(c))
            return own, core_move(jnp.stack(own))
        return from_planes(pack_of(0)), jnp.stack(from_planes(pack_of(1)))

    def project_pack(side):
        def part(weight):
            return lax.dynamic_slice(weight, (side * RH, g * CG), (RH, CG)).reshape(RH, HG, DH)

        pairs = jnp.concatenate([part(key_weight), part(value_weight)], axis=2).reshape(RH, 2 * CG)
        columns = jnp.concatenate([pairs, part(query_weight).reshape(RH, CG)], axis=1)
        wide = columns.shape[1]
        rows = [
            jnp.pad(attention_gain[None], ((0, 0), (0, wide - R0))),
            jnp.pad(feedforward_gain[None], ((0, 6), (0, wide - R0))),
            jnp.pad(bias_table, ((0, 0), (0, wide - H))),
        ]
        return jnp.concatenate([columns] + rows, axis=0)

    def middle_pack(side):
        FB = F0 // 8
        outer = lax.dynamic_slice(outer_weight, (side * (F0 // 2) + FB * (f ^ g), 0), (FB, D))
        inner = jnp.concatenate(
            [
                lax.dynamic_slice(inner_weight, (0, z * F0 + side * (F0 // 2) + FB * (z ^ g)), (R0, FB))
                for z in range(4)
            ],
            axis=1,
        )
        out = lax.dynamic_slice(output_weight, (0, side * (D // 2)), (R0, D // 2))
        return jnp.concatenate([out, inner, outer[:, : D // 2], outer[:, D // 2 :]], axis=0)

    marks = jnp.pad(segments.astype(bf16), ((0, 15), (0, D - T)))
    xs = from_group(jnp.concatenate([activations[0], marks], axis=0))
    ws, wo = both_halves(project_pack)
    cots = from_group(cotangent[0])
    ms, mo = both_halves(middle_pack)

    normed, kv, query, gains, table = call(
        functools.partial(project_kernel, T),
        (
            shape((4 * T, D), bf16),
            shape((HG, 4 * T, 128), bf16),
            shape((HG, 4 * T, 128), bf16),
            shape((8, D), f32),
            shape((32, 128), f32),
        ),
        [ids] + xs + ws + [wo],
        scalars=1,
        scratch=[pltpu.VMEM((4, 2, RH, 3 * CG), bf16), pltpu.VMEM((4, 16, 3 * CG), f32)],
    )
    tiles = call(functools.partial(tiles_kernel, T), shape((HG, 5, T, T), f32), [ids, table], scalars=1)

    slot = jnp.arange(4, dtype=jnp.int32) ^ g
    q_at = slot * C + c
    seg_q = jnp.concatenate([x[T : T + 1, :T] for x in xs], axis=0).astype(f32)
    if fast:
        kv_pack = jnp.concatenate([kv.reshape(HG * 4 * T, 128), jnp.pad(seg_q, ((0, 12), (0, 0))).astype(bf16)], axis=0)
        kv_other = core_move(kv_pack)
        blocks = [kv, kv_other[: HG * 4 * T].reshape(HG, 4 * T, 128)]
        seg_k = jnp.concatenate([seg_q, kv_other[HG * 4 * T : HG * 4 * T + 4].astype(f32)], axis=0)
        k_at = jnp.concatenate([slot * C + c, slot * C + 1 - c])
    else:
        members = [[a * C + b for b in range(C)] for a in range(GROUPS)]
        blocks = [lax.all_gather(kv, "seq", axis=0, axis_index_groups=members)]
        seg_k = lax.all_gather(seg_q.astype(bf16), "seq", axis=0, axis_index_groups=members)
        seg_k = seg_k.reshape(C * 4, T).astype(f32)
        k_at = (slot[None, :] * C + jnp.arange(C, dtype=jnp.int32)[:, None]).reshape(C * 4)
    context, lse = call(
        functools.partial(forward_kernel, T, C, fast),
        (shape((4 * T, CG), bf16), shape((2, 8, 2 * T), f32)),
        [ids, q_at, k_at, query, seg_q, seg_k, tiles] + blocks,
        scalars=3,
        scratch=[pltpu.VMEM((C * 4, T, 128), f32)],
        mib=48,
    )
    ctxs = from_group(context)

    FH = F0 // 2
    outs = call(
        functools.partial(middle_kernel, T),
        (shape((T, D), f32),)
        + (shape((T, D), bf16),) * 3
        + (shape((4 * T, CG), bf16),) * 4
        + (shape((4 * T, D), f32),)
        + (shape((4 * T, D), bf16),) * 4
        + (shape((1, D), f32),),
        [ids] + xs + cots + ctxs + ms + [mo, gains],
        scalars=1,
        scratch=[
            pltpu.VMEM((4, 2, R0, D // 2), bf16),
            pltpu.VMEM((2, 4, R0, FH), bf16),
            pltpu.VMEM((2, 4, F0 // 8, D), bf16),
            pltpu.VMEM((8, 128), f32),
        ],
        mib=48,
    )
    res0, res_send, gcs = outs[0], outs[1:4], outs[4:8]
    grads, normed_ffn, active, ginner, branch, second_gain = outs[8:14]
    got = [gcs[0]] + [group_move(gcs[k], k) for k in (1, 2, 3)]
    res_got = [group_move(res_send[k - 1], k) for k in (1, 2, 3)]
    result = res0 + res_got[0].astype(f32) + res_got[1].astype(f32) + res_got[2].astype(f32)

    R = D // 8
    keep, send = call(
        functools.partial(weight_kernel, T),
        (shape((3, 4, R, D), f32), shape((3, 4, R, D), bf16)),
        [ids, normed_ffn, active, ginner, branch] + cots + ctxs,
        scalars=1,
        scratch=[
            pltpu.VMEM((4, 2, R, D), f32),
            pltpu.VMEM((2, 4, R, D), f32),
            pltpu.VMEM((4, 2, R, D), f32),
        ],
        mib=48,
    )

    if fast:
        back_outs = (
            shape((4 * T, CG), bf16),
            shape((HG, 4 * T, 128), f32),
            shape((HG, 4 * T, 128), bf16),
            shape((HG, 5, T, T), f32),
        )
        back_scratch = [pltpu.VMEM((C * 4, T, 128), f32), pltpu.VMEM((HG, 8 * T, 128), f32)]
    else:
        back_outs = (
            shape((4 * T, CG), bf16),
            shape((C, HG, 4 * T, 128), f32),
            shape((HG, 5, T, T), f32),
        )
        back_scratch = [pltpu.VMEM((C * 4, T, 128), f32)]
    back = call(
        functools.partial(backward_kernel, T, C, fast),
        back_outs,
        [ids, q_at, k_at, query, seg_q, seg_k, tiles, lse] + got + blocks,
        scalars=3,
        scratch=back_scratch,
        mib=48,
    )
    if fast:
        dq, down, doth, sums = back
        dmore = core_move(doth)
    else:
        dq, dall, sums = back
        down = lax.psum_scatter(dall, "seq", scatter_dimension=0, axis_index_groups=members)
        dmore = jnp.zeros((HG, 4 * T, 128), bf16)

    own, s1, s2, s3, joined, first_gain = call(
        functools.partial(tail_kernel, T),
        (shape((T, D), f32),)
        + (shape((T, D), bf16),) * 3
        + (shape((4 * T, 3 * CG), bf16), shape((1, D), f32)),
        [ids] + xs + [dq, down, dmore, grads, gains] + ws + [wo],
        scalars=1,
        scratch=[pltpu.VMEM((4, 2, RH, 3 * CG), bf16)],
    )
    parts = [group_move(v, k) for k, v in ((1, s1), (2, s2), (3, s3))]
    input_gradient = own + parts[0].astype(f32) + parts[1].astype(f32) + parts[2].astype(f32)

    table_row = call(functools.partial(table_kernel, T), shape((1, 32 * H), f32), [ids, sums], scalars=1)
    keep_p, send_p, extra = call(
        functools.partial(project_grad_kernel, T),
        (shape((4, R, 3 * CG), f32), shape((4 * R + 16, 3 * CG), bf16), shape((8, 3 * CG), f32)),
        [ids, normed, joined, second_gain, first_gain, table_row],
        scalars=1,
        scratch=[pltpu.VMEM((4, 2, R, 3 * CG), f32)],
    )

    def both(value):
        count = value.shape[0] // 2
        return value[:count].astype(f32) + value[count:].astype(f32)

    def halves(value):
        high = value.astype(bf16)
        return jnp.concatenate([high, (value - high.astype(f32)).astype(bf16)], axis=0)

    RR = R // 4
    if fast:
        total = keep + core_move(send).astype(f32)
        inner_t = total[0].reshape(4, 4, RR, D)
        outer_t = total[1]
        wout_t = total[2]

        def toward(k):
            at = f ^ k
            left = lax.dynamic_index_in_dim(inner_t, at, 1, False).reshape(R, D)
            right = lax.dynamic_index_in_dim(outer_t, at ^ g, 0, False)
            return jnp.concatenate([left, right], axis=0)

        mine = toward(0)
        for k in (1, 2, 3):
            mine = mine + plane_move(toward(k).astype(bf16), k).astype(f32)
        outer_mine = mine[R:].astype(bf16)
        inner_mine = mine[:R].reshape(4, RR, D)
        pairs = []
        for a in range(GROUPS):
            for b in range(C):
                for z in range(fsdps):
                    pairs.append(((a * C + b) * fsdps + z, ((a ^ z) * C + b) * fsdps + z))
        outer_grad = lax.ppermute(outer_mine, ("seq", "fsdp"), pairs).astype(f32)
        wout = lax.dynamic_index_in_dim(wout_t, g, 0, False)
        for k in (1, 2, 3):
            piece = lax.dynamic_index_in_dim(wout_t, g ^ k, 0, False).astype(bf16)
            wout = wout + group_move(piece, k).astype(f32)
        wout = wout.reshape(4, RR, D)

        more = core_move(send_p)
        project_t = (keep_p + more[: 4 * R].reshape(4, R, 3 * CG).astype(f32)).reshape(4, 4, RR, 3 * CG)
        extra = extra + both(more[4 * R :])
        carried = halves(extra)
        sent = []
        for k in (1, 2, 3):
            left = lax.dynamic_index_in_dim(project_t, f ^ k, 1, False).reshape(R, 3 * CG)
            right = lax.dynamic_index_in_dim(wout, f ^ k, 0, False).reshape(RR * D // (3 * CG), 3 * CG)
            block = jnp.concatenate([left, right], axis=0).astype(bf16)
            sent.append(plane_move(jnp.concatenate([block, carried], axis=0), k))
        project_m = lax.dynamic_index_in_dim(project_t, f, 1, False)
        output_grad = lax.dynamic_index_in_dim(wout, f, 0, False)
        RW = RR * D // (3 * CG)
        for piece in sent:
            project_m = project_m + piece[:R].reshape(4, RR, 3 * CG).astype(f32)
            output_grad = output_grad + piece[R : R + RW].reshape(RR, D).astype(f32)
            extra = extra + both(piece[R + RW :])
        carried = halves(extra)
        slots = []
        RI = RR * D // (3 * CG)
        for k in range(4):
            left = lax.dynamic_index_in_dim(project_m, g ^ k, 0, False)
            right = lax.dynamic_index_in_dim(inner_mine, g ^ k, 0, False).reshape(RI, 3 * CG)
            block = jnp.concatenate([left, right], axis=0).astype(bf16)
            if k == 0:
                slots.append(block)
                continue
            piece = group_move(jnp.concatenate([block, carried], axis=0), k)
            slots.append(piece[: RR + RI])
            extra = extra + both(piece[RR + RI :])
        stacked = jnp.stack(slots)
        ordered = jnp.stack([lax.dynamic_index_in_dim(stacked, g ^ a, 0, False) for a in range(4)])
        project_o = ordered[:, :RR].astype(f32)
        inner_o = ordered[:, RR:].reshape(4, RR, 2, 4, RR * 4).astype(f32)
        pairs_o = project_o[:, :, : 2 * CG].reshape(4, RR, HG, 2, DH)
        key_grad = pairs_o[:, :, :, 0].transpose(1, 0, 2, 3).reshape(RR, D)
        value_grad = pairs_o[:, :, :, 1].transpose(1, 0, 2, 3).reshape(RR, D)
        query_grad = project_o[:, :, 2 * CG :].transpose(1, 0, 2).reshape(RR, D)
        blocks_o = [inner_o[z ^ b, :, e, z] for z in range(4) for e in range(2) for b in range(4)]
        inner_grad = jnp.concatenate(blocks_o, axis=1)
    else:
        FB = F0 // 8
        axes = ("seq", "fsdp")

        def product(left, right):
            return lax.optimization_barrier(mm(left, right, TN))

        def spread(whole, axis):
            blocks = []
            for z in range(4):
                for e in range(2):
                    block = lax.slice_in_dim(whole, (4 * e + z) * FB, (4 * e + z + 1) * FB, axis=axis)
                    blocks += [block * (b == (z ^ g)).astype(f32) for b in range(4)]
            return jnp.concatenate(blocks, axis=axis)

        inner_w = spread(product(normed_ffn, ginner), 1)
        outer_w = spread(product(active, jnp.concatenate(cots, axis=0)), 0)
        out_w = jnp.zeros((4, CG, D), f32)
        for k in range(4):
            ctx = ctxs[k].reshape(4, T, CG)[jnp.array([m ^ k for m in range(4)])].reshape(4 * T, CG)
            out_w = lax.dynamic_update_slice_in_dim(out_w, product(ctx, branch)[None], g ^ k, 0)
        joined_w = product(normed, joined)
        pairs_w = joined_w[:, : 2 * CG].reshape(D, HG, 2, DH)

        def whole(part):
            return lax.dynamic_update_slice(jnp.zeros((D, D), f32), part.reshape(D, CG), (0, g * CG))

        def scatter(part):
            return lax.psum_scatter(part, axes, scatter_dimension=0, tiled=True)

        query_grad = scatter(whole(joined_w[:, 2 * CG :]))
        key_grad = scatter(whole(pairs_w[:, :, 0]))
        value_grad = scatter(whole(pairs_w[:, :, 1]))
        output_grad = scatter(out_w.reshape(D, D))
        inner_grad = scatter(inner_w)
        outer_grad = scatter(outer_w)
        extra = lax.psum(extra, axes)
    at = position * fsdps + f
    own_gain = D // (seqs * fsdps)
    second_vec = jnp.concatenate([extra[0, : D // 2], extra[1, : D // 2]])
    first_vec = jnp.concatenate([extra[2, : D // 2], extra[3, : D // 2]])
    second_grad = lax.dynamic_slice_in_dim(second_vec, at * own_gain, own_gain)
    first_grad = lax.dynamic_slice_in_dim(first_vec, at * own_gain, own_gain)
    table_grad = extra[4, : 32 * H].reshape(H, 32).T
    return (
        result[None],
        input_gradient[None],
        first_grad,
        query_grad,
        key_grad,
        value_grad,
        output_grad,
        table_grad,
        second_grad,
        inner_grad,
        outer_grad,
    )


def solution(mesh):
    return jax.shard_map(
        functools.partial(on_device, mesh.shape["seq"], mesh.shape["fsdp"]),
        mesh=mesh,
        in_specs=(
            P("fsdp", "seq", None),
            P("fsdp", "seq"),
            P("fsdp", "seq", None),
            P("fsdp"),
            P("fsdp", None),
            P("fsdp", None),
            P("fsdp", None),
            P("fsdp", None),
            P("fsdp", None),
            P("fsdp"),
            P("fsdp", None),
            P("fsdp", None),
        ),
        out_specs=(
            P("fsdp", "seq", None),
            P("fsdp", "seq", None),
            P(("seq", "fsdp")),
            P(("seq", "fsdp"), None),
            P(("seq", "fsdp"), None),
            P(("seq", "fsdp"), None),
            P(("seq", "fsdp"), None),
            P(),
            P(("seq", "fsdp")),
            P(("seq", "fsdp"), None),
            P(("seq", "fsdp"), None),
        ),
        check_vma=False,
    )
```

```python
import functools

import jax
import jax.numpy as jnp
from jax import lax
from jax.experimental import pallas as pl
from jax.experimental.pallas import tpu as pltpu
from jax.sharding import PartitionSpec as P

D = 768
H = 12
DH = 64
GROUPS = 4
HG = H // GROUPS
CG = HG * DH

epsilon = 1e-06
FORCE_GENERIC = False
SCALE = 10**6
neg_fill = -1e30
limits = (12, 16, 23, 32, 46, 64, 91)
root_half = 0.7071067811865476
inv_root_tau = 0.3989422804014327
bf16 = jnp.bfloat16
f32 = jnp.float32
NT = (((1,), (1,)), ((), ()))
TN = (((0,), (0,)), ((), ()))
NN = (((1,), (0,)), ((), ()))


def mm(a, b, dims=NN):
    return lax.dot_general(a, b, dims, preferred_element_type=f32)


def bucket_of(offset):
    distance = jnp.abs(offset)
    farther = jnp.zeros_like(offset) + 8
    for limit in limits:
        farther = farther + (distance >= limit).astype(jnp.int32)
    nearer = jnp.where(distance < 8, distance, farther)
    return nearer + jnp.where(offset > 0, 16, 0)


def call(kernel, outs, args, scalars=1, scratch=(), mib=16, us=2, far=()):
    vmem = pl.BlockSpec(memory_space=pltpu.VMEM)
    smem = pl.BlockSpec(memory_space=pltpu.SMEM)
    hbm = pl.BlockSpec(memory_space=pltpu.HBM)
    return pl.pallas_call(
        kernel,
        out_shape=outs,
        in_specs=[smem] * scalars + [hbm if n in far else vmem for n in range(scalars, len(args))],
        out_specs=jax.tree.map(lambda _: vmem, outs),
        scratch_shapes=scratch,
        compiler_params=pltpu.CompilerParams(vmem_limit_bytes=mib << 20),
        cost_estimate=pl.CostEstimate(flops=us * SCALE, bytes_accessed=1 << 10, transcendentals=0),
    )(*args)


def shape(dims, kind):
    return jax.ShapeDtypeStruct(dims, kind)


def project_kernel(T, fast, ids, *refs):
    half, f = ids[1], ids[2]
    ws, os = refs[0:4], refs[4:8]
    xs = [refs[8].at[k] for k in range(4)]
    if fast:
        xs += [refs[9].at[k] for k in range(4)]
    normed, kv, query, marks, gains, table, W, small = refs[-8:]
    rows = W.shape[2]
    for k in range(4):
        z = f ^ k
        W[z, half] = ws[k][:rows, :]
        W[z, 1 - half] = os[k][:rows, :]
        small[z] = ws[k][rows:, :].astype(f32)
    gain = jnp.concatenate([small[z, 0:1, 0 : D // 4] for z in range(4)], axis=1)
    gains[0:1, :] = gain
    gains[1:2, :] = jnp.concatenate([small[z, 1:2, 0 : D // 4] for z in range(4)], axis=1)
    table[...] = jnp.concatenate([small[z, 8:16, 0:128] for z in range(4)], axis=0)
    weight = W[...].reshape(D, 3 * CG)
    count = len(xs)
    seg = [xs[k][T:, :].astype(f32)[0:1, :128] for k in range(count)]
    marks[...] = jnp.concatenate(seg + [jnp.zeros((8 - count, 128), f32)] * (count < 8), axis=0)
    for i in range(count // 2):
        parts = []
        for k in (2 * i, 2 * i + 1):
            x = xs[k][:T, :].astype(f32)
            s = lax.rsqrt(jnp.mean(x * x, axis=-1, keepdims=True) + epsilon)
            parts.append((x * s * gain).astype(bf16))
        n = jnp.concatenate(parts, axis=0)
        at = slice(2 * i * T, (2 * i + 2) * T)
        normed[at, :] = n
        out = mm(n, weight if i < 2 else weight[:, : 2 * CG])
        for h in range(HG):
            kv[h, at, :] = out[:, 128 * h : 128 * h + 128].astype(bf16)
        if i < 2:
            blank = jnp.zeros((2 * T, DH), f32)
            for h in range(HG):
                q = out[:, 2 * CG + DH * h : 2 * CG + DH * (h + 1)]
                query[h, at, :] = jnp.concatenate([q, blank], axis=1).astype(bf16)


def tiles_kernel(T, ids, table, tiles):
    g = ids[0]
    lane = lax.broadcasted_iota(jnp.int32, (32, 128), 1)
    m = lax.broadcasted_iota(jnp.int32, (32, 2 * T), 1)
    label = lax.broadcasted_iota(jnp.int32, (32, 2 * T), 0)
    for h in range(HG):
        column = jnp.sum(jnp.where(lane == HG * g + h, table[...], 0.0), axis=1, keepdims=True)
        for d in range(5):
            if d in (0, 4):
                one = column[15 if d == 0 else 31 :][:1, :]
                tiles[h, d] = jnp.broadcast_to(one, (T, T))
                continue
            offset = T * (d - 2) - jnp.where(m < T, m, m - 2 * T)
            hot = jnp.where(bucket_of(offset) == label, column, 0.0)
            along = jnp.sum(hot, axis=0, keepdims=True)
            wide = jnp.broadcast_to(along, (T, 2 * T))
            tiles[h, d] = pltpu.roll(wide, 0, 1, stride=1, stride_axis=0)[:, :T]


def tile_of(key_at, query_at):
    return jnp.clip(key_at - query_at, -2, 2) + 2


def mark_columns(T, count, marks, columns):
    across = jnp.concatenate([marks[...], jnp.zeros((128 - marks.shape[0], 128), f32)], axis=0).T
    for t in range(count):
        columns[t] = jnp.broadcast_to(across[:, t : t + 1], (T, 128))


def masked_scores(T, scores, base, pair, h, q_at, k_at, seg_q, columns, tiles):
    pieces = []
    for t in range(8):
        kt = base + t
        bias = jnp.concatenate([tiles[h, tile_of(k_at[kt], q_at[2 * pair + j])] for j in range(2)], axis=1)
        column = jnp.concatenate([columns[kt], columns[kt]], axis=1)
        piece = scores[t * T : (t + 1) * T] + bias
        pieces.append(jnp.where(column == seg_q, piece, neg_fill))
    return jnp.concatenate(pieces, axis=0)


def pick_keys(blocks, i, h):
    if len(blocks[0].shape) == 3:
        return blocks[0][h]
    return jnp.concatenate([blocks[0][2 * i, h], blocks[0][2 * i + 1, h]], axis=0)


def forward_kernel(T, nb, fast, ids, q_at, k_at, query, seg_q, seg_k, tiles, *rest):
    blocks, (context, lse, columns) = rest[:-3], rest[-3:]
    mark_columns(T, nb * 4, seg_k, columns)

    def pair_step(pair, carry):
        at = pl.ds(pl.multiple_of(pair * 2 * T, 2 * T), 2 * T)
        seg = jnp.concatenate([seg_q[pl.ds(2 * pair + j, 1), :] for j in range(2)], axis=1)
        out = []
        for h in range(HG):
            q = query[h, at, :]

            def chunk(i, state):
                peak, total, acc = state
                keys = pick_keys(blocks, i, h)
                s = masked_scores(T, mm(keys, q, NT), 8 * i, pair, h, q_at, k_at, seg, columns, tiles)
                top = jnp.maximum(peak, jnp.max(s, axis=0, keepdims=True))
                p = jnp.exp(s - top)
                fade = jnp.exp(peak - top)
                total = total * fade + jnp.sum(p, axis=0, keepdims=True)
                acc = acc * fade + mm(keys, p.astype(bf16), TN)
                return top, total, acc

            start = (
                jnp.full((1, 2 * T), neg_fill, f32),
                jnp.zeros((1, 2 * T), f32),
                jnp.zeros((128, 2 * T), f32),
            )
            if fast:
                peak, total, acc = chunk(0, start)
            else:
                peak, total, acc = lax.fori_loop(0, nb // 2, chunk, start)
            out.append(acc[DH:, :] / total)
            lse[pair, h : h + 1, :] = peak + jnp.log(total)
        joined = jnp.concatenate(out, axis=0)
        context[at, :] = joined.T.astype(bf16)
        return carry

    lax.fori_loop(0, 2, pair_step, 0)


def backward_kernel(T, nb, fast, ids, q_at, k_at, query, seg_q, seg_k, tiles, lse, g0, g1, g2, g3, *rest):
    nin = 1
    blocks = rest[:nin]
    if fast:
        dquery, down, doth, sums, columns, dkv = rest[nin:]
    else:
        dquery, dkv, sums, columns = rest[nin:]
    mark_columns(T, nb * 4, seg_k, columns)
    sums[...] = jnp.zeros_like(sums)
    dkv[...] = jnp.zeros_like(dkv)

    def pair_step(pair, carry):
        at = pl.ds(pl.multiple_of(pair * 2 * T, 2 * T), 2 * T)
        seg = jnp.concatenate([seg_q[pl.ds(2 * pair + j, 1), :] for j in range(2)], axis=1)
        grad = g0[at, :].astype(f32) + g1[at, :].astype(f32) + g2[at, :].astype(f32) + g3[at, :].astype(f32)
        blank = jnp.zeros((2 * T, DH), f32)
        out = []
        for h in range(HG):
            q = query[h, at, :]
            do = jnp.concatenate([blank, grad[:, DH * h : DH * (h + 1)]], axis=1).astype(bf16)
            row = lse[pair, h : h + 1, :]

            def probs_of(i):
                keys = pick_keys(blocks, i, h)
                s = masked_scores(T, mm(keys, q, NT), 8 * i, pair, h, q_at, k_at, seg, columns, tiles)
                return keys, jnp.exp(s - row), mm(keys, do, NT)

            def finish(i, keys, p, dp, delta):
                ds = p * (dp - delta)
                for t in range(8):
                    for j in range(2):
                        index = tile_of(k_at[8 * i + t], q_at[2 * pair + j])
                        sums[h, index] += ds[t * T : (t + 1) * T, j * T : (j + 1) * T]
                ds = ds.astype(bf16)
                both = jnp.concatenate([ds, p.astype(bf16)], axis=1)
                piece = mm(both, jnp.concatenate([q, do], axis=0))
                if fast:
                    dkv[h] += piece
                else:
                    dkv[2 * i, h] += piece[: 4 * T]
                    dkv[2 * i + 1, h] += piece[4 * T :]
                return mm(keys, ds, TN)[:DH, :]

            if fast:
                keys, p, dp = probs_of(0)
                delta = jnp.sum(p * dp, axis=0, keepdims=True)
                dq = finish(0, keys, p, dp, delta)
            else:

                def first(i, delta):
                    keys, p, dp = probs_of(i)
                    return delta + jnp.sum(p * dp, axis=0, keepdims=True)

                delta = lax.fori_loop(0, nb // 2, first, jnp.zeros((1, 2 * T), f32))

                def second(i, dq):
                    keys, p, dp = probs_of(i)
                    return dq + finish(i, keys, p, dp, delta)

                dq = lax.fori_loop(0, nb // 2, second, jnp.zeros((DH, 2 * T), f32))
            out.append(dq)
        dquery[at, :] = jnp.concatenate(out, axis=0).T.astype(bf16)
        return carry

    lax.fori_loop(0, 2, pair_step, 0)
    if fast:
        for h in range(HG):
            down[h] = dkv[h, : 4 * T, :].astype(bf16)
            doth[h] = dkv[h, 4 * T :, :].astype(bf16)


def exact_mm(value, chosen):
    high = value.astype(bf16)
    low = (value - high.astype(f32)).astype(bf16)
    return mm(high, chosen) + mm(low, chosen)


def table_kernel(T, ids, sums, out):
    g = ids[0]
    row = lax.broadcasted_iota(jnp.int32, (T, T), 0)
    lane = lax.broadcasted_iota(jnp.int32, (T, T), 1)
    mirror = (row + lane == T - 1).astype(bf16)
    blank = jnp.zeros((T, T), f32)
    offset = lax.broadcasted_iota(jnp.int32, (2 * T, 128), 0) - (T - 1)
    label = lax.broadcasted_iota(jnp.int32, (2 * T, 128), 1)
    label8 = lax.broadcasted_iota(jnp.int32, (8, 128), 1)
    total = jnp.zeros((8, 128), f32)
    for d in range(5):
        lines = []
        for h in range(HG):
            if d in (0, 4):
                lines.append(jnp.sum(sums[h, d], axis=0, keepdims=True))
            else:
                moved = jnp.concatenate([exact_mm(sums[h, d], mirror), blank], axis=1)
                moved = pltpu.roll(moved, 0, 1, stride=1, stride_axis=0)
                lines.append(jnp.sum(moved, axis=0, keepdims=True))
        block = jnp.concatenate(lines + [jnp.zeros((8 - HG, lines[0].shape[1]), f32)], axis=0)
        if d in (0, 4):
            whole = jnp.sum(block, axis=1, keepdims=True)
            total = total + jnp.where(label8 == (15 if d == 0 else 31), whole, 0.0)
        else:
            total = total + exact_mm(block, (bucket_of(offset + T * (d - 2)) == label).astype(bf16))
    pieces = []
    for a in range(GROUPS):
        for h in range(HG):
            pieces.append(jnp.where(g == a, total[h : h + 1, :32], 0.0))
    out[...] = jnp.concatenate(pieces, axis=1)


def middle_kernel(T, ids, *refs):
    g, half, f = ids[0], ids[1], ids[2]
    x, ctx, gains = refs[0:3]
    cots, ws, others = refs[3:7], refs[7:11], refs[11:15]
    res0, sends, gcs = refs[15], refs[16:19], refs[19:23]
    grads, normed, active, ginner, branch, cot_all, gain_grad = refs[23:30]
    WO, W1, W2, held = refs[30:34]
    rows, low = WO.shape[2], WO.shape[2] // 2
    FH = W1.shape[3]
    for k in range(4):
        z = f ^ k
        cot_all[g ^ k] = cots[k][...]
        for at, pieces in ((half, ws), (1 - half, others)):
            piece = pieces[k]
            WO[z, at] = piece[:rows]
            W1[at, z] = piece[rows : 2 * rows]
            W2[at, z, :, 0 : D // 2] = piece[2 * rows : 2 * rows + low]
            W2[at, z, :, D // 2 :] = piece[2 * rows + low :]
    gain = gains[1:2, :]
    gain_grad[...] = jnp.zeros_like(gain_grad)

    def out_rows(a):
        return jnp.concatenate([WO[a, 0], WO[a, 1]], axis=1)

    for i in range(2):
        at = slice(2 * i * T, (2 * i + 2) * T)
        slots = (2 * i, 2 * i + 1)
        att = jnp.concatenate([x[m, :T, :] for m in slots], axis=0).astype(f32)
        cot = jnp.concatenate([cot_all[m] for m in slots], axis=0)
        for a in range(4):
            att = att + mm(ctx[a, at, :], out_rows(a))
        s = lax.rsqrt(jnp.mean(att * att, axis=-1, keepdims=True) + epsilon)
        n = (att * s * gain).astype(bf16)
        normed[at, :] = n
        result = None
        gn = None
        for c in range(2):
            columns = slice(c * FH, (c + 1) * FH)
            w1 = W1[c].reshape(D, FH)
            w2 = W2[c].reshape(FH, D)
            inner = mm(n, w1)
            cdf = 0.5 * (1.0 + lax.erf(inner * root_half))
            act = (inner * cdf).astype(bf16)
            slope = cdf + inner * jnp.exp(-0.5 * inner * inner) * inv_root_tau
            part = mm(act, w2)
            result = part if result is None else result + part
            ga = mm(cot, w2, NT).astype(bf16)
            gi = (ga.astype(f32) * slope).astype(bf16)
            part = mm(gi, w1, NT)
            gn = part if gn is None else gn + part
            active[at, columns] = act
            ginner[at, columns] = gi
        for index, m in enumerate(slots):
            held[m] = result[index * T : (index + 1) * T]

            @pl.when(g == m)
            def _():
                held[m] += att[index * T : (index + 1) * T]

        u = gn * gain
        gain_grad[...] += jnp.sum(gn * att * s, axis=0, keepdims=True)
        grad = 0.25 * cot.astype(f32) + s * u - att * (s * s * s) * jnp.mean(u * att, axis=-1, keepdims=True)
        grads[at, :] = grad
        gb = grad.astype(bf16)
        branch[at, :] = gb
        for k in range(4):
            gcs[k][at, :] = mm(gb, out_rows(g ^ k), NT).astype(bf16)
    res0[...] = held[g]
    for k in (1, 2, 3):
        sends[k - 1][...] = held[g ^ k].astype(bf16)


def weight_kernel(T, ids, normed, active, ginner, branch, cot, ctx, keep, send, gi, go, gw):
    c = ids[3]
    R = D // 8
    gi[...] = mm(normed[...], ginner[...], TN).reshape(4, 2, R, D)
    go[...] = mm(active[...], cot[...].reshape(4 * T, D), TN).reshape(2, 4, R, D)
    gb = branch[...]
    for a in range(4):
        gw[a] = mm(ctx[a], gb, TN).reshape(2, R, D)
    for a in range(4):
        keep[0, a] = gi[a, c]
        keep[1, a] = go[c, a]
        keep[2, a] = gw[a, c]
        send[0, a] = gi[a, 1 - c].astype(bf16)
        send[1, a] = go[1 - c, a].astype(bf16)
        send[2, a] = gw[a, 1 - c].astype(bf16)


def tail_kernel(T, ids, x_all, dq, down, doth, grads, gains, *refs):
    g, half, f = ids[0], ids[1], ids[2]
    ws, os, rs = refs[0:4], refs[4:8], refs[8:11]
    own, s1, s2, s3, joined, gain_grad, W, held = refs[11:]
    rows = W.shape[2]
    sends = (s1, s2, s3)
    for k in range(4):
        z = f ^ k
        W[z, half] = ws[k][:rows, :]
        W[z, 1 - half] = os[k][:rows, :]
    weight = W[...].reshape(D, 3 * CG)
    gain = gains[0:1, :]
    gain_grad[...] = jnp.zeros_like(gain_grad)
    for i in range(2):
        at = slice(2 * i * T, (2 * i + 2) * T)
        parts = [(down[h, at, :].astype(f32) + doth[h, at, :].astype(f32)).astype(bf16) for h in range(HG)]
        dqkv = jnp.concatenate(parts + [dq[at, :]], axis=1)
        joined[at, :] = dqkv
        gn = mm(dqkv, weight, NT)
        x = jnp.concatenate([x_all[m, :T, :] for m in (2 * i, 2 * i + 1)], axis=0).astype(f32)
        s = lax.rsqrt(jnp.mean(x * x, axis=-1, keepdims=True) + epsilon)
        u = gn * gain
        gain_grad[...] += jnp.sum(gn * x * s, axis=0, keepdims=True)
        total = grads[at, :] + s * u - x * (s * s * s) * jnp.mean(u * x, axis=-1, keepdims=True)
        for index, m in enumerate((2 * i, 2 * i + 1)):
            held[m] = total[index * T : (index + 1) * T]
    own[...] = held[g]
    for k in (1, 2, 3):
        sends[k - 1][:T, :] = held[g ^ k].astype(bf16)
        sends[k - 1][T:, :] = rs[k - 1][...]


def split_rows(value):
    high = value.astype(bf16)
    return jnp.concatenate([high, (value - high.astype(f32)).astype(bf16)], axis=0)


def project_grad_kernel(T, ids, normed, dq, down, doth, keep, send, gw):
    c = ids[3]
    R = D // 8
    own = jnp.concatenate([down[h] for h in range(HG)], axis=1)
    other = jnp.concatenate([doth[h] for h in range(HG)], axis=1)
    pairs = mm(normed[...], jnp.concatenate([own, other], axis=0), TN)
    single = mm(normed[: 4 * T, :], dq[...], TN)
    gw[...] = jnp.concatenate([pairs, single], axis=1).reshape(4, 2, R, 3 * CG)
    for a in range(4):
        keep[a] = gw[a, c]
        send[a * R : (a + 1) * R, :] = gw[a, 1 - c].astype(bf16)


def extra_kernel(second, first, table, block, send):
    wide = jnp.zeros((1, 3 * CG - D // 2), f32)
    vectors = [second[:, : D // 2], second[:, D // 2 :], first[:, : D // 2], first[:, D // 2 :], table[...]]
    rows = jnp.concatenate([jnp.concatenate([v, wide], axis=1) for v in vectors], axis=0)
    rows = jnp.concatenate([rows, jnp.zeros((3, 3 * CG), f32)], axis=0)
    block[...] = rows
    send[...] = split_rows(rows)


def start_kernel(T, C, ids, q, k, v, first, second, table, x, seg, out, x_out, small, held, gain1, gain2, rows8, marks, sems):
    place = lax.axis_index("seq")
    g = lax.div(place, C)
    side = lax.rem(place, C) if ids is None else ids[1]
    rows = out.shape[0] - 16
    at = pl.ds(pl.multiple_of(side * rows, rows), rows)
    lanes = pl.ds(pl.multiple_of(128 * (g + lax.div(g, 2)), 128), 256)
    pairs = [(w.at[at, lanes], held.at[n]) for n, w in enumerate((q, k, v))]
    pairs += [(first, gain1), (second, gain2), (table, rows8), (seg, marks), (x.at[0], x_out.at[:T])]
    copies = [pltpu.make_async_copy(a, b, sems.at[n]) for n, (a, b) in enumerate(pairs)]
    for copy in copies:
        copy.start()
    small[...] = jnp.zeros_like(small)
    for copy in copies:
        copy.wait()
    mark = jnp.concatenate([marks[...].astype(f32), jnp.zeros((15, T), f32)], axis=0)
    x_out[T:, :] = jnp.concatenate([mark, jnp.zeros((16, D - T), f32)], axis=1).astype(bf16)
    small[0:1, 0 : D // 4] = gain1[...].reshape(1, D // 4).astype(f32)
    small[1:2, 0 : D // 4] = gain2[...].reshape(1, D // 4).astype(f32)
    small[8:16, 0:H] = rows8[...].astype(f32)
    out[rows:, :] = small[...].astype(bf16)
    for odd in range(2):

        @pl.when(lax.rem(g, 2) == odd)
        def _():
            pieces = []
            for h in range(HG):
                here = slice(DH * (odd + h), DH * (odd + h + 1))
                pieces += [held[1, :, here], held[2, :, here]]
            pieces.append(held[0, :, DH * odd : DH * odd + CG])
            out[:rows, :] = jnp.concatenate(pieces, axis=1)


def middle_pack_kernel(ids, wo, inner, outer, out, held, block, sems):
    g, side, f = ids[0], ids[1], ids[2]
    R0, F0 = wo.shape[0], outer.shape[0]
    FB, low = F0 // 8, R0 // 2
    half = F0 // 2
    pairs = [
        (wo.at[:, pl.ds(pl.multiple_of(side * half, 128), half)], out.at[:R0]),
        (outer.at[pl.ds(pl.multiple_of(side * half + FB * (f ^ g), FB), FB)], block),
    ]
    for z in range(4):
        base = (2 * z + side) * half + 128 * lax.div(z ^ g, 2)
        pairs.append((inner.at[:, pl.ds(pl.multiple_of(base, 128), 256)], held.at[z]))
    copies = [pltpu.make_async_copy(a, b, sems.at[n]) for n, (a, b) in enumerate(pairs)]
    for copy in copies:
        copy.start()
    for copy in copies:
        copy.wait()
    for a in range(GROUPS):

        @pl.when(g == a)
        def _():
            starts = [FB * (z ^ a) - 128 * ((z ^ a) // 2) for z in range(4)]
            picked = jnp.concatenate([held[z, :, n : n + FB] for z, n in enumerate(starts)], axis=1)
            out[R0 : 2 * R0, :] = picked

    out[2 * R0 : 2 * R0 + low, :] = block[:, : D // 2]
    out[2 * R0 + low :, :] = block[:, D // 2 :]


def added(refs):
    value = refs[0][...].astype(f32)
    for r in refs[1:]:
        value = value + r[...].astype(f32)
    return value


def join_kernel(ids, keep, more, far, near, p1, p2, p3, wown, total):
    g, f = ids[0], ids[2]
    R = D // 8
    total[...] = (keep[0] + more[0].astype(f32)).reshape(4, 4, R // 4, D)

    def toward(at):
        right = keep[1, at ^ g] + more[1, at ^ g].astype(f32)
        return [total[a, at] for a in range(4)] + [right]

    far[...] = jnp.concatenate(toward(f ^ 1) + toward(f ^ 3), axis=0).astype(bf16)
    near[...] = jnp.concatenate(toward(f) + toward(f ^ 2), axis=0)
    for k, out in enumerate((wown, p1, p2, p3)):
        out[...] = (keep[2, g ^ k] + more[2, g ^ k].astype(f32)).astype(out.dtype)


def middle_half_kernel(near, more, send, mine):
    value = near[...] + more[...].astype(f32)
    count = mine.shape[0]
    mine[...] = value[:count]
    send[:count, :] = value[count:].astype(bf16)
    send[count:, :] = jnp.zeros((send.shape[0] - count, send.shape[1]), bf16)


def middle_sum_kernel(own, more, inner, outer):
    R = D // 8
    value = own[...] + more[: 2 * R, :].astype(f32)
    inner[...] = value[:R]
    outer[...] = value[R:].astype(bf16)


def unsplit(block):
    return block[:8] + block[8:]


def narrow(block):
    wide = 3 * CG
    right = block[:, wide:]
    rows = block.shape[0] // 3
    folded = jnp.concatenate([right[n * rows : (n + 1) * rows] for n in range(3)], axis=1)
    return jnp.concatenate([block[:, :wide], folded], axis=0)


def widen(block):
    rows = D // 32
    folded = block[rows:]
    wide = D - 3 * CG
    right = jnp.concatenate([folded[:, n * wide : (n + 1) * wide] for n in range(3)], axis=0)
    return jnp.concatenate([block[:rows], right], axis=1)


def project_join_kernel(ids, keep, more, extra, extra_more, wown, p1, p2, p3, far, near, extra_out, total, out_total):
    f = ids[2]
    R = D // 8
    total[...] = (keep[...] + more[...].astype(f32).reshape(4, R, 3 * CG)).reshape(4, 4, R // 4, 3 * CG)
    out_total[...] = added((wown, p1, p2, p3)).reshape(4, R // 4, D)
    ex = extra[...] + unsplit(extra_more[...].astype(f32))
    extra_out[...] = ex

    def toward(at):
        return [total[a, at] for a in range(4)]

    far[: 2 * R, :] = jnp.concatenate(toward(f ^ 1) + toward(f ^ 3), axis=0).astype(bf16)
    data = jnp.concatenate([narrow(out_total[f ^ 1]), narrow(out_total[f ^ 3])], axis=0).astype(bf16)
    far[2 * R : 2 * R + data.shape[0], :] = data
    far[2 * R + data.shape[0] :, :] = split_rows(ex)
    kept = [toward(at) + [narrow(out_total[at])] for at in (f, f ^ 2)]
    near[...] = jnp.concatenate(kept[0] + kept[1], axis=0)


def project_half_kernel(near, more, extra, send, mine, extra_out):
    R = D // 8
    got, tail = more[: 2 * R, :].astype(f32), more[2 * R :, :].astype(f32)
    count = mine.shape[0]
    low = count - R
    ex = extra[...] + unsplit(tail[2 * low :])
    extra_out[...] = ex
    mine[:R, :] = near[:R, :] + got[:R]
    mine[R:, :] = near[R:count, :] + tail[:low]
    send[:R, :] = (near[count : count + R, :] + got[R:]).astype(bf16)
    send[R:count, :] = (near[count + R :, :] + tail[low : 2 * low]).astype(bf16)
    send[count:, :] = split_rows(ex)


def project_plane_kernel(ids, own, more, extra, inner, s1, s2, s3, mine, extra_out, output, total, held):
    g = ids[0]
    R = D // 8
    RR = R // 4
    got = more[...].astype(f32)
    value = own[...] + got[: own.shape[0]]
    ex = extra[...] + unsplit(got[own.shape[0] :])
    extra_out[...] = ex
    output[...] = widen(value[R:])
    total[...] = value[:R].reshape(4, RR, 3 * CG)
    held[...] = inner[...].reshape(4, RR, D)
    high = ex.astype(bf16).astype(f32)
    low = ex - high
    tail = jnp.concatenate([high[:, : D // 2], low[:, : D // 2], jnp.zeros((8, 3 * CG), f32)], axis=1)
    for k, out in enumerate((mine, s1, s2, s3)):
        block = jnp.concatenate([total[g ^ k], held[g ^ k]], axis=1)
        out[...] = block if k == 0 else jnp.concatenate([block, tail], axis=0).astype(bf16)


def final_kernel(where, own, r1, r2, r3, extra, outer_in, query, key, value, inner, first, second, table, outer, slots, rows):
    g, at = where[0], where[1]
    RR = D // 32
    ex = extra[...][:, : D // 2]
    slots[g] = own[...]
    for k, r in ((1, r1), (2, r2), (3, r3)):
        got = r[...].astype(f32)
        slots[g ^ k] = got[:RR]
        ex = ex + got[RR:, : D // 2] + got[RR:, D // 2 : D]
    query[...] = jnp.concatenate([slots[a, :, 2 * CG : 3 * CG] for a in range(4)], axis=1)
    for part, out in enumerate((key, value)):
        starts = [128 * h + DH * part for h in range(HG)]
        out[...] = jnp.concatenate([slots[a, :, n : n + DH] for a in range(4) for n in starts], axis=1)
    base = 3 * CG
    for z in range(4):
        for e in range(2):
            n = base + (4 * e + z) * 4 * RR
            inner[:, (8 * z + 4 * e) * 4 * RR : (8 * z + 4 * e + 4) * 4 * RR] = jnp.concatenate(
                [slots[z ^ b, :, n : n + 4 * RR] for b in range(4)], axis=1
            )
    own_gain = first.shape[1]
    for r, out in ((0, second), (2, first)):
        whole = jnp.concatenate([ex[r : r + 1], ex[r + 1 : r + 2]], axis=1)
        count = D // own_gain
        rows[...] = jnp.concatenate([whole[:, own_gain * n : own_gain * (n + 1)] for n in range(count)], axis=0)
        out[...] = rows[pl.ds(at, 1), :]
    table[...] = jnp.concatenate([ex[4:5, 32 * h : 32 * (h + 1)] for h in range(H)], axis=0)
    outer[...] = outer_in[...].astype(f32)


def on_device(seqs, fsdps, *args):
    (
        activations,
        segments,
        cotangent,
        attention_gain,
        query_weight,
        key_weight,
        value_weight,
        output_weight,
        bias_table,
        feedforward_gain,
        inner_weight,
        outer_weight,
    ) = args
    T = activations.shape[1]
    C = seqs // GROUPS
    fast = C == 2 and not FORCE_GENERIC
    position = lax.axis_index("seq")
    f = lax.axis_index("fsdp")
    g, c = position // C, position % C
    half = c if fast else 0
    ids = jnp.stack([g, half, f, c]).astype(jnp.int32)
    R0 = query_weight.shape[0]
    RH = R0 // 2
    F0 = outer_weight.shape[0]

    def group_move(value, k):
        pairs = [(a * C + b, (a ^ k) * C + b) for a in range(GROUPS) for b in range(C)]
        return lax.ppermute(value, "seq", pairs)

    def plane_move(value, k):
        return lax.ppermute(value, "fsdp", [(i, i ^ k) for i in range(fsdps)])

    def core_move(value):
        return lax.ppermute(value, "seq", [(i, i ^ 1) for i in range(seqs)])

    def from_group(value):
        return [value] + [group_move(value, k) for k in (1, 2, 3)]

    def from_planes(value):
        return [value] + [plane_move(value, k) for k in (1, 2, 3)]

    def ids_for(side):
        return jnp.stack([g, jnp.asarray(side, jnp.int32), f, c]).astype(jnp.int32)

    def start(side):
        own = fast and side is half
        kernel = functools.partial(start_kernel, T, C)
        return call(
            functools.partial(kernel, None) if own else kernel,
            (shape((RH + 16, 3 * CG), bf16), shape((T + 16, D), bf16)),
            ([] if own else [ids_for(side)])
            + [
                query_weight,
                key_weight,
                value_weight,
                attention_gain,
                feedforward_gain,
                bias_table,
                activations,
                segments,
            ],
            scratch=[
                pltpu.VMEM((16, 3 * CG), f32),
                pltpu.VMEM((3, RH, 256), bf16),
                pltpu.VMEM((R0,), bf16),
                pltpu.VMEM((R0,), bf16),
                pltpu.VMEM(bias_table.shape, bf16),
                pltpu.VMEM((1, T), jnp.int32),
                pltpu.SemaphoreType.DMA((8,)),
            ],
            us=1,
            mib=60,
            scalars=0 if own else 1,
            far=range(9),
        )

    def middle_pack(side):
        return call(
            middle_pack_kernel,
            shape((3 * R0, D // 2), bf16),
            [ids_for(side), output_weight, inner_weight, outer_weight],
            scratch=[
                pltpu.VMEM((4, R0, 256), bf16),
                pltpu.VMEM((F0 // 8, D), bf16),
                pltpu.SemaphoreType.DMA((6,)),
            ],
            us=1,
            mib=60,
            far=(1, 2, 3),
        )

    def after(values, *earlier):
        return lax.optimization_barrier((values, earlier))[0]

    def ring(value):
        return lax.ppermute(value, "fsdp", [(i, (i + 1) % fsdps) for i in range(fsdps)])

    token_groups = [[a * C + b for a in range(GROUPS)] for b in range(C)]

    def gather(value):
        return lax.all_gather(value, "seq", axis=0, axis_index_groups=token_groups)

    w_pack, x_pack = start(half)
    m_pack = middle_pack(half)
    ws = from_planes(w_pack)
    ms = from_planes(m_pack)
    x_all = gather(after(x_pack, m_pack))
    cots = from_group(after(cotangent[0], x_all))
    if fast:
        xo = [core_move(after(x_all, *ws))]
        wo = [core_move(w) for w in ws]
    else:
        xo = []
        wo = from_planes(start(1)[0])

    wide_t = (8 if fast else 4) * T
    normed, kv, query, marks, gains, table = call(
        functools.partial(project_kernel, T, fast),
        (
            shape((wide_t, D), bf16),
            shape((HG, wide_t, 128), bf16),
            shape((HG, 4 * T, 128), bf16),
            shape((8, 128), f32),
            shape((8, D), f32),
            shape((32, 128), f32),
        ),
        [ids] + ws + wo + [x_all] + xo,
        scratch=[pltpu.VMEM((4, 2, RH, 3 * CG), bf16), pltpu.VMEM((4, 16, 3 * CG), f32)],
        us=1,
    )
    tiles = call(functools.partial(tiles_kernel, T), shape((HG, 5, T, T), f32), [ids, table], us=1)

    slot = jnp.arange(4, dtype=jnp.int32)
    q_at = slot * C + c
    seg_q = marks
    blocks = [kv]
    if fast:
        seg_k = marks
        k_at = jnp.concatenate([slot * C + c, slot * C + 1 - c])
    else:
        members = [[a * C + b for b in range(C)] for a in range(GROUPS)]
        blocks = [lax.all_gather(kv, "seq", axis=0, axis_index_groups=members)]
        seg_k = lax.all_gather(marks[:4].astype(bf16), "seq", axis=0, axis_index_groups=members)
        seg_k = seg_k.reshape(C * 4, T).astype(f32)
        k_at = (slot[None, :] * C + jnp.arange(C, dtype=jnp.int32)[:, None]).reshape(C * 4)
    context, lse = call(
        functools.partial(forward_kernel, T, C, fast),
        (shape((4 * T, CG), bf16), shape((2, 8, 2 * T), f32)),
        [ids, q_at, k_at, query, seg_q, seg_k, tiles] + blocks,
        scalars=3,
        scratch=[pltpu.VMEM((C * 4, T, 128), f32)],
        mib=16 if fast else 48,
        us=1,
    )
    ctx_all = gather(context)
    cots, ms = after((tuple(cots), tuple(ms)), ctx_all)
    if fast:
        mo = [core_move(m) for m in ms]
    else:
        mo = from_planes(middle_pack(1))

    FH = F0 // 2
    outs = call(
        functools.partial(middle_kernel, T),
        (shape((T, D), f32),)
        + (shape((T, D), bf16),) * 3
        + (shape((4 * T, CG), bf16),) * 4
        + (shape((4 * T, D), f32),)
        + (shape((4 * T, D), bf16),) * 4
        + (shape((4, T, D), bf16), shape((1, D), f32)),
        [ids, x_all, ctx_all, gains] + list(cots) + list(ms) + mo,
        scratch=[
            pltpu.VMEM((4, 2, R0, D // 2), bf16),
            pltpu.VMEM((2, 4, R0, FH), bf16),
            pltpu.VMEM((2, 4, F0 // 8, D), bf16),
            pltpu.VMEM((4, T, D), f32),
        ],
        mib=24,
        us=10,
    )
    res0, res_send, gcs = outs[0], outs[1:4], outs[4:8]
    grads, normed_ffn, active, ginner, branch, cot_all, second_gain = outs[8:15]
    got = [gcs[0]] + [group_move(gcs[k], k) for k in (1, 2, 3)]
    R = D // 8
    keep, send = call(
        functools.partial(weight_kernel, T),
        (shape((3, 4, R, D), f32), shape((3, 4, R, D), bf16)),
        [ids, normed_ffn, active, ginner, branch, cot_all, ctx_all],
        scratch=[
            pltpu.VMEM((4, 2, R, D), f32),
            pltpu.VMEM((2, 4, R, D), f32),
            pltpu.VMEM((4, 2, R, D), f32),
        ],
        mib=24,
        us=5,
    )

    RR = R // 4
    if fast:
        far, near, p1, p2, p3, wown = call(
            join_kernel,
            (shape((4 * R, D), bf16), shape((4 * R, D), f32)) + (shape((R, D), bf16),) * 3 + (shape((R, D), f32),),
            [ids, keep, core_move(send)],
            scratch=[pltpu.VMEM((4, 4, RR, D), f32)],
        )
        middle_more = plane_move(far, 1)
        got = list(after(tuple(got), far, p1))
        ps = [group_move(p, k) for k, p in ((1, p1), (2, p2), (3, p3))]
    if fast:
        back_outs = (
            shape((4 * T, CG), bf16),
            shape((HG, 4 * T, 128), bf16),
            shape((HG, 4 * T, 128), bf16),
            shape((HG, 5, T, T), f32),
        )
        back_scratch = [pltpu.VMEM((C * 4, T, 128), f32), pltpu.VMEM((HG, 8 * T, 128), f32)]
    else:
        back_outs = (
            shape((4 * T, CG), bf16),
            shape((C, HG, 4 * T, 128), f32),
            shape((HG, 5, T, T), f32),
        )
        back_scratch = [pltpu.VMEM((C * 4, T, 128), f32)]
    back = call(
        functools.partial(backward_kernel, T, C, fast),
        back_outs,
        [ids, q_at, k_at, query, seg_q, seg_k, tiles, lse] + got + blocks,
        scalars=3,
        scratch=back_scratch,
        mib=20 if fast else 56,
        us=30000,
    )
    if fast:
        dq, down, doth, sums = back
        doth = after(doth, *ps)
        middle_send, middle_mine = call(
            middle_half_kernel,
            (shape((2 * R + 16, D), bf16), shape((2 * R, D), f32)),
            [near, middle_more],
            scalars=0,
            us=1,
        )
        middle_last = plane_move(middle_send, 2)
        doth = after(doth, middle_send)
        dmore = core_move(doth)
        keep_p, send_p = call(
            functools.partial(project_grad_kernel, T),
            (shape((4, R, 3 * CG), f32), shape((4 * R, 3 * CG), bf16)),
            [ids, normed, dq, down, doth],
            scratch=[pltpu.VMEM((4, 2, R, 3 * CG), f32)],
        )
        RB = R + RR * D // (3 * CG)
        project_more = core_move(send_p)
    else:
        dq, dall, sums = back
        down = lax.psum_scatter(dall, "seq", scatter_dimension=0, axis_index_groups=members)
        down, dmore = down.astype(bf16), jnp.zeros((HG, 4 * T, 128), bf16)

    own, s1, s2, s3, joined, first_gain = call(
        functools.partial(tail_kernel, T),
        (shape((T, D), f32),)
        + (shape((2 * T, D), bf16),) * 3
        + (shape((4 * T, 3 * CG), bf16), shape((1, D), f32)),
        [ids, x_all, dq, down, dmore, grads, gains] + ws + wo + list(res_send),
        scratch=[pltpu.VMEM((4, 2, RH, 3 * CG), bf16), pltpu.VMEM((4, T, D), f32)],
    )
    table_row = call(functools.partial(table_kernel, T), shape((1, 32 * H), f32), [ids, sums])
    small = shape((8, 3 * CG), f32), shape((16, 3 * CG), bf16)
    extra, extra_send = call(extra_kernel, small, [second_gain, first_gain, table_row], scalars=0, us=1)
    if fast:
        RB = R + RR * D // (3 * CG)
        project_far, project_near, extra = call(
            project_join_kernel,
            (shape((2 * RB + 16, 3 * CG), bf16),)
            + (shape((2 * RB, 3 * CG), f32), shape((8, 3 * CG), f32)),
            [ids, keep_p, project_more, extra, core_move(extra_send), wown] + ps,
            scratch=[pltpu.VMEM((4, 4, RR, 3 * CG), f32), pltpu.VMEM((4, RR, D), f32)],
            us=1,
        )
        send, mine, extra = call(
            project_half_kernel,
            (shape((RB + 16, 3 * CG), bf16), shape((RB, 3 * CG), f32), shape((8, 3 * CG), f32)),
            [after(project_near, middle_last), plane_move(project_far, 1), extra],
            scalars=0,
            us=1,
        )
        more = plane_move(send, 2)
        s1, s2, s3 = after((s1, s2, s3), project_far)
    parts = [group_move(v, k) for k, v in ((1, s1), (2, s2), (3, s3))]
    input_gradient = own + parts[0][:T].astype(f32) + parts[1][:T].astype(f32) + parts[2][:T].astype(f32)
    result = res0 + parts[0][T:].astype(f32) + parts[1][T:].astype(f32) + parts[2][T:].astype(f32)
    if fast:
        inner_mine, outer_mine = call(
            middle_sum_kernel,
            (shape((R, D), f32), shape((R, D), bf16)),
            [middle_mine, middle_last],
            scalars=0,
            us=1,
        )
        pairs = []
        for a in range(GROUPS):
            for b in range(C):
                for z in range(fsdps):
                    pairs.append(((a * C + b) * fsdps + z, ((a ^ z) * C + b) * fsdps + z))
        outer_got = lax.ppermute(outer_mine, ("seq", "fsdp"), pairs)
        wide = 3 * CG + D
        t1, t2, t3, tmine, extra, output_grad = call(
            project_plane_kernel,
            (shape((RR + 8, wide), bf16),) * 3
            + (shape((RR, wide), f32), shape((8, 3 * CG), f32), shape((RR, D), f32)),
            [ids, mine, more, extra, inner_mine],
            scratch=[pltpu.VMEM((4, RR, 3 * CG), f32), pltpu.VMEM((4, RR, D), f32)],
            us=1,
        )
        ts = [group_move(t, k) for k, t in ((1, t1), (2, t2), (3, t3))]
        where = jnp.stack([g, position * fsdps + f]).astype(jnp.int32)
        count = D // (seqs * fsdps)
        query_grad, key_grad, value_grad, inner_grad, first_grad, second_grad, table_grad, outer_grad = call(
            final_kernel,
            (shape((RR, D), f32),) * 3
            + (shape((RR, 4 * F0), f32), shape((1, count), f32), shape((1, count), f32), shape((H, 32), f32))
            + (shape((R, D), f32),),
            [where, tmine] + ts + [extra, outer_got],
            scratch=[pltpu.VMEM((4, RR, wide), f32), pltpu.VMEM((D // count, count), f32)],
            us=1,
        )
        first_grad, second_grad = first_grad.reshape(count), second_grad.reshape(count)
        table_grad = table_grad.T
    else:
        FB = F0 // 8
        axes = ("seq", "fsdp")

        def product(left, right):
            return lax.optimization_barrier(mm(left, right, TN))

        def spread(whole, axis):
            blocks = []
            for z in range(4):
                for e in range(2):
                    block = lax.slice_in_dim(whole, (4 * e + z) * FB, (4 * e + z + 1) * FB, axis=axis)
                    blocks += [block * (b == (z ^ g)).astype(f32) for b in range(4)]
            return jnp.concatenate(blocks, axis=axis)

        inner_w = spread(product(normed_ffn, ginner), 1)
        outer_w = spread(product(active, cot_all.reshape(4 * T, D)), 0)
        out_w = jnp.zeros((4, CG, D), f32)
        for k in range(4):
            out_w = lax.dynamic_update_slice_in_dim(out_w, product(ctx_all[k], branch)[None], k, 0)
        joined_w = product(normed, joined)
        pairs_w = joined_w[:, : 2 * CG].reshape(D, HG, 2, DH)

        def whole(part):
            return lax.dynamic_update_slice(jnp.zeros((D, D), f32), part.reshape(D, CG), (0, g * CG))

        def scatter(part):
            return lax.psum_scatter(part, axes, scatter_dimension=0, tiled=True)

        query_grad = scatter(whole(joined_w[:, 2 * CG :]))
        key_grad = scatter(whole(pairs_w[:, :, 0]))
        value_grad = scatter(whole(pairs_w[:, :, 1]))
        output_grad = scatter(out_w.reshape(D, D))
        inner_grad = scatter(inner_w)
        outer_grad = scatter(outer_w)
        extra = lax.psum(extra, axes)
        at = position * fsdps + f
        count = D // (seqs * fsdps)
        second_vec = jnp.concatenate([extra[0, : D // 2], extra[1, : D // 2]])
        first_vec = jnp.concatenate([extra[2, : D // 2], extra[3, : D // 2]])
        second_grad = lax.dynamic_slice_in_dim(second_vec, at * count, count)
        first_grad = lax.dynamic_slice_in_dim(first_vec, at * count, count)
        table_grad = extra[4, : 32 * H].reshape(H, 32).T
    return (
        result[None],
        input_gradient[None],
        first_grad,
        query_grad,
        key_grad,
        value_grad,
        output_grad,
        table_grad,
        second_grad,
        inner_grad,
        outer_grad,
    )


def solution(mesh):
    return jax.shard_map(
        functools.partial(on_device, mesh.shape["seq"], mesh.shape["fsdp"]),
        mesh=mesh,
        in_specs=(
            P("fsdp", "seq", None),
            P("fsdp", "seq"),
            P("fsdp", "seq", None),
            P("fsdp"),
            P("fsdp", None),
            P("fsdp", None),
            P("fsdp", None),
            P("fsdp", None),
            P("fsdp", None),
            P("fsdp"),
            P("fsdp", None),
            P("fsdp", None),
        ),
        out_specs=(
            P("fsdp", "seq", None),
            P("fsdp", "seq", None),
            P(("seq", "fsdp")),
            P(("seq", "fsdp"), None),
            P(("seq", "fsdp"), None),
            P(("seq", "fsdp"), None),
            P(("seq", "fsdp"), None),
            P(),
            P(("seq", "fsdp")),
            P(("seq", "fsdp"), None),
            P(("seq", "fsdp"), None),
        ),
        check_vma=False,
    )
```

```python
import functools

import jax
import jax.numpy as jnp
from jax import lax
from jax.experimental import pallas as pl
from jax.experimental.pallas import tpu as pltpu
from jax.sharding import PartitionSpec as P

D = 768
H = 12
DH = 64
GROUPS = 4
HG = H // GROUPS
CG = HG * DH

epsilon = 1e-06
FORCE_GENERIC = False
SCALE = 10**6
neg_fill = -1e30
limits = (12, 16, 23, 32, 46, 64, 91)
root_half = 0.7071067811865476
inv_root_tau = 0.3989422804014327
bf16 = jnp.bfloat16
f32 = jnp.float32
NT = (((1,), (1,)), ((), ()))
TN = (((0,), (0,)), ((), ()))
NN = (((1,), (0,)), ((), ()))


def mm(a, b, dims=NN):
    return lax.dot_general(a, b, dims, preferred_element_type=f32)


def bucket_of(offset):
    distance = jnp.abs(offset)
    farther = jnp.zeros_like(offset) + 8
    for limit in limits:
        farther = farther + (distance >= limit).astype(jnp.int32)
    nearer = jnp.where(distance < 8, distance, farther)
    return nearer + jnp.where(offset > 0, 16, 0)


def call(kernel, outs, args, scalars=1, scratch=(), mib=12, us=2, far=()):
    vmem = pl.BlockSpec(memory_space=pltpu.VMEM)
    smem = pl.BlockSpec(memory_space=pltpu.SMEM)
    hbm = pl.BlockSpec(memory_space=pltpu.HBM)
    return pl.pallas_call(
        kernel,
        out_shape=outs,
        in_specs=[smem] * scalars + [hbm if n in far else vmem for n in range(scalars, len(args))],
        out_specs=jax.tree.map(lambda _: vmem, outs),
        scratch_shapes=scratch,
        compiler_params=pltpu.CompilerParams(vmem_limit_bytes=mib << 20),
        cost_estimate=pl.CostEstimate(flops=us * SCALE, bytes_accessed=1 << 10, transcendentals=0),
    )(*args)


def shape(dims, kind):
    return jax.ShapeDtypeStruct(dims, kind)


def project_kernel(T, fast, ids, *refs):
    half, f = ids[1], ids[2]
    ws, os = refs[0:4], refs[4:8]
    xs = [refs[8].at[k] for k in range(4)]
    if fast:
        xs += [refs[9].at[k] for k in range(4)]
    normed, kv, query, marks, gains, table, W, small = refs[-8:]
    rows = W.shape[2]
    for k in range(4):
        z = f ^ k
        W[z, half] = ws[k][:rows, :]
        W[z, 1 - half] = os[k][:rows, :]
        small[z] = ws[k][rows:, :].astype(f32)
    gain = jnp.concatenate([small[z, 0:1, 0 : D // 4] for z in range(4)], axis=1)
    gains[0:1, :] = gain
    gains[1:2, :] = jnp.concatenate([small[z, 1:2, 0 : D // 4] for z in range(4)], axis=1)
    table[...] = jnp.concatenate([small[z, 8:16, 0:128] for z in range(4)], axis=0)
    weight = W[...].reshape(D, 3 * CG)
    count = len(xs)
    seg = [xs[k][T:, :].astype(f32)[0:1, :128] for k in range(count)]
    marks[...] = jnp.concatenate(seg + [jnp.zeros((8 - count, 128), f32)] * (count < 8), axis=0)
    for i in range(count // 2):
        parts = []
        for k in (2 * i, 2 * i + 1):
            x = xs[k][:T, :].astype(f32)
            s = lax.rsqrt(jnp.mean(x * x, axis=-1, keepdims=True) + epsilon)
            parts.append((x * s * gain).astype(bf16))
        n = jnp.concatenate(parts, axis=0)
        at = slice(2 * i * T, (2 * i + 2) * T)
        normed[at, :] = n
        out = mm(n, weight if i < 2 else weight[:, : 2 * CG])
        for h in range(HG):
            kv[h, at, :] = out[:, 128 * h : 128 * h + 128].astype(bf16)
        if i < 2:
            blank = jnp.zeros((2 * T, DH), f32)
            for h in range(HG):
                q = out[:, 2 * CG + DH * h : 2 * CG + DH * (h + 1)]
                query[h, at, :] = jnp.concatenate([q, blank], axis=1).astype(bf16)


def tiles_kernel(T, ids, table, tiles):
    g = ids[0]
    lane = lax.broadcasted_iota(jnp.int32, (32, 128), 1)
    m = lax.broadcasted_iota(jnp.int32, (32, 2 * T), 1)
    label = lax.broadcasted_iota(jnp.int32, (32, 2 * T), 0)
    for h in range(HG):
        column = jnp.sum(jnp.where(lane == HG * g + h, table[...], 0.0), axis=1, keepdims=True)
        for d in range(5):
            if d in (0, 4):
                one = column[15 if d == 0 else 31 :][:1, :]
                tiles[h, d] = jnp.broadcast_to(one, (T, T))
                continue
            offset = T * (d - 2) - jnp.where(m < T, m, m - 2 * T)
            hot = jnp.where(bucket_of(offset) == label, column, 0.0)
            along = jnp.sum(hot, axis=0, keepdims=True)
            wide = jnp.broadcast_to(along, (T, 2 * T))
            tiles[h, d] = pltpu.roll(wide, 0, 1, stride=1, stride_axis=0)[:, :T]


def tile_of(key_at, query_at):
    return jnp.clip(key_at - query_at, -2, 2) + 2


def mark_columns(T, count, marks, columns):
    across = jnp.concatenate([marks[...], jnp.zeros((128 - marks.shape[0], 128), f32)], axis=0).T
    for t in range(count):
        columns[t] = jnp.broadcast_to(across[:, t : t + 1], (T, 128))


def masked_scores(T, scores, base, pair, h, q_at, k_at, seg_q, columns, tiles):
    pieces = []
    for t in range(8):
        kt = base + t
        bias = jnp.concatenate([tiles[h, tile_of(k_at[kt], q_at[2 * pair + j])] for j in range(2)], axis=1)
        column = jnp.concatenate([columns[kt], columns[kt]], axis=1)
        piece = scores[t * T : (t + 1) * T] + bias
        pieces.append(jnp.where(column == seg_q, piece, neg_fill))
    return jnp.concatenate(pieces, axis=0)


def pick_keys(blocks, i, h):
    if len(blocks[0].shape) == 3:
        return blocks[0][h]
    return jnp.concatenate([blocks[0][2 * i, h], blocks[0][2 * i + 1, h]], axis=0)


def forward_kernel(T, nb, fast, ids, q_at, k_at, query, seg_q, seg_k, tiles, *rest):
    blocks, (context, lse, columns) = rest[:-3], rest[-3:]
    mark_columns(T, nb * 4, seg_k, columns)

    def pair_step(pair, carry):
        at = pl.ds(pl.multiple_of(pair * 2 * T, 2 * T), 2 * T)
        seg = jnp.concatenate([seg_q[pl.ds(2 * pair + j, 1), :] for j in range(2)], axis=1)
        out = []
        for h in range(HG):
            q = query[h, at, :]

            def chunk(i, state):
                peak, total, acc = state
                keys = pick_keys(blocks, i, h)
                s = masked_scores(T, mm(keys, q, NT), 8 * i, pair, h, q_at, k_at, seg, columns, tiles)
                top = jnp.maximum(peak, jnp.max(s, axis=0, keepdims=True))
                p = jnp.exp(s - top)
                fade = jnp.exp(peak - top)
                total = total * fade + jnp.sum(p, axis=0, keepdims=True)
                acc = acc * fade + mm(keys, p.astype(bf16), TN)
                return top, total, acc

            start = (
                jnp.full((1, 2 * T), neg_fill, f32),
                jnp.zeros((1, 2 * T), f32),
                jnp.zeros((128, 2 * T), f32),
            )
            if fast:
                peak, total, acc = chunk(0, start)
            else:
                peak, total, acc = lax.fori_loop(0, nb // 2, chunk, start)
            out.append(acc[DH:, :] / total)
            lse[pair, h : h + 1, :] = peak + jnp.log(total)
        joined = jnp.concatenate(out, axis=0)
        context[at, :] = joined.T.astype(bf16)
        return carry

    lax.fori_loop(0, 2, pair_step, 0)


def backward_kernel(T, nb, fast, ids, q_at, k_at, query, seg_q, seg_k, tiles, lse, g0, g1, g2, g3, *rest):
    nin = 1
    blocks = rest[:nin]
    if fast:
        dquery, down, doth, sums, columns, dkv = rest[nin:]
    else:
        dquery, dkv, sums, columns = rest[nin:]
    mark_columns(T, nb * 4, seg_k, columns)
    sums[...] = jnp.zeros_like(sums)
    dkv[...] = jnp.zeros_like(dkv)

    def pair_step(pair, carry):
        at = pl.ds(pl.multiple_of(pair * 2 * T, 2 * T), 2 * T)
        seg = jnp.concatenate([seg_q[pl.ds(2 * pair + j, 1), :] for j in range(2)], axis=1)
        grad = g0[at, :].astype(f32) + g1[at, :].astype(f32) + g2[at, :].astype(f32) + g3[at, :].astype(f32)
        blank = jnp.zeros((2 * T, DH), f32)
        out = []
        for h in range(HG):
            q = query[h, at, :]
            do = jnp.concatenate([blank, grad[:, DH * h : DH * (h + 1)]], axis=1).astype(bf16)
            row = lse[pair, h : h + 1, :]

            def probs_of(i):
                keys = pick_keys(blocks, i, h)
                s = masked_scores(T, mm(keys, q, NT), 8 * i, pair, h, q_at, k_at, seg, columns, tiles)
                return keys, jnp.exp(s - row), mm(keys, do, NT)

            def finish(i, keys, p, dp, delta):
                ds = p * (dp - delta)
                for t in range(8):
                    for j in range(2):
                        index = tile_of(k_at[8 * i + t], q_at[2 * pair + j])
                        sums[h, index] += ds[t * T : (t + 1) * T, j * T : (j + 1) * T]
                ds = ds.astype(bf16)
                both = jnp.concatenate([ds, p.astype(bf16)], axis=1)
                piece = mm(both, jnp.concatenate([q, do], axis=0))
                if fast:
                    dkv[h] += piece
                else:
                    dkv[2 * i, h] += piece[: 4 * T]
                    dkv[2 * i + 1, h] += piece[4 * T :]
                return mm(keys, ds, TN)[:DH, :]

            if fast:
                keys, p, dp = probs_of(0)
                delta = jnp.sum(p * dp, axis=0, keepdims=True)
                dq = finish(0, keys, p, dp, delta)
            else:

                def first(i, delta):
                    keys, p, dp = probs_of(i)
                    return delta + jnp.sum(p * dp, axis=0, keepdims=True)

                delta = lax.fori_loop(0, nb // 2, first, jnp.zeros((1, 2 * T), f32))

                def second(i, dq):
                    keys, p, dp = probs_of(i)
                    return dq + finish(i, keys, p, dp, delta)

                dq = lax.fori_loop(0, nb // 2, second, jnp.zeros((DH, 2 * T), f32))
            out.append(dq)
        dquery[at, :] = jnp.concatenate(out, axis=0).T.astype(bf16)
        return carry

    lax.fori_loop(0, 2, pair_step, 0)
    if fast:
        for h in range(HG):
            down[h] = dkv[h, : 4 * T, :].astype(bf16)
            doth[h] = dkv[h, 4 * T :, :].astype(bf16)


def exact_mm(value, chosen):
    high = value.astype(bf16)
    low = (value - high.astype(f32)).astype(bf16)
    return mm(high, chosen) + mm(low, chosen)


def table_kernel(T, ids, sums, out):
    g = ids[0]
    row = lax.broadcasted_iota(jnp.int32, (T, T), 0)
    lane = lax.broadcasted_iota(jnp.int32, (T, T), 1)
    mirror = (row + lane == T - 1).astype(bf16)
    blank = jnp.zeros((T, T), f32)
    offset = lax.broadcasted_iota(jnp.int32, (2 * T, 128), 0) - (T - 1)
    label = lax.broadcasted_iota(jnp.int32, (2 * T, 128), 1)
    label8 = lax.broadcasted_iota(jnp.int32, (8, 128), 1)
    total = jnp.zeros((8, 128), f32)
    for d in range(5):
        lines = []
        for h in range(HG):
            if d in (0, 4):
                lines.append(jnp.sum(sums[h, d], axis=0, keepdims=True))
            else:
                moved = jnp.concatenate([exact_mm(sums[h, d], mirror), blank], axis=1)
                moved = pltpu.roll(moved, 0, 1, stride=1, stride_axis=0)
                lines.append(jnp.sum(moved, axis=0, keepdims=True))
        block = jnp.concatenate(lines + [jnp.zeros((8 - HG, lines[0].shape[1]), f32)], axis=0)
        if d in (0, 4):
            whole = jnp.sum(block, axis=1, keepdims=True)
            total = total + jnp.where(label8 == (15 if d == 0 else 31), whole, 0.0)
        else:
            total = total + exact_mm(block, (bucket_of(offset + T * (d - 2)) == label).astype(bf16))
    pieces = []
    for a in range(GROUPS):
        for h in range(HG):
            pieces.append(jnp.where(g == a, total[h : h + 1, :32], 0.0))
    out[...] = jnp.concatenate(pieces, axis=1)


def middle_kernel(T, ids, *refs):
    g, half, f = ids[0], ids[1], ids[2]
    x, ctx, gains = refs[0:3]
    cot_all, ws, others = refs[3], refs[4:8], refs[8:12]
    res0, sends, gcs = refs[12], refs[13:16], refs[16:20]
    grads, normed, active, ginner, branch = refs[20:25]
    WO, W1, W2, held = refs[25:29]
    rows, low = WO.shape[2], WO.shape[2] // 2
    FH = W1.shape[3]
    for k in range(4):
        z = f ^ k
        for at, pieces in ((half, ws), (1 - half, others)):
            piece = pieces[k]
            WO[z, at] = piece[:rows]
            W1[at, z] = piece[rows : 2 * rows]
            W2[at, z, :, 0 : D // 2] = piece[2 * rows : 2 * rows + low]
            W2[at, z, :, D // 2 :] = piece[2 * rows + low :]
    gain = gains[1:2, :]

    def out_rows(a):
        return jnp.concatenate([WO[a, 0], WO[a, 1]], axis=1)

    for i in range(2):
        at = slice(2 * i * T, (2 * i + 2) * T)
        slots = (2 * i, 2 * i + 1)
        att = jnp.concatenate([x[m, :T, :] for m in slots], axis=0).astype(f32)
        cot = jnp.concatenate([cot_all[m] for m in slots], axis=0)
        for a in range(4):
            att = att + mm(ctx[a, at, :], out_rows(a))
        s = lax.rsqrt(jnp.mean(att * att, axis=-1, keepdims=True) + epsilon)
        n = (att * s * gain).astype(bf16)
        normed[at, :] = n
        result = None
        gn = None
        for c in range(2):
            columns = slice(c * FH, (c + 1) * FH)
            w1 = W1[c].reshape(D, FH)
            w2 = W2[c].reshape(FH, D)
            inner = mm(n, w1)
            cdf = 0.5 * (1.0 + lax.erf(inner * root_half))
            act = (inner * cdf).astype(bf16)
            slope = cdf + inner * jnp.exp(-0.5 * inner * inner) * inv_root_tau
            part = mm(act, w2)
            result = part if result is None else result + part
            ga = mm(cot, w2, NT).astype(bf16)
            gi = (ga.astype(f32) * slope).astype(bf16)
            part = mm(gi, w1, NT)
            gn = part if gn is None else gn + part
            active[at, columns] = act
            ginner[at, columns] = gi
        for index, m in enumerate(slots):
            held[m] = result[index * T : (index + 1) * T]

            @pl.when(g == m)
            def _():
                held[m] += att[index * T : (index + 1) * T]

        u = gn * gain
        grad = 0.25 * cot.astype(f32) + s * u - att * (s * s * s) * jnp.mean(u * att, axis=-1, keepdims=True)
        grads[at, :] = grad
        gb = grad.astype(bf16)
        branch[at, :] = gb
        for k in range(4):
            gcs[k][at, :] = mm(gb, out_rows(g ^ k), NT).astype(bf16)
    res0[...] = held[g]
    for k in (1, 2, 3):
        sends[k - 1][...] = held[g ^ k].astype(bf16)


def weight_kernel(T, ids, normed, active, ginner, branch, cot, ctx, keep, send, gi, go, gw):
    c = ids[3]
    R = D // 8
    gi[...] = mm(normed[...], ginner[...], TN).reshape(4, 2, R, D)
    go[...] = mm(active[...], cot[...].reshape(4 * T, D), TN).reshape(2, 4, R, D)
    gb = branch[...]
    for a in range(4):
        gw[a] = mm(ctx[a], gb, TN).reshape(2, R, D)
    for a in range(4):
        keep[0, a] = gi[a, c]
        keep[1, a] = go[c, a]
        keep[2, a] = gw[a, c]
        send[0, a] = gi[a, 1 - c].astype(bf16)
        send[1, a] = go[1 - c, a].astype(bf16)
        send[2, a] = gw[a, 1 - c].astype(bf16)


def tail_kernel(T, ids, x_all, dq, down, doth, grads, gains, *refs):
    g, half, f = ids[0], ids[1], ids[2]
    ws, os, rs = refs[0:4], refs[4:8], refs[8:11]
    own, s1, s2, s3, joined, W, held = refs[11:]
    rows = W.shape[2]
    sends = (s1, s2, s3)
    for k in range(4):
        z = f ^ k
        W[z, half] = ws[k][:rows, :]
        W[z, 1 - half] = os[k][:rows, :]
    weight = W[...].reshape(D, 3 * CG)
    gain = gains[0:1, :]
    for i in range(2):
        at = slice(2 * i * T, (2 * i + 2) * T)
        parts = [(down[h, at, :].astype(f32) + doth[h, at, :].astype(f32)).astype(bf16) for h in range(HG)]
        dqkv = jnp.concatenate(parts + [dq[at, :]], axis=1)
        joined[at, :] = dqkv
        gn = mm(dqkv, weight, NT)
        x = jnp.concatenate([x_all[m, :T, :] for m in (2 * i, 2 * i + 1)], axis=0).astype(f32)
        s = lax.rsqrt(jnp.mean(x * x, axis=-1, keepdims=True) + epsilon)
        u = gn * gain
        total = grads[at, :] + s * u - x * (s * s * s) * jnp.mean(u * x, axis=-1, keepdims=True)
        for index, m in enumerate((2 * i, 2 * i + 1)):
            held[m] = total[index * T : (index + 1) * T]
    own[...] = held[g]
    for k in (1, 2, 3):
        sends[k - 1][:T, :] = held[g ^ k].astype(bf16)
        sends[k - 1][T:, :] = rs[k - 1][...]


def split_rows(value):
    high = value.astype(bf16)
    return jnp.concatenate([high, (value - high.astype(f32)).astype(bf16)], axis=0)


def project_grad_kernel(T, ids, normed, dq, down, doth, keep, send, gw):
    c = ids[3]
    R = D // 8
    own = jnp.concatenate([down[h] for h in range(HG)], axis=1)
    other = jnp.concatenate([doth[h] for h in range(HG)], axis=1)
    pairs = mm(normed[...], jnp.concatenate([own, other], axis=0), TN)
    single = mm(normed[: 4 * T, :], dq[...], TN)
    gw[...] = jnp.concatenate([pairs, single], axis=1).reshape(4, 2, R, 3 * CG)
    for a in range(4):
        keep[a] = gw[a, c]
        send[a * R : (a + 1) * R, :] = gw[a, 1 - c].astype(bf16)


def extra_kernel(table, block, send):
    rows = jnp.concatenate([table[...], jnp.zeros((1, 3 * CG - 32 * H), f32)], axis=1)
    rows = jnp.concatenate([rows, jnp.zeros((7, 3 * CG), f32)], axis=0)
    block[...] = rows
    send[...] = split_rows(rows)


def start_kernel(T, C, ids, q, k, v, first, second, table, x, seg, out, x_out, small, held, gain1, gain2, rows8, marks, sems):
    place = lax.axis_index("seq")
    g = lax.div(place, C)
    side = lax.rem(place, C) if ids is None else ids[1]
    rows = out.shape[0] - 16
    at = pl.ds(pl.multiple_of(side * rows, rows), rows)
    lanes = pl.ds(pl.multiple_of(128 * (g + lax.div(g, 2)), 128), 256)
    pairs = [(w.at[at, lanes], held.at[n]) for n, w in enumerate((q, k, v))]
    pairs += [(first, gain1), (second, gain2), (table, rows8), (seg, marks), (x.at[0], x_out.at[:T])]
    copies = [pltpu.make_async_copy(a, b, sems.at[n]) for n, (a, b) in enumerate(pairs)]
    for copy in copies:
        copy.start()
    small[...] = jnp.zeros_like(small)
    for copy in copies:
        copy.wait()
    mark = jnp.concatenate([marks[...].astype(f32), jnp.zeros((15, T), f32)], axis=0)
    x_out[T:, :] = jnp.concatenate([mark, jnp.zeros((16, D - T), f32)], axis=1).astype(bf16)
    small[0:1, 0 : D // 4] = gain1[...].reshape(1, D // 4).astype(f32)
    small[1:2, 0 : D // 4] = gain2[...].reshape(1, D // 4).astype(f32)
    small[8:16, 0:H] = rows8[...].astype(f32)
    out[rows:, :] = small[...].astype(bf16)
    for odd in range(2):

        @pl.when(lax.rem(g, 2) == odd)
        def _():
            pieces = []
            for h in range(HG):
                here = slice(DH * (odd + h), DH * (odd + h + 1))
                pieces += [held[1, :, here], held[2, :, here]]
            pieces.append(held[0, :, DH * odd : DH * odd + CG])
            out[:rows, :] = jnp.concatenate(pieces, axis=1)


def middle_pack_kernel(C, ids, wo, inner, outer, out, held, block, sems):
    place, f = lax.axis_index("seq"), lax.axis_index("fsdp")
    g = lax.div(place, C)
    side = lax.rem(place, C) if ids is None else ids[1]
    R0, F0 = wo.shape[0], outer.shape[0]
    FB, low = F0 // 8, R0 // 2
    half = F0 // 2
    pairs = [
        (wo.at[:, pl.ds(pl.multiple_of(side * half, 128), half)], out.at[:R0]),
        (outer.at[pl.ds(pl.multiple_of(side * half + FB * (f ^ g), FB), FB)], block),
    ]
    for z in range(4):
        base = (2 * z + side) * half + 128 * lax.div(z ^ g, 2)
        pairs.append((inner.at[:, pl.ds(pl.multiple_of(base, 128), 256)], held.at[z]))
    copies = [pltpu.make_async_copy(a, b, sems.at[n]) for n, (a, b) in enumerate(pairs)]
    for copy in copies:
        copy.start()
    for copy in copies:
        copy.wait()
    for a in range(GROUPS):

        @pl.when(g == a)
        def _():
            starts = [FB * (z ^ a) - 128 * ((z ^ a) // 2) for z in range(4)]
            picked = jnp.concatenate([held[z, :, n : n + FB] for z, n in enumerate(starts)], axis=1)
            out[R0 : 2 * R0, :] = picked

    out[2 * R0 : 2 * R0 + low, :] = block[:, : D // 2]
    out[2 * R0 + low :, :] = block[:, D // 2 :]


def added(refs):
    value = refs[0][...].astype(f32)
    for r in refs[1:]:
        value = value + r[...].astype(f32)
    return value


def join_kernel(ids, keep, more, far, near, p1, p2, p3, wown, total):
    g, f = ids[0], ids[2]
    R = D // 8
    total[...] = (keep[0] + more[0].astype(f32)).reshape(4, 4, R // 4, D)

    def toward(at):
        right = keep[1, at ^ g] + more[1, at ^ g].astype(f32)
        return [total[a, at] for a in range(4)] + [right]

    far[...] = jnp.concatenate(toward(f ^ 2) + toward(f ^ 3), axis=0).astype(bf16)
    near[...] = jnp.concatenate(toward(f) + toward(f ^ 1), axis=0)
    for k, out in enumerate((wown, p1, p2, p3)):
        out[...] = (keep[2, g ^ k] + more[2, g ^ k].astype(f32)).astype(out.dtype)


def middle_half_kernel(near, more, send, mine):
    value = near[...] + more[...].astype(f32)
    count = mine.shape[0]
    mine[...] = value[:count]
    send[...] = value[count:].astype(bf16)


def rows_kernel(ids, *refs):
    qs, ws, os = refs[0:4], refs[4:8], refs[8:12]
    first, second, narrow_rows, wide_rows = refs[12:16]
    half, f, c = ids[1], ids[2], ids[3]
    R = D // 8
    RR, R0 = R // 4, D // 4
    for k in range(4):
        narrow_rows[f ^ k] = qs[k][:R, :].astype(f32)
        for at, pieces in ((half, ws), (1 - half, os)):
            wide_rows[f ^ k, at] = pieces[k][R0 : 2 * R0, :].astype(f32)
    at = pl.ds(pl.multiple_of(RR * f, 8), RR)
    there = pl.ds(pl.multiple_of(R * c + RR * f, 8), RR)
    for a in range(4):
        first[a * RR : (a + 1) * RR, :] = narrow_rows[a, at, :]
        rows = jnp.concatenate([wide_rows[a, 0, there, :], wide_rows[a, 1, there, :]], axis=1)
        second[a * RR : (a + 1) * RR, :] = rows


def middle_sum_kernel(own, more, rows, inner, outer, sums):
    R = D // 8
    value = own[...] + more[...].astype(f32)
    inner[...] = value[:R]
    outer[...] = value[R:].astype(bf16)
    sums[...] = jnp.sum(rows[...] * value[:R], axis=1, keepdims=True)


def unsplit(block):
    return block[:8] + block[8:]


def narrow(block):
    wide = 3 * CG
    right = block[:, wide:]
    rows = block.shape[0] // 3
    folded = jnp.concatenate([right[n * rows : (n + 1) * rows] for n in range(3)], axis=1)
    return jnp.concatenate([block[:, :wide], folded], axis=0)


def widen(block):
    rows = D // 32
    folded = block[rows:]
    wide = D - 3 * CG
    right = jnp.concatenate([folded[:, n * wide : (n + 1) * wide] for n in range(3)], axis=0)
    return jnp.concatenate([block[:rows], right], axis=1)


def project_join_kernel(ids, keep, more, extra, extra_more, wown, p1, p2, p3, far, near, extra_out, total, out_total):
    f = ids[2]
    R = D // 8
    total[...] = (keep[...] + more[...].astype(f32).reshape(4, R, 3 * CG)).reshape(4, 4, R // 4, 3 * CG)
    out_total[...] = added((wown, p1, p2, p3)).reshape(4, R // 4, D)
    ex = extra[...] + unsplit(extra_more[...].astype(f32))
    extra_out[...] = ex

    def toward(at):
        return [total[a, at] for a in range(4)]

    far[: 2 * R, :] = jnp.concatenate(toward(f ^ 1) + toward(f ^ 3), axis=0).astype(bf16)
    data = jnp.concatenate([narrow(out_total[f ^ 1]), narrow(out_total[f ^ 3])], axis=0).astype(bf16)
    far[2 * R : 2 * R + data.shape[0], :] = data
    far[2 * R + data.shape[0] :, :] = split_rows(ex)
    kept = [toward(at) + [narrow(out_total[at])] for at in (f, f ^ 2)]
    near[...] = jnp.concatenate(kept[0] + kept[1], axis=0)


def project_half_kernel(near, more, extra, send, mine, extra_out):
    R = D // 8
    got, tail = more[: 2 * R, :].astype(f32), more[2 * R :, :].astype(f32)
    count = mine.shape[0]
    low = count - R
    ex = extra[...] + unsplit(tail[2 * low :])
    extra_out[...] = ex
    mine[:R, :] = near[:R, :] + got[:R]
    mine[R:, :] = near[R:count, :] + tail[:low]
    send[:R, :] = (near[count : count + R, :] + got[R:]).astype(bf16)
    send[R:count, :] = (near[count + R :, :] + tail[low : 2 * low]).astype(bf16)
    send[count:, :] = split_rows(ex)


def project_plane_kernel(ids, own, more, extra, inner, second, rows, s1, s2, s3, mine, extra_out, output, total, held, sums):
    g = ids[0]
    R = D // 8
    RR = R // 4
    got = more[...].astype(f32)
    value = own[...] + got[: own.shape[0]]
    ex = extra[...] + unsplit(got[own.shape[0] :])
    extra_out[...] = ex
    output[...] = widen(value[R:])
    total[...] = value[:R].reshape(4, RR, 3 * CG)
    held[...] = inner[...].reshape(4, RR, D)
    products = jnp.sum(rows[...] * value[:R], axis=1, keepdims=True)
    lane = lax.broadcasted_iota(jnp.int32, (RR, 128), 1)
    for a in range(4):
        one = products[a * RR : (a + 1) * RR, :]
        two = second[a * RR : (a + 1) * RR, :]
        columns = jnp.zeros((RR, 128), f32)
        for n, part in enumerate((one, two)):
            high = part.astype(bf16).astype(f32)
            columns = jnp.where(lane == 2 * n, high, columns)
            columns = jnp.where(lane == 2 * n + 1, part - high, columns)
        sums[a] = columns
    high = ex.astype(bf16).astype(f32)
    low = ex - high
    width = 3 * CG + D + 128
    tail = jnp.concatenate([high[:, : D // 2], low[:, : D // 2], jnp.zeros((8, width - D), f32)], axis=1)
    for k, out in enumerate((mine, s1, s2, s3)):
        block = jnp.concatenate([total[g ^ k], held[g ^ k], sums[g ^ k]], axis=1)
        out[...] = block if k == 0 else jnp.concatenate([block, tail], axis=0).astype(bf16)


def final_kernel(where, own, r1, r2, r3, extra, outer_in, gains, query, key, value, inner, first, second, table, outer, slots, rows):
    g, at = where[0], where[1]
    RR = D // 32
    ex = extra[...][:, : D // 2]
    slots[g] = own[...]
    for k, r in ((1, r1), (2, r2), (3, r3)):
        got = r[...].astype(f32)
        slots[g ^ k] = got[:RR]
        ex = ex + got[RR:, : D // 2] + got[RR:, D // 2 : D]
    query[...] = jnp.concatenate([slots[a, :, 2 * CG : 3 * CG] for a in range(4)], axis=1)
    for part, out in enumerate((key, value)):
        starts = [128 * h + DH * part for h in range(HG)]
        out[...] = jnp.concatenate([slots[a, :, n : n + DH] for a in range(4) for n in starts], axis=1)
    base = 3 * CG
    for z in range(4):
        for e in range(2):
            n = base + (4 * e + z) * 4 * RR
            inner[:, (8 * z + 4 * e) * 4 * RR : (8 * z + 4 * e + 4) * 4 * RR] = jnp.concatenate(
                [slots[z ^ b, :, n : n + 4 * RR] for b in range(4)], axis=1
            )
    columns = slots[0, :, base + D :] + slots[1, :, base + D :] + slots[2, :, base + D :] + slots[3, :, base + D :]
    square = jnp.concatenate([columns, jnp.zeros((128 - RR, 128), f32)], axis=0).T
    for n, out in enumerate((first, second)):
        whole = gains[n : n + 1, :]
        rows[...] = jnp.concatenate([whole[:, RR * m : RR * (m + 1)] for m in range(D // RR)], axis=0)
        out[...] = (square[2 * n : 2 * n + 1, :RR] + square[2 * n + 1 : 2 * n + 2, :RR]) / rows[pl.ds(at, 1), :]
    table[...] = jnp.concatenate([ex[0:1, 32 * h : 32 * (h + 1)] for h in range(H)], axis=0)
    outer[...] = outer_in[...].astype(f32)


def on_device(seqs, fsdps, *args):
    (
        activations,
        segments,
        cotangent,
        attention_gain,
        query_weight,
        key_weight,
        value_weight,
        output_weight,
        bias_table,
        feedforward_gain,
        inner_weight,
        outer_weight,
    ) = args
    T = activations.shape[1]
    C = seqs // GROUPS
    fast = C == 2 and not FORCE_GENERIC
    position = lax.axis_index("seq")
    f = lax.axis_index("fsdp")
    g, c = position // C, position % C
    half = c if fast else 0
    ids = jnp.stack([g, half, f, c]).astype(jnp.int32)
    R0 = query_weight.shape[0]
    RH = R0 // 2
    F0 = outer_weight.shape[0]

    def group_move(value, k):
        pairs = [(a * C + b, (a ^ k) * C + b) for a in range(GROUPS) for b in range(C)]
        return lax.ppermute(value, "seq", pairs)

    def plane_move(value, k):
        return lax.ppermute(value, "fsdp", [(i, i ^ k) for i in range(fsdps)])

    def core_move(value):
        return lax.ppermute(value, "seq", [(i, i ^ 1) for i in range(seqs)])

    def from_group(value):
        return [value] + [group_move(value, k) for k in (1, 2, 3)]

    def from_planes(value):
        return [value] + [plane_move(value, k) for k in (1, 2, 3)]

    def ids_for(side):
        return jnp.stack([g, jnp.asarray(side, jnp.int32), f, c]).astype(jnp.int32)

    def start(side):
        own = fast and side is half
        kernel = functools.partial(start_kernel, T, C)
        return call(
            functools.partial(kernel, None) if own else kernel,
            (shape((RH + 16, 3 * CG), bf16), shape((T + 16, D), bf16)),
            ([] if own else [ids_for(side)])
            + [
                query_weight,
                key_weight,
                value_weight,
                attention_gain,
                feedforward_gain,
                bias_table,
                activations,
                segments,
            ],
            scratch=[
                pltpu.VMEM((16, 3 * CG), f32),
                pltpu.VMEM((3, RH, 256), bf16),
                pltpu.VMEM((R0,), bf16),
                pltpu.VMEM((R0,), bf16),
                pltpu.VMEM(bias_table.shape, bf16),
                pltpu.VMEM((1, T), jnp.int32),
                pltpu.SemaphoreType.DMA((8,)),
            ],
            us=1,
            mib=60,
            scalars=0 if own else 1,
            far=range(9),
        )

    def middle_pack(side):
        own = fast and side is half
        kernel = functools.partial(middle_pack_kernel, C)
        return call(
            functools.partial(kernel, None) if own else kernel,
            shape((3 * R0, D // 2), bf16),
            ([] if own else [ids_for(side)]) + [output_weight, inner_weight, outer_weight],
            scratch=[
                pltpu.VMEM((4, R0, 256), bf16),
                pltpu.VMEM((F0 // 8, D), bf16),
                pltpu.SemaphoreType.DMA((6,)),
            ],
            us=1,
            mib=60,
            scalars=0 if own else 1,
            far=range(4),
        )

    def after(values, *earlier):
        return lax.optimization_barrier((values, earlier))[0]

    def ring(value):
        return lax.ppermute(value, "fsdp", [(i, (i + 1) % fsdps) for i in range(fsdps)])

    token_groups = [[a * C + b for a in range(GROUPS)] for b in range(C)]

    def gather(value):
        return lax.all_gather(value, "seq", axis=0, axis_index_groups=token_groups)

    w_pack, x_pack = start(half)
    output_weight, inner_weight, outer_weight, w_pack = after(
        (output_weight, inner_weight, outer_weight, w_pack), w_pack
    )
    m_pack = middle_pack(half)
    ws = from_planes(w_pack)
    m1, m2 = plane_move(m_pack, 1), plane_move(m_pack, 2)
    x_all = gather(after(x_pack, m_pack))
    if fast:
        xo = [core_move(after(x_all, *ws))]
        wo = [core_move(w) for w in ws]
    else:
        xo = []
        wo = from_planes(start(1)[0])

    wide_t = (8 if fast else 4) * T
    normed, kv, query, marks, gains, table = call(
        functools.partial(project_kernel, T, fast),
        (
            shape((wide_t, D), bf16),
            shape((HG, wide_t, 128), bf16),
            shape((HG, 4 * T, 128), bf16),
            shape((8, 128), f32),
            shape((8, D), f32),
            shape((32, 128), f32),
        ),
        [ids] + ws + wo + [x_all] + xo,
        scratch=[pltpu.VMEM((4, 2, RH, 3 * CG), bf16), pltpu.VMEM((4, 16, 3 * CG), f32)],
        us=1,
    )
    tiles = call(functools.partial(tiles_kernel, T), shape((HG, 5, T, T), f32), [ids, table], us=1)

    slot = jnp.arange(4, dtype=jnp.int32)
    q_at = slot * C + c
    seg_q = marks
    blocks = [kv]
    if fast:
        seg_k = marks
        k_at = jnp.concatenate([slot * C + c, slot * C + 1 - c])
    else:
        members = [[a * C + b for b in range(C)] for a in range(GROUPS)]
        blocks = [lax.all_gather(kv, "seq", axis=0, axis_index_groups=members)]
        seg_k = lax.all_gather(marks[:4].astype(bf16), "seq", axis=0, axis_index_groups=members)
        seg_k = seg_k.reshape(C * 4, T).astype(f32)
        k_at = (slot[None, :] * C + jnp.arange(C, dtype=jnp.int32)[:, None]).reshape(C * 4)
    context, lse = call(
        functools.partial(forward_kernel, T, C, fast),
        (shape((4 * T, CG), bf16), shape((2, 8, 2 * T), f32)),
        [ids, q_at, k_at, query, seg_q, seg_k, tiles] + blocks,
        scalars=3,
        scratch=[pltpu.VMEM((C * 4, T, 128), f32)],
        mib=16 if fast else 48,
        us=1,
    )
    if fast:
        mo = [core_move(m_pack)]
        ctx_all = gather(after(context, *mo))
        m1, m2 = after((m1, m2), ctx_all)
        m3 = plane_move(m2, 1)
        mo += [core_move(m1), core_move(m2)]
        cot_all = gather(after(cotangent[0], ctx_all, *mo))
        m3 = after(m3, cot_all)
        mo.append(core_move(m3))
    else:
        ctx_all = gather(context)
        m3 = plane_move(m2, 1)
        cot_all = gather(cotangent[0])
        mo = from_planes(middle_pack(1))
    ms = (m_pack, m1, m2, m3)

    FH = F0 // 2
    outs = call(
        functools.partial(middle_kernel, T),
        (shape((T, D), f32),)
        + (shape((T, D), bf16),) * 3
        + (shape((4 * T, CG), bf16),) * 4
        + (shape((4 * T, D), f32),)
        + (shape((4 * T, D), bf16),) * 4,
        [ids, x_all, ctx_all, gains, cot_all] + list(ms) + mo,
        scratch=[
            pltpu.VMEM((4, 2, R0, D // 2), bf16),
            pltpu.VMEM((2, 4, R0, FH), bf16),
            pltpu.VMEM((2, 4, F0 // 8, D), bf16),
            pltpu.VMEM((4, T, D), f32),
        ],
        mib=24,
        us=10,
    )
    res0, res_send, gcs = outs[0], outs[1:4], outs[4:8]
    grads, normed_ffn, active, ginner, branch = outs[8:13]
    got = [gcs[0]] + [group_move(gcs[k], k) for k in (1, 2, 3)]
    R = D // 8
    keep, send = call(
        functools.partial(weight_kernel, T),
        (shape((3, 4, R, D), f32), shape((3, 4, R, D), bf16)),
        [ids, normed_ffn, active, ginner, branch, cot_all, ctx_all],
        scratch=[
            pltpu.VMEM((4, 2, R, D), f32),
            pltpu.VMEM((2, 4, R, D), f32),
            pltpu.VMEM((4, 2, R, D), f32),
        ],
        mib=24,
        us=5,
    )

    RR = R // 4
    if fast:
        far, near, p1, p2, p3, wown = call(
            join_kernel,
            (shape((4 * R, D), bf16), shape((4 * R, D), f32)) + (shape((R, D), bf16),) * 3 + (shape((R, D), f32),),
            [ids, keep, core_move(send)],
            scratch=[pltpu.VMEM((4, 4, RR, D), f32)],
        )
        middle_more = plane_move(far, 2)
        first_rows, second_rows = call(
            rows_kernel,
            (shape((R, 3 * CG), f32), shape((R, D), f32)),
            [ids] + ws + list(ms) + mo,
            scratch=[pltpu.VMEM((4, R, 3 * CG), f32), pltpu.VMEM((4, 2, R0, F0 // 2), f32)],
            us=1,
        )
        got = list(after(tuple(got), far, p1, second_rows))
        ps = [group_move(p, k) for k, p in ((1, p1), (2, p2), (3, p3))]
    if fast:
        back_outs = (
            shape((4 * T, CG), bf16),
            shape((HG, 4 * T, 128), bf16),
            shape((HG, 4 * T, 128), bf16),
            shape((HG, 5, T, T), f32),
        )
        back_scratch = [pltpu.VMEM((C * 4, T, 128), f32), pltpu.VMEM((HG, 8 * T, 128), f32)]
    else:
        back_outs = (
            shape((4 * T, CG), bf16),
            shape((C, HG, 4 * T, 128), f32),
            shape((HG, 5, T, T), f32),
        )
        back_scratch = [pltpu.VMEM((C * 4, T, 128), f32)]
    back = call(
        functools.partial(backward_kernel, T, C, fast),
        back_outs,
        [ids, q_at, k_at, query, seg_q, seg_k, tiles, lse] + got + blocks,
        scalars=3,
        scratch=back_scratch,
        mib=20 if fast else 56,
        us=30000,
    )
    if fast:
        dq, down, doth, sums = back
        doth = after(doth, *ps)
        dmore = core_move(doth)
        keep_p, send_p = call(
            functools.partial(project_grad_kernel, T),
            (shape((4, R, 3 * CG), f32), shape((4 * R, 3 * CG), bf16)),
            [ids, normed, dq, down, doth],
            scratch=[pltpu.VMEM((4, 2, R, 3 * CG), f32)],
        )
        RB = R + RR * D // (3 * CG)
        project_more = core_move(send_p)
    else:
        dq, dall, sums = back
        down = lax.psum_scatter(dall, "seq", scatter_dimension=0, axis_index_groups=members)
        down, dmore = down.astype(bf16), jnp.zeros((HG, 4 * T, 128), bf16)

    table_row = call(functools.partial(table_kernel, T), shape((1, 32 * H), f32), [ids, sums])
    small = shape((8, 3 * CG), f32), shape((16, 3 * CG), bf16)
    extra, extra_send = call(extra_kernel, small, [table_row], scalars=0, us=1)
    if fast:
        RB = R + RR * D // (3 * CG)
        extra, middle_more = after((extra, middle_more), middle_more)
        project_far, project_near, extra = call(
            project_join_kernel,
            (shape((2 * RB + 16, 3 * CG), bf16),)
            + (shape((2 * RB, 3 * CG), f32), shape((8, 3 * CG), f32)),
            [ids, keep_p, project_more, extra, core_move(extra_send), wown] + ps,
            scratch=[pltpu.VMEM((4, 4, RR, 3 * CG), f32), pltpu.VMEM((4, RR, D), f32)],
            us=1,
        )
        dmore = after(dmore, project_far)
    own, s1, s2, s3, joined = call(
        functools.partial(tail_kernel, T),
        (shape((T, D), f32),)
        + (shape((2 * T, D), bf16),) * 3
        + (shape((4 * T, 3 * CG), bf16),),
        [ids, x_all, dq, down, dmore, grads, gains] + ws + wo + list(res_send),
        scratch=[pltpu.VMEM((4, 2, RH, 3 * CG), bf16), pltpu.VMEM((4, T, D), f32)],
    )
    if fast:
        middle_send, middle_mine = call(
            middle_half_kernel,
            (shape((2 * R, D), bf16), shape((2 * R, D), f32)),
            [near, middle_more],
            scalars=0,
            us=1,
        )
        project_more = plane_move(project_far, 1)
        middle_send = after(middle_send, project_more)
        middle_last = plane_move(middle_send, 1)
        send, mine, extra = call(
            project_half_kernel,
            (shape((RB + 16, 3 * CG), bf16), shape((RB, 3 * CG), f32), shape((8, 3 * CG), f32)),
            [after(project_near, middle_send), project_more, extra],
            scalars=0,
            us=1,
        )
        more = plane_move(send, 2)
        s1, s2, s3 = after((s1, s2, s3), project_far)
    parts = [group_move(v, k) for k, v in ((1, s1), (2, s2), (3, s3))]
    input_gradient = own + parts[0][:T].astype(f32) + parts[1][:T].astype(f32) + parts[2][:T].astype(f32)
    result = res0 + parts[0][T:].astype(f32) + parts[1][T:].astype(f32) + parts[2][T:].astype(f32)
    if fast:
        inner_mine, outer_mine, second_sums = call(
            middle_sum_kernel,
            (shape((R, D), f32), shape((R, D), bf16), shape((R, 1), f32)),
            [middle_mine, middle_last, second_rows],
            scalars=0,
            us=1,
        )
        pairs = []
        for a in range(GROUPS):
            for b in range(C):
                for z in range(fsdps):
                    pairs.append(((a * C + b) * fsdps + z, ((a ^ z) * C + b) * fsdps + z))
        outer_got = lax.ppermute(outer_mine, ("seq", "fsdp"), pairs)
        wide = 3 * CG + D + 128
        t1, t2, t3, tmine, extra, output_grad = call(
            project_plane_kernel,
            (shape((RR + 8, wide), bf16),) * 3
            + (shape((RR, wide), f32), shape((8, 3 * CG), f32), shape((RR, D), f32)),
            [ids, mine, more, extra, inner_mine, second_sums, first_rows],
            scratch=[
                pltpu.VMEM((4, RR, 3 * CG), f32),
                pltpu.VMEM((4, RR, D), f32),
                pltpu.VMEM((4, RR, 128), f32),
            ],
            us=1,
        )
        ts = [group_move(t, k) for k, t in ((1, t1), (2, t2), (3, t3))]
        where = jnp.stack([g, position * fsdps + f]).astype(jnp.int32)
        count = D // (seqs * fsdps)
        query_grad, key_grad, value_grad, inner_grad, first_grad, second_grad, table_grad, outer_grad = call(
            final_kernel,
            (shape((RR, D), f32),) * 3
            + (shape((RR, 4 * F0), f32), shape((1, count), f32), shape((1, count), f32), shape((H, 32), f32))
            + (shape((R, D), f32),),
            [where, tmine] + ts + [extra, outer_got, gains],
            scratch=[pltpu.VMEM((4, RR, wide), f32), pltpu.VMEM((D // count, count), f32)],
            us=1,
        )
        first_grad, second_grad = first_grad.reshape(count), second_grad.reshape(count)
        table_grad = table_grad.T
    else:
        FB = F0 // 8
        axes = ("seq", "fsdp")

        def product(left, right):
            return lax.optimization_barrier(mm(left, right, TN))

        def spread(whole, axis):
            blocks = []
            for z in range(4):
                for e in range(2):
                    block = lax.slice_in_dim(whole, (4 * e + z) * FB, (4 * e + z + 1) * FB, axis=axis)
                    blocks += [block * (b == (z ^ g)).astype(f32) for b in range(4)]
            return jnp.concatenate(blocks, axis=axis)

        inner_p = product(normed_ffn, ginner)
        inner_w = spread(inner_p, 1)
        outer_w = spread(product(active, cot_all.reshape(4 * T, D)), 0)
        out_w = jnp.zeros((4, CG, D), f32)
        for k in range(4):
            out_w = lax.dynamic_update_slice_in_dim(out_w, product(ctx_all[k], branch)[None], k, 0)
        joined_w = product(normed, joined)
        pairs_w = joined_w[:, : 2 * CG].reshape(D, HG, 2, DH)

        def whole(part):
            return lax.dynamic_update_slice(jnp.zeros((D, D), f32), part.reshape(D, CG), (0, g * CG))

        def scatter(part):
            return lax.psum_scatter(part, axes, scatter_dimension=0, tiled=True)

        query_grad = scatter(whole(joined_w[:, 2 * CG :]))
        key_grad = scatter(whole(pairs_w[:, :, 0]))
        value_grad = scatter(whole(pairs_w[:, :, 1]))
        output_grad = scatter(out_w.reshape(D, D))
        inner_grad = scatter(inner_w)
        outer_grad = scatter(outer_w)
        extra = lax.psum(extra, axes)
        order = f ^ jnp.arange(4)

        def by_plane(slots, low, high):
            return jnp.stack([v[low:high] for v in slots])[order].astype(f32)

        pair = jnp.stack([by_plane(ws, 0, RH), by_plane(wo, 0, RH)], axis=1).reshape(D, 3 * CG)
        first_vec = jnp.sum(pair * joined_w, axis=1)
        wide = jnp.concatenate([by_plane(v, R0, 2 * R0).reshape(D, F0 // 2) for v in (ms, mo)], axis=1)
        second_vec = jnp.sum(wide * inner_p, axis=1)
        first_vec = lax.psum(first_vec, axes) / gains[0]
        second_vec = lax.psum(second_vec, axes) / gains[1]
        at = position * fsdps + f
        count = D // (seqs * fsdps)
        second_grad = lax.dynamic_slice_in_dim(second_vec, at * count, count)
        first_grad = lax.dynamic_slice_in_dim(first_vec, at * count, count)
        table_grad = extra[0, : 32 * H].reshape(H, 32).T
    return (
        result[None],
        input_gradient[None],
        first_grad,
        query_grad,
        key_grad,
        value_grad,
        output_grad,
        table_grad,
        second_grad,
        inner_grad,
        outer_grad,
    )


def solution(mesh):
    return jax.shard_map(
        functools.partial(on_device, mesh.shape["seq"], mesh.shape["fsdp"]),
        mesh=mesh,
        in_specs=(
            P("fsdp", "seq", None),
            P("fsdp", "seq"),
            P("fsdp", "seq", None),
            P("fsdp"),
            P("fsdp", None),
            P("fsdp", None),
            P("fsdp", None),
            P("fsdp", None),
            P("fsdp", None),
            P("fsdp"),
            P("fsdp", None),
            P("fsdp", None),
        ),
        out_specs=(
            P("fsdp", "seq", None),
            P("fsdp", "seq", None),
            P(("seq", "fsdp")),
            P(("seq", "fsdp"), None),
            P(("seq", "fsdp"), None),
            P(("seq", "fsdp"), None),
            P(("seq", "fsdp"), None),
            P(),
            P(("seq", "fsdp")),
            P(("seq", "fsdp"), None),
            P(("seq", "fsdp"), None),
        ),
        check_vma=False,
    )
```

```python
import functools

import jax
import jax.numpy as jnp
from jax import lax
from jax.experimental import pallas as pl
from jax.experimental.pallas import tpu as pltpu
from jax.sharding import PartitionSpec as P

D = 768
H = 12
DH = 64
GROUPS = 4
HG = H // GROUPS
CG = HG * DH

epsilon = 1e-06
FORCE_GENERIC = False
SCALE = 10**6
neg_fill = -1e30
limits = (12, 16, 23, 32, 46, 64, 91)
root_half = 0.7071067811865476
inv_root_tau = 0.3989422804014327
bf16 = jnp.bfloat16
f32 = jnp.float32
NT = (((1,), (1,)), ((), ()))
TN = (((0,), (0,)), ((), ()))
NN = (((1,), (0,)), ((), ()))


def mm(a, b, dims=NN):
    return lax.dot_general(a, b, dims, preferred_element_type=f32)


def bucket_of(offset):
    distance = jnp.abs(offset)
    farther = jnp.zeros_like(offset) + 8
    for limit in limits:
        farther = farther + (distance >= limit).astype(jnp.int32)
    nearer = jnp.where(distance < 8, distance, farther)
    return nearer + jnp.where(offset > 0, 16, 0)


def call(kernel, outs, args, scalars=1, scratch=(), mib=12, us=2, far=()):
    vmem = pl.BlockSpec(memory_space=pltpu.VMEM)
    smem = pl.BlockSpec(memory_space=pltpu.SMEM)
    hbm = pl.BlockSpec(memory_space=pltpu.HBM)
    return pl.pallas_call(
        kernel,
        out_shape=outs,
        in_specs=[smem] * scalars + [hbm if n in far else vmem for n in range(scalars, len(args))],
        out_specs=jax.tree.map(lambda _: vmem, outs),
        scratch_shapes=scratch,
        compiler_params=pltpu.CompilerParams(vmem_limit_bytes=mib << 20),
        cost_estimate=pl.CostEstimate(flops=us * SCALE, bytes_accessed=1 << 10, transcendentals=0),
    )(*args)


def shape(dims, kind):
    return jax.ShapeDtypeStruct(dims, kind)


def project_kernel(T, fast, ids, *refs):
    half, f = ids[1], ids[2]
    ws, os = refs[0:4], refs[4:8]
    xs = [refs[8].at[k] for k in range(4)]
    if fast:
        xs += [refs[9].at[k] for k in range(4)]
    normed, kv, query, marks, gains, W, small = refs[-7:]
    rows = W.shape[2]
    for k in range(4):
        z = f ^ k
        W[z, half] = ws[k][:rows, :]
        W[z, 1 - half] = os[k][:rows, :]
        small[z] = ws[k][rows:, :].astype(f32)
    gain = jnp.concatenate([small[z, 0:1, 0 : D // 4] for z in range(4)], axis=1)
    gains[0:1, :] = gain
    gains[1:2, :] = jnp.concatenate([small[z, 1:2, 0 : D // 4] for z in range(4)], axis=1)
    weight = W[...].reshape(D, 3 * CG)
    count = len(xs)
    seg = [xs[k][T:, :].astype(f32)[0:1, :128] for k in range(count)]
    marks[...] = jnp.concatenate(seg + [jnp.zeros((8 - count, 128), f32)] * (count < 8), axis=0)
    for i in range(count // 2):
        parts = []
        for k in (2 * i, 2 * i + 1):
            x = xs[k][:T, :].astype(f32)
            s = lax.rsqrt(jnp.mean(x * x, axis=-1, keepdims=True) + epsilon)
            parts.append((x * s * gain).astype(bf16))
        n = jnp.concatenate(parts, axis=0)
        at = slice(2 * i * T, (2 * i + 2) * T)
        normed[at, :] = n
        out = mm(n, weight if i < 2 else weight[:, : 2 * CG])
        for h in range(HG):
            kv[h, at, :] = out[:, 128 * h : 128 * h + 128].astype(bf16)
        if i < 2:
            blank = jnp.zeros((2 * T, DH), f32)
            for h in range(HG):
                q = out[:, 2 * CG + DH * h : 2 * CG + DH * (h + 1)]
                query[h, at, :] = jnp.concatenate([q, blank], axis=1).astype(bf16)


def tiles_kernel(T, ids, w0, w1, w2, w3, tiles, small):
    g, f = ids[0], ids[2]
    rows = w0.shape[0] - 16
    for k, w in enumerate((w0, w1, w2, w3)):
        small[f ^ k] = w[rows:, :].astype(f32)
    table = jnp.concatenate([small[z, 8:16, 0:128] for z in range(4)], axis=0)
    lane = lax.broadcasted_iota(jnp.int32, (32, 128), 1)
    m = lax.broadcasted_iota(jnp.int32, (32, 2 * T), 1)
    label = lax.broadcasted_iota(jnp.int32, (32, 2 * T), 0)
    for h in range(HG):
        column = jnp.sum(jnp.where(lane == HG * g + h, table, 0.0), axis=1, keepdims=True)
        for d in range(5):
            if d in (0, 4):
                one = column[15 if d == 0 else 31 :][:1, :]
                tiles[h, d] = jnp.broadcast_to(one, (T, T))
                continue
            offset = T * (d - 2) - jnp.where(m < T, m, m - 2 * T)
            hot = jnp.where(bucket_of(offset) == label, column, 0.0)
            along = jnp.sum(hot, axis=0, keepdims=True)
            wide = jnp.broadcast_to(along, (T, 2 * T))
            tiles[h, d] = pltpu.roll(wide, 0, 1, stride=1, stride_axis=0)[:, :T]


def tile_of(key_at, query_at):
    return jnp.clip(key_at - query_at, -2, 2) + 2


def mark_columns(T, count, marks, columns):
    across = jnp.concatenate([marks[...], jnp.zeros((128 - marks.shape[0], 128), f32)], axis=0).T
    for t in range(count):
        columns[t] = jnp.broadcast_to(across[:, t : t + 1], (T, 128))


def masked_scores(T, scores, base, pair, h, q_at, k_at, seg_q, columns, tiles):
    pieces = []
    for t in range(8):
        kt = base + t
        bias = jnp.concatenate([tiles[h, tile_of(k_at[kt], q_at[2 * pair + j])] for j in range(2)], axis=1)
        column = jnp.concatenate([columns[kt], columns[kt]], axis=1)
        piece = scores[t * T : (t + 1) * T] + bias
        pieces.append(jnp.where(column == seg_q, piece, neg_fill))
    return jnp.concatenate(pieces, axis=0)


def pick_keys(blocks, i, h):
    if len(blocks[0].shape) == 3:
        return blocks[0][h]
    return jnp.concatenate([blocks[0][2 * i, h], blocks[0][2 * i + 1, h]], axis=0)


def forward_kernel(T, nb, fast, ids, q_at, k_at, query, seg_q, seg_k, tiles, *rest):
    blocks, (context, lse, columns) = rest[:-3], rest[-3:]
    mark_columns(T, nb * 4, seg_k, columns)

    def pair_step(pair, carry):
        at = pl.ds(pl.multiple_of(pair * 2 * T, 2 * T), 2 * T)
        seg = jnp.concatenate([seg_q[pl.ds(2 * pair + j, 1), :] for j in range(2)], axis=1)
        out = []
        for h in range(HG):
            q = query[h, at, :]

            def chunk(i, state):
                peak, total, acc = state
                keys = pick_keys(blocks, i, h)
                s = masked_scores(T, mm(keys, q, NT), 8 * i, pair, h, q_at, k_at, seg, columns, tiles)
                top = jnp.maximum(peak, jnp.max(s, axis=0, keepdims=True))
                p = jnp.exp(s - top)
                fade = jnp.exp(peak - top)
                total = total * fade + jnp.sum(p, axis=0, keepdims=True)
                acc = acc * fade + mm(keys, p.astype(bf16), TN)
                return top, total, acc

            start = (
                jnp.full((1, 2 * T), neg_fill, f32),
                jnp.zeros((1, 2 * T), f32),
                jnp.zeros((128, 2 * T), f32),
            )
            if fast:
                peak, total, acc = chunk(0, start)
            else:
                peak, total, acc = lax.fori_loop(0, nb // 2, chunk, start)
            out.append(acc[DH:, :] / total)
            lse[pair, h : h + 1, :] = peak + jnp.log(total)
        joined = jnp.concatenate(out, axis=0)
        context[at, :] = joined.T.astype(bf16)
        return carry

    lax.fori_loop(0, 2, pair_step, 0)


def backward_kernel(T, nb, fast, ids, q_at, k_at, query, seg_q, seg_k, tiles, lse, g0, g1, g2, g3, *rest):
    nin = 1
    blocks = rest[:nin]
    if fast:
        dquery, down, doth, sums, columns, dkv = rest[nin:]
    else:
        dquery, dkv, sums, columns = rest[nin:]
    mark_columns(T, nb * 4, seg_k, columns)
    sums[...] = jnp.zeros_like(sums)
    dkv[...] = jnp.zeros_like(dkv)

    def pair_step(pair, carry):
        at = pl.ds(pl.multiple_of(pair * 2 * T, 2 * T), 2 * T)
        seg = jnp.concatenate([seg_q[pl.ds(2 * pair + j, 1), :] for j in range(2)], axis=1)
        grad = g0[at, :].astype(f32) + g1[at, :].astype(f32) + g2[at, :].astype(f32) + g3[at, :].astype(f32)
        blank = jnp.zeros((2 * T, DH), f32)
        out = []
        for h in range(HG):
            q = query[h, at, :]
            do = jnp.concatenate([blank, grad[:, DH * h : DH * (h + 1)]], axis=1).astype(bf16)
            row = lse[pair, h : h + 1, :]

            def probs_of(i):
                keys = pick_keys(blocks, i, h)
                s = masked_scores(T, mm(keys, q, NT), 8 * i, pair, h, q_at, k_at, seg, columns, tiles)
                return keys, jnp.exp(s - row), mm(keys, do, NT)

            def finish(i, keys, p, dp, delta):
                ds = p * (dp - delta)
                for t in range(8):
                    for j in range(2):
                        index = tile_of(k_at[8 * i + t], q_at[2 * pair + j])
                        sums[h, index] += ds[t * T : (t + 1) * T, j * T : (j + 1) * T]
                ds = ds.astype(bf16)
                both = jnp.concatenate([ds, p.astype(bf16)], axis=1)
                piece = mm(both, jnp.concatenate([q, do], axis=0))
                if fast:
                    dkv[h] += piece
                else:
                    dkv[2 * i, h] += piece[: 4 * T]
                    dkv[2 * i + 1, h] += piece[4 * T :]
                return mm(keys, ds, TN)[:DH, :]

            if fast:
                keys, p, dp = probs_of(0)
                delta = jnp.sum(p * dp, axis=0, keepdims=True)
                dq = finish(0, keys, p, dp, delta)
            else:

                def first(i, delta):
                    keys, p, dp = probs_of(i)
                    return delta + jnp.sum(p * dp, axis=0, keepdims=True)

                delta = lax.fori_loop(0, nb // 2, first, jnp.zeros((1, 2 * T), f32))

                def second(i, dq):
                    keys, p, dp = probs_of(i)
                    return dq + finish(i, keys, p, dp, delta)

                dq = lax.fori_loop(0, nb // 2, second, jnp.zeros((DH, 2 * T), f32))
            out.append(dq)
        dquery[at, :] = jnp.concatenate(out, axis=0).T.astype(bf16)
        return carry

    lax.fori_loop(0, 2, pair_step, 0)
    if fast:
        for h in range(HG):
            down[h] = dkv[h, : 4 * T, :].astype(bf16)
            doth[h] = dkv[h, 4 * T :, :].astype(bf16)


def exact_mm(value, chosen):
    high = value.astype(bf16)
    low = (value - high.astype(f32)).astype(bf16)
    return mm(high, chosen) + mm(low, chosen)


def table_kernel(T, ids, sums, out):
    g = ids[0]
    row = lax.broadcasted_iota(jnp.int32, (T, T), 0)
    lane = lax.broadcasted_iota(jnp.int32, (T, T), 1)
    mirror = (row + lane == T - 1).astype(bf16)
    blank = jnp.zeros((T, T), f32)
    offset = lax.broadcasted_iota(jnp.int32, (2 * T, 128), 0) - (T - 1)
    label = lax.broadcasted_iota(jnp.int32, (2 * T, 128), 1)
    label8 = lax.broadcasted_iota(jnp.int32, (8, 128), 1)
    total = jnp.zeros((8, 128), f32)
    for d in range(5):
        lines = []
        for h in range(HG):
            if d in (0, 4):
                lines.append(jnp.sum(sums[h, d], axis=0, keepdims=True))
            else:
                moved = jnp.concatenate([exact_mm(sums[h, d], mirror), blank], axis=1)
                moved = pltpu.roll(moved, 0, 1, stride=1, stride_axis=0)
                lines.append(jnp.sum(moved, axis=0, keepdims=True))
        block = jnp.concatenate(lines + [jnp.zeros((8 - HG, lines[0].shape[1]), f32)], axis=0)
        if d in (0, 4):
            whole = jnp.sum(block, axis=1, keepdims=True)
            total = total + jnp.where(label8 == (15 if d == 0 else 31), whole, 0.0)
        else:
            total = total + exact_mm(block, (bucket_of(offset + T * (d - 2)) == label).astype(bf16))
    pieces = []
    for a in range(GROUPS):
        for h in range(HG):
            pieces.append(jnp.where(g == a, total[h : h + 1, :32], 0.0))
    out[...] = jnp.concatenate(pieces, axis=1)


def middle_kernel(T, ids, *refs):
    g, half, f = ids[0], ids[1], ids[2]
    x, ctx, gains = refs[0:3]
    cots, ws, others = refs[3:7], refs[7:11], refs[11:15]
    res0, sends, gcs = refs[15], refs[16:19], refs[19:23]
    grads, normed, active, ginner, branch, cot_all = refs[23:29]
    WO, W1, W2, held = refs[29:33]
    for k in range(4):
        cot_all[g ^ k] = cots[k][...]
    rows, low = WO.shape[2], WO.shape[2] // 2
    FH = W1.shape[3]
    for k in range(4):
        z = f ^ k
        for at, pieces in ((half, ws), (1 - half, others)):
            piece = pieces[k]
            WO[z, at] = piece[:rows]
            W1[at, z] = piece[rows : 2 * rows]
            W2[at, z, :, 0 : D // 2] = piece[2 * rows : 2 * rows + low]
            W2[at, z, :, D // 2 :] = piece[2 * rows + low :]
    gain = gains[1:2, :]

    def out_rows(a):
        return jnp.concatenate([WO[a, 0], WO[a, 1]], axis=1)

    for i in range(2):
        at = slice(2 * i * T, (2 * i + 2) * T)
        slots = (2 * i, 2 * i + 1)
        att = jnp.concatenate([x[m, :T, :] for m in slots], axis=0).astype(f32)
        cot = jnp.concatenate([cot_all[m] for m in slots], axis=0)
        for a in range(4):
            att = att + mm(ctx[a, at, :], out_rows(a))
        s = lax.rsqrt(jnp.mean(att * att, axis=-1, keepdims=True) + epsilon)
        n = (att * s * gain).astype(bf16)
        normed[at, :] = n
        result = None
        gn = None
        for c in range(2):
            columns = slice(c * FH, (c + 1) * FH)
            w1 = W1[c].reshape(D, FH)
            w2 = W2[c].reshape(FH, D)
            inner = mm(n, w1)
            cdf = 0.5 * (1.0 + lax.erf(inner * root_half))
            act = (inner * cdf).astype(bf16)
            slope = cdf + inner * jnp.exp(-0.5 * inner * inner) * inv_root_tau
            part = mm(act, w2)
            result = part if result is None else result + part
            ga = mm(cot, w2, NT).astype(bf16)
            gi = (ga.astype(f32) * slope).astype(bf16)
            part = mm(gi, w1, NT)
            gn = part if gn is None else gn + part
            active[at, columns] = act
            ginner[at, columns] = gi
        for index, m in enumerate(slots):
            held[m] = result[index * T : (index + 1) * T]

            @pl.when(g == m)
            def _():
                held[m] += att[index * T : (index + 1) * T]

        u = gn * gain
        grad = 0.25 * cot.astype(f32) + s * u - att * (s * s * s) * jnp.mean(u * att, axis=-1, keepdims=True)
        grads[at, :] = grad
        gb = grad.astype(bf16)
        branch[at, :] = gb
        for k in range(4):
            gcs[k][at, :] = mm(gb, out_rows(g ^ k), NT).astype(bf16)
    res0[...] = held[g]
    for k in (1, 2, 3):
        sends[k - 1][...] = held[g ^ k].astype(bf16)


def weight_kernel(T, ids, normed, active, ginner, branch, cot, ctx, keep, send, gi, go, gw):
    c = ids[3]
    R = D // 8
    gi[...] = mm(normed[...], ginner[...], TN).reshape(4, 2, R, D)
    go[...] = mm(active[...], cot[...].reshape(4 * T, D), TN).reshape(2, 4, R, D)
    gb = branch[...]
    for a in range(4):
        gw[a] = mm(ctx[a], gb, TN).reshape(2, R, D)
    for a in range(4):
        keep[0, a] = gi[a, c]
        keep[1, a] = go[c, a]
        keep[2, a] = gw[a, c]
        send[0, a] = gi[a, 1 - c].astype(bf16)
        send[1, a] = go[1 - c, a].astype(bf16)
        send[2, a] = gw[a, 1 - c].astype(bf16)


def tail_kernel(T, ids, x_all, dq, down, doth, grads, gains, *refs):
    g, half, f = ids[0], ids[1], ids[2]
    ws, os, rs = refs[0:4], refs[4:8], refs[8:11]
    own, s1, s2, s3, joined, W, held = refs[11:]
    rows = W.shape[2]
    sends = (s1, s2, s3)
    for k in range(4):
        z = f ^ k
        W[z, half] = ws[k][:rows, :]
        W[z, 1 - half] = os[k][:rows, :]
    weight = W[...].reshape(D, 3 * CG)
    gain = gains[0:1, :]
    for i in range(2):
        at = slice(2 * i * T, (2 * i + 2) * T)
        parts = [(down[h, at, :].astype(f32) + doth[h, at, :].astype(f32)).astype(bf16) for h in range(HG)]
        dqkv = jnp.concatenate(parts + [dq[at, :]], axis=1)
        joined[at, :] = dqkv
        gn = mm(dqkv, weight, NT)
        x = jnp.concatenate([x_all[m, :T, :] for m in (2 * i, 2 * i + 1)], axis=0).astype(f32)
        s = lax.rsqrt(jnp.mean(x * x, axis=-1, keepdims=True) + epsilon)
        u = gn * gain
        total = grads[at, :] + s * u - x * (s * s * s) * jnp.mean(u * x, axis=-1, keepdims=True)
        for index, m in enumerate((2 * i, 2 * i + 1)):
            held[m] = total[index * T : (index + 1) * T]
    own[...] = held[g]
    for k in (1, 2, 3):
        sends[k - 1][:T, :] = held[g ^ k].astype(bf16)
        sends[k - 1][T:, :] = rs[k - 1][...]


def split_rows(value):
    high = value.astype(bf16)
    return jnp.concatenate([high, (value - high.astype(f32)).astype(bf16)], axis=0)


def project_grad_kernel(T, ids, normed, dq, down, doth, keep, e0, e1, gw):
    c = ids[3]
    R = D // 8
    own = jnp.concatenate([down[h] for h in range(HG)], axis=1)
    other = jnp.concatenate([doth[h] for h in range(HG)], axis=1)
    pairs = mm(normed[...], jnp.concatenate([own, other], axis=0), TN)
    single = mm(normed[: 4 * T, :], dq[...], TN)
    gw[...] = jnp.concatenate([pairs, single], axis=1).reshape(4, 2, R, 3 * CG)
    for a in range(4):
        keep[a] = gw[a, c]
        (e0, e1)[a // 2][a % 2] = gw[a, 1 - c].astype(bf16)


def extra_kernel(table, block, send):
    rows = jnp.concatenate([table[...], jnp.zeros((1, 3 * CG - 32 * H), f32)], axis=1)
    rows = jnp.concatenate([rows, jnp.zeros((7, 3 * CG), f32)], axis=0)
    block[...] = rows
    send[...] = split_rows(rows)


def start_steps(T, C, ids, q, k, v, first, second, table, x, seg, out, x_out, small, held, gain1, gain2, rows8, marks, sems):
    place = lax.axis_index("seq")
    g = lax.div(place, C)
    side = lax.rem(place, C) if ids is None else ids[1]
    rows = out.shape[0] - 16
    at = pl.ds(pl.multiple_of(side * rows, rows), rows)
    lanes = pl.ds(pl.multiple_of(128 * (g + lax.div(g, 2)), 128), 256)
    pairs = [(w.at[at, lanes], held.at[n]) for n, w in enumerate((q, k, v))]
    pairs += [(first, gain1), (second, gain2), (table, rows8), (seg, marks), (x.at[0], x_out.at[:T])]
    copies = [pltpu.make_async_copy(a, b, sems.at[n]) for n, (a, b) in enumerate(pairs)]
    for copy in copies:
        copy.start()
    small[...] = jnp.zeros_like(small)
    yield
    for copy in copies:
        copy.wait()
    mark = jnp.concatenate([marks[...].astype(f32), jnp.zeros((15, T), f32)], axis=0)
    x_out[T:, :] = jnp.concatenate([mark, jnp.zeros((16, D - T), f32)], axis=1).astype(bf16)
    small[0:1, 0 : D // 4] = gain1[...].reshape(1, D // 4).astype(f32)
    small[1:2, 0 : D // 4] = gain2[...].reshape(1, D // 4).astype(f32)
    small[8:16, 0:H] = rows8[...].astype(f32)
    out[rows:, :] = small[...].astype(bf16)
    for odd in range(2):

        @pl.when(lax.rem(g, 2) == odd)
        def _():
            pieces = []
            for h in range(HG):
                here = slice(DH * (odd + h), DH * (odd + h + 1))
                pieces += [held[1, :, here], held[2, :, here]]
            pieces.append(held[0, :, DH * odd : DH * odd + CG])
            out[:rows, :] = jnp.concatenate(pieces, axis=1)


def middle_steps(C, ids, wo, inner, outer, out, held, block, sems):
    place, f = lax.axis_index("seq"), lax.axis_index("fsdp")
    g = lax.div(place, C)
    side = lax.rem(place, C) if ids is None else ids[1]
    R0, F0 = wo.shape[0], outer.shape[0]
    FB, low = F0 // 8, R0 // 2
    half = F0 // 2
    pairs = [
        (wo.at[:, pl.ds(pl.multiple_of(side * half, 128), half)], out.at[:R0]),
        (outer.at[pl.ds(pl.multiple_of(side * half + FB * (f ^ g), FB), FB)], block),
    ]
    for z in range(4):
        base = (2 * z + side) * half + 128 * lax.div(z ^ g, 2)
        pairs.append((inner.at[:, pl.ds(pl.multiple_of(base, 128), 256)], held.at[z]))
    copies = [pltpu.make_async_copy(a, b, sems.at[n]) for n, (a, b) in enumerate(pairs)]
    for copy in copies:
        copy.start()
    yield
    for copy in copies:
        copy.wait()
    for a in range(GROUPS):

        @pl.when(g == a)
        def _():
            starts = [FB * (z ^ a) - 128 * ((z ^ a) // 2) for z in range(4)]
            picked = jnp.concatenate([held[z, :, n : n + FB] for z, n in enumerate(starts)], axis=1)
            out[R0 : 2 * R0, :] = picked

    out[2 * R0 : 2 * R0 + low, :] = block[:, : D // 2]
    out[2 * R0 + low :, :] = block[:, D // 2 :]


def start_kernel(T, C, ids, *refs):
    inputs, outputs, scratch = refs[:11], refs[11:14], refs[14:]
    steps = [
        start_steps(T, C, ids, *inputs[:8], *outputs[:2], *scratch[:7]),
        middle_steps(C, ids, *inputs[8:], outputs[2], *scratch[7:]),
    ]
    for step in steps:
        next(step)
    for step in steps:
        next(step, None)


def added(refs):
    value = refs[0][...].astype(f32)
    for r in refs[1:]:
        value = value + r[...].astype(f32)
    return value


def join_kernel(ids, keep, more, far, near, p1, p2, p3, wown, total):
    g, f = ids[0], ids[2]
    R = D // 8
    total[...] = (keep[0] + more[0].astype(f32)).reshape(4, 4, R // 4, D)

    def toward(at):
        right = keep[1, at ^ g] + more[1, at ^ g].astype(f32)
        return [total[a, at] for a in range(4)] + [right]

    far[...] = jnp.concatenate(toward(f ^ 2) + toward(f ^ 3), axis=0).astype(bf16)
    near[...] = jnp.concatenate(toward(f) + toward(f ^ 1), axis=0)
    for k, out in enumerate((wown, p1, p2, p3)):
        out[...] = (keep[2, g ^ k] + more[2, g ^ k].astype(f32)).astype(out.dtype)


def middle_half_kernel(near, more, send, mine):
    value = near[...] + more[...].astype(f32)
    count = mine.shape[0]
    mine[...] = value[:count]
    send[...] = value[count:].astype(bf16)


def rows_kernel(ids, *refs):
    qs, ws, os = refs[0:4], refs[4:8], refs[8:12]
    first, second, narrow_rows, wide_rows = refs[12:16]
    half, f, c = ids[1], ids[2], ids[3]
    R = D // 8
    RR, R0 = R // 4, D // 4
    for k in range(4):
        narrow_rows[f ^ k] = qs[k][:R, :].astype(f32)
        for at, pieces in ((half, ws), (1 - half, os)):
            wide_rows[f ^ k, at] = pieces[k][R0 : 2 * R0, :].astype(f32)
    at = pl.ds(pl.multiple_of(RR * f, 8), RR)
    there = pl.ds(pl.multiple_of(R * c + RR * f, 8), RR)
    for a in range(4):
        first[a * RR : (a + 1) * RR, :] = narrow_rows[a, at, :]
        rows = jnp.concatenate([wide_rows[a, 0, there, :], wide_rows[a, 1, there, :]], axis=1)
        second[a * RR : (a + 1) * RR, :] = rows


def middle_sum_kernel(own, more, rows, inner, outer, sums):
    R = D // 8
    value = own[...] + more[...].astype(f32)
    inner[...] = value[:R]
    outer[...] = value[R:].astype(bf16)
    sums[...] = jnp.sum(rows[...] * value[:R], axis=1, keepdims=True)


def unsplit(block):
    return block[:8] + block[8:]


def narrow(block):
    wide = 3 * CG
    right = block[:, wide:]
    rows = block.shape[0] // 3
    folded = jnp.concatenate([right[n * rows : (n + 1) * rows] for n in range(3)], axis=1)
    return jnp.concatenate([block[:, :wide], folded], axis=0)


def widen(block):
    rows = D // 32
    folded = block[rows:]
    wide = D - 3 * CG
    right = jnp.concatenate([folded[:, n * wide : (n + 1) * wide] for n in range(3)], axis=0)
    return jnp.concatenate([block[:rows], right], axis=1)


def project_join_kernel(ids, keep, m0, m1, extra, extra_more, wown, p1, p2, p3, far, near, extra_out, total, out_total):
    f = ids[2]
    R = D // 8
    for a in range(4):
        total[a] = (keep[a] + (m0, m1)[a // 2][a % 2].astype(f32)).reshape(4, R // 4, 3 * CG)
    out_total[...] = added((wown, p1, p2, p3)).reshape(4, R // 4, D)
    ex = extra[...] + unsplit(extra_more[...].astype(f32))
    extra_out[...] = ex

    def toward(at):
        return [total[a, at] for a in range(4)]

    far[: 2 * R, :] = jnp.concatenate(toward(f ^ 1) + toward(f ^ 3), axis=0).astype(bf16)
    data = jnp.concatenate([narrow(out_total[f ^ 1]), narrow(out_total[f ^ 3])], axis=0).astype(bf16)
    far[2 * R : 2 * R + data.shape[0], :] = data
    far[2 * R + data.shape[0] :, :] = split_rows(ex)
    kept = [toward(at) + [narrow(out_total[at])] for at in (f, f ^ 2)]
    near[...] = jnp.concatenate(kept[0] + kept[1], axis=0)


def project_half_kernel(near, more, extra, send, mine, extra_out):
    R = D // 8
    got, tail = more[: 2 * R, :].astype(f32), more[2 * R :, :].astype(f32)
    count = mine.shape[0]
    low = count - R
    ex = extra[...] + unsplit(tail[2 * low :])
    extra_out[...] = ex
    mine[:R, :] = near[:R, :] + got[:R]
    mine[R:, :] = near[R:count, :] + tail[:low]
    send[:R, :] = (near[count : count + R, :] + got[R:]).astype(bf16)
    send[R:count, :] = (near[count + R :, :] + tail[low : 2 * low]).astype(bf16)
    send[count:, :] = split_rows(ex)


def project_plane_kernel(ids, own, more, extra, inner, second, rows, s1, s2, s3, mine, extra_out, output, total, held, sums):
    g = ids[0]
    R = D // 8
    RR = R // 4
    got = more[...].astype(f32)
    value = own[...] + got[: own.shape[0]]
    ex = extra[...] + unsplit(got[own.shape[0] :])
    extra_out[...] = ex
    output[...] = widen(value[R:])
    total[...] = value[:R].reshape(4, RR, 3 * CG)
    held[...] = inner[...].reshape(4, RR, D)
    products = jnp.sum(rows[...] * value[:R], axis=1, keepdims=True)
    lane = lax.broadcasted_iota(jnp.int32, (RR, 128), 1)
    for a in range(4):
        one = products[a * RR : (a + 1) * RR, :]
        two = second[a * RR : (a + 1) * RR, :]
        columns = jnp.zeros((RR, 128), f32)
        for n, part in enumerate((one, two)):
            high = part.astype(bf16).astype(f32)
            columns = jnp.where(lane == 2 * n, high, columns)
            columns = jnp.where(lane == 2 * n + 1, part - high, columns)
        sums[a] = columns
    high = ex.astype(bf16).astype(f32)
    low = ex - high
    width = 3 * CG + D + 128
    tail = jnp.concatenate([high[:, : D // 2], low[:, : D // 2], jnp.zeros((8, width - D), f32)], axis=1)
    for k, out in enumerate((mine, s1, s2, s3)):
        block = jnp.concatenate([total[g ^ k], held[g ^ k], sums[g ^ k]], axis=1)
        out[...] = block if k == 0 else jnp.concatenate([block, tail], axis=0).astype(bf16)


def final_kernel(where, own, r1, r2, r3, extra, outer_in, gains, query, key, value, inner, first, second, table, outer, slots, rows):
    g, at = where[0], where[1]
    RR = D // 32
    ex = extra[...][:, : D // 2]
    slots[g] = own[...]
    for k, r in ((1, r1), (2, r2), (3, r3)):
        got = r[...].astype(f32)
        slots[g ^ k] = got[:RR]
        ex = ex + got[RR:, : D // 2] + got[RR:, D // 2 : D]
    query[...] = jnp.concatenate([slots[a, :, 2 * CG : 3 * CG] for a in range(4)], axis=1)
    for part, out in enumerate((key, value)):
        starts = [128 * h + DH * part for h in range(HG)]
        out[...] = jnp.concatenate([slots[a, :, n : n + DH] for a in range(4) for n in starts], axis=1)
    base = 3 * CG
    for z in range(4):
        for e in range(2):
            n = base + (4 * e + z) * 4 * RR
            inner[:, (8 * z + 4 * e) * 4 * RR : (8 * z + 4 * e + 4) * 4 * RR] = jnp.concatenate(
                [slots[z ^ b, :, n : n + 4 * RR] for b in range(4)], axis=1
            )
    columns = slots[0, :, base + D :] + slots[1, :, base + D :] + slots[2, :, base + D :] + slots[3, :, base + D :]
    square = jnp.concatenate([columns, jnp.zeros((128 - RR, 128), f32)], axis=0).T
    for n, out in enumerate((first, second)):
        whole = gains[n : n + 1, :]
        rows[...] = jnp.concatenate([whole[:, RR * m : RR * (m + 1)] for m in range(D // RR)], axis=0)
        out[...] = (square[2 * n : 2 * n + 1, :RR] + square[2 * n + 1 : 2 * n + 2, :RR]) / rows[pl.ds(at, 1), :]
    table[...] = jnp.concatenate([ex[0:1, 32 * h : 32 * (h + 1)] for h in range(H)], axis=0)
    outer[...] = outer_in[...].astype(f32)


def on_device(seqs, fsdps, *args):
    (
        activations,
        segments,
        cotangent,
        attention_gain,
        query_weight,
        key_weight,
        value_weight,
        output_weight,
        bias_table,
        feedforward_gain,
        inner_weight,
        outer_weight,
    ) = args
    T = activations.shape[1]
    C = seqs // GROUPS
    fast = C == 2 and not FORCE_GENERIC
    position = lax.axis_index("seq")
    f = lax.axis_index("fsdp")
    g, c = position // C, position % C
    half = c if fast else 0
    ids = jnp.stack([g, half, f, c]).astype(jnp.int32)
    R0 = query_weight.shape[0]
    RH = R0 // 2
    F0 = outer_weight.shape[0]

    def group_move(value, k):
        pairs = [(a * C + b, (a ^ k) * C + b) for a in range(GROUPS) for b in range(C)]
        return lax.ppermute(value, "seq", pairs)

    def plane_move(value, k):
        return lax.ppermute(value, "fsdp", [(i, i ^ k) for i in range(fsdps)])

    def core_move(value):
        return lax.ppermute(value, "seq", [(i, i ^ 1) for i in range(seqs)])

    def from_group(value):
        return [value] + [group_move(value, k) for k in (1, 2, 3)]

    def from_planes(value):
        return [value] + [plane_move(value, k) for k in (1, 2, 3)]

    def ids_for(side):
        return jnp.stack([g, jnp.asarray(side, jnp.int32), f, c]).astype(jnp.int32)

    def start(side):
        own = fast and side is half
        kernel = functools.partial(start_kernel, T, C)
        return call(
            functools.partial(kernel, None) if own else kernel,
            (shape((RH + 16, 3 * CG), bf16), shape((T + 16, D), bf16), shape((3 * R0, D // 2), bf16)),
            ([] if own else [ids_for(side)])
            + [
                query_weight,
                key_weight,
                value_weight,
                attention_gain,
                feedforward_gain,
                bias_table,
                activations,
                segments,
                output_weight,
                inner_weight,
                outer_weight,
            ],
            scratch=[
                pltpu.VMEM((16, 3 * CG), f32),
                pltpu.VMEM((3, RH, 256), bf16),
                pltpu.VMEM((R0,), bf16),
                pltpu.VMEM((R0,), bf16),
                pltpu.VMEM(bias_table.shape, bf16),
                pltpu.VMEM((1, T), jnp.int32),
                pltpu.SemaphoreType.DMA((8,)),
                pltpu.VMEM((4, R0, 256), bf16),
                pltpu.VMEM((F0 // 8, D), bf16),
                pltpu.SemaphoreType.DMA((6,)),
            ],
            us=1,
            mib=60,
            scalars=0 if own else 1,
            far=range(12),
        )

    def after(values, *earlier):
        return lax.optimization_barrier((values, earlier))[0]

    def ring(value):
        return lax.ppermute(value, "fsdp", [(i, (i + 1) % fsdps) for i in range(fsdps)])

    token_groups = [[a * C + b for a in range(GROUPS)] for b in range(C)]

    def gather(value):
        return lax.all_gather(value, "seq", axis=0, axis_index_groups=token_groups)

    w_pack, x_pack, m_pack = start(half)
    ws = from_planes(w_pack)
    m1, m2 = plane_move(m_pack, 1), plane_move(m_pack, 2)
    x_all = gather(x_pack)
    if fast:
        xo = [core_move(after(x_all, *ws))]
        wo = [core_move(w) for w in ws]
    else:
        xo = []
        wo = from_planes(start(1)[0])

    tiles = call(
        functools.partial(tiles_kernel, T),
        shape((HG, 5, T, T), f32),
        [ids] + ws,
        scratch=[pltpu.VMEM((4, 16, 3 * CG), f32)],
        us=1,
    )
    x_all, tiles = after((x_all, tiles), tiles)
    wide_t = (8 if fast else 4) * T
    normed, kv, query, marks, gains = call(
        functools.partial(project_kernel, T, fast),
        (
            shape((wide_t, D), bf16),
            shape((HG, wide_t, 128), bf16),
            shape((HG, 4 * T, 128), bf16),
            shape((8, 128), f32),
            shape((8, D), f32),
        ),
        [ids] + ws + wo + [x_all] + xo,
        scratch=[pltpu.VMEM((4, 2, RH, 3 * CG), bf16), pltpu.VMEM((4, 16, 3 * CG), f32)],
        us=1,
    )

    cots = from_group(after(cotangent[0], kv))
    slot = jnp.arange(4, dtype=jnp.int32)
    q_at = slot * C + c
    seg_q = marks
    blocks = [kv]
    if fast:
        seg_k = marks
        k_at = jnp.concatenate([slot * C + c, slot * C + 1 - c])
    else:
        members = [[a * C + b for b in range(C)] for a in range(GROUPS)]
        blocks = [lax.all_gather(kv, "seq", axis=0, axis_index_groups=members)]
        seg_k = lax.all_gather(marks[:4].astype(bf16), "seq", axis=0, axis_index_groups=members)
        seg_k = seg_k.reshape(C * 4, T).astype(f32)
        k_at = (slot[None, :] * C + jnp.arange(C, dtype=jnp.int32)[:, None]).reshape(C * 4)
    context, lse = call(
        functools.partial(forward_kernel, T, C, fast),
        (shape((4 * T, CG), bf16), shape((2, 8, 2 * T), f32)),
        [ids, q_at, k_at, query, seg_q, seg_k, tiles] + blocks,
        scalars=3,
        scratch=[pltpu.VMEM((C * 4, T, 128), f32)],
        mib=16 if fast else 48,
        us=1,
    )
    if fast:
        context, m1, m2, cots = after((context, m1, m2, tuple(cots)), context)
        mo = [core_move(m_pack), core_move(m1)]
        m2 = after(m2, *mo)
        m3 = plane_move(m2, 1)
        ctx_all = gather(after(context, *mo, *cots))
        m2, m3 = after((m2, m3), ctx_all)
        mo += [core_move(m2), core_move(m3)]
    else:
        ctx_all = gather(context)
        m3 = plane_move(m2, 1)
        mo = from_planes(start(1)[2])
    ms = (m_pack, m1, m2, m3)

    FH = F0 // 2
    outs = call(
        functools.partial(middle_kernel, T),
        (shape((T, D), f32),)
        + (shape((T, D), bf16),) * 3
        + (shape((4 * T, CG), bf16),) * 4
        + (shape((4 * T, D), f32),)
        + (shape((4 * T, D), bf16),) * 4
        + (shape((4, T, D), bf16),),
        [ids, x_all, ctx_all, gains] + list(cots) + list(ms) + mo,
        scratch=[
            pltpu.VMEM((4, 2, R0, D // 2), bf16),
            pltpu.VMEM((2, 4, R0, FH), bf16),
            pltpu.VMEM((2, 4, F0 // 8, D), bf16),
            pltpu.VMEM((4, T, D), f32),
        ],
        mib=24,
        us=10,
    )
    res0, res_send, gcs = outs[0], outs[1:4], outs[4:8]
    grads, normed_ffn, active, ginner, branch, cot_all = outs[8:14]
    got = [gcs[0]] + [group_move(gcs[k], k) for k in (1, 2, 3)]
    R = D // 8
    keep, send = call(
        functools.partial(weight_kernel, T),
        (shape((3, 4, R, D), f32), shape((3, 4, R, D), bf16)),
        [ids, normed_ffn, active, ginner, branch, cot_all, ctx_all],
        scratch=[
            pltpu.VMEM((4, 2, R, D), f32),
            pltpu.VMEM((2, 4, R, D), f32),
            pltpu.VMEM((4, 2, R, D), f32),
        ],
        mib=24,
        us=5,
    )

    RR = R // 4
    if fast:
        far, near, p1, p2, p3, wown = call(
            join_kernel,
            (shape((4 * R, D), bf16), shape((4 * R, D), f32)) + (shape((R, D), bf16),) * 3 + (shape((R, D), f32),),
            [ids, keep, core_move(send)],
            scratch=[pltpu.VMEM((4, 4, RR, D), f32)],
        )
        middle_more = plane_move(far, 2)
        first_rows, second_rows = call(
            rows_kernel,
            (shape((R, 3 * CG), f32), shape((R, D), f32)),
            [ids] + ws + list(ms) + mo,
            scratch=[pltpu.VMEM((4, R, 3 * CG), f32), pltpu.VMEM((4, 2, R0, F0 // 2), f32)],
            us=1,
        )
        got = list(after(tuple(got), far, p1, second_rows))
        ps = [group_move(p, k) for k, p in ((1, p1), (2, p2), (3, p3))]
    if fast:
        back_outs = (
            shape((4 * T, CG), bf16),
            shape((HG, 4 * T, 128), bf16),
            shape((HG, 4 * T, 128), bf16),
            shape((HG, 5, T, T), f32),
        )
        back_scratch = [pltpu.VMEM((C * 4, T, 128), f32), pltpu.VMEM((HG, 8 * T, 128), f32)]
    else:
        back_outs = (
            shape((4 * T, CG), bf16),
            shape((C, HG, 4 * T, 128), f32),
            shape((HG, 5, T, T), f32),
        )
        back_scratch = [pltpu.VMEM((C * 4, T, 128), f32)]
    back = call(
        functools.partial(backward_kernel, T, C, fast),
        back_outs,
        [ids, q_at, k_at, query, seg_q, seg_k, tiles, lse] + got + blocks,
        scalars=3,
        scratch=back_scratch,
        mib=20 if fast else 56,
        us=30000,
    )
    if fast:
        dq, down, doth, sums = back
        doth = after(doth, *ps)
        dmore = core_move(doth)
        keep_p, *send_p = call(
            functools.partial(project_grad_kernel, T),
            (shape((4, R, 3 * CG), f32),) + (shape((2, R, 3 * CG), bf16),) * 2,
            [ids, normed, dq, down, doth],
            scratch=[pltpu.VMEM((4, 2, R, 3 * CG), f32)],
        )
        RB = R + RR * D // (3 * CG)
        project_more = [core_move(v) for v in send_p]
    else:
        dq, dall, sums = back
        down = lax.psum_scatter(dall, "seq", scatter_dimension=0, axis_index_groups=members)
        down, dmore = down.astype(bf16), jnp.zeros((HG, 4 * T, 128), bf16)

    table_row = call(functools.partial(table_kernel, T), shape((1, 32 * H), f32), [ids, sums])
    small = shape((8, 3 * CG), f32), shape((16, 3 * CG), bf16)
    extra, extra_send = call(extra_kernel, small, [table_row], scalars=0, us=1)
    if fast:
        RB = R + RR * D // (3 * CG)
        project_far, project_near, extra = call(
            project_join_kernel,
            (shape((2 * RB + 16, 3 * CG), bf16),)
            + (shape((2 * RB, 3 * CG), f32), shape((8, 3 * CG), f32)),
            [ids, keep_p] + project_more + [extra, core_move(extra_send), wown] + ps,
            scratch=[pltpu.VMEM((4, 4, RR, 3 * CG), f32), pltpu.VMEM((4, RR, D), f32)],
            us=1,
        )
        dmore = after(dmore, project_far)
    own, s1, s2, s3, joined = call(
        functools.partial(tail_kernel, T),
        (shape((T, D), f32),)
        + (shape((2 * T, D), bf16),) * 3
        + (shape((4 * T, 3 * CG), bf16),),
        [ids, x_all, dq, down, dmore, grads, gains] + ws + wo + list(res_send),
        scratch=[pltpu.VMEM((4, 2, RH, 3 * CG), bf16), pltpu.VMEM((4, T, D), f32)],
    )
    if fast:
        middle_send, middle_mine = call(
            middle_half_kernel,
            (shape((2 * R, D), bf16), shape((2 * R, D), f32)),
            [near, middle_more],
            scalars=0,
            us=1,
        )
        project_more = plane_move(project_far, 1)
        middle_send = after(middle_send, project_more)
        middle_last = plane_move(middle_send, 1)
        send, mine, extra = call(
            project_half_kernel,
            (shape((RB + 16, 3 * CG), bf16), shape((RB, 3 * CG), f32), shape((8, 3 * CG), f32)),
            [after(project_near, middle_send), project_more, extra],
            scalars=0,
            us=1,
        )
        more = plane_move(send, 2)
        s1, s2, s3 = after((s1, s2, s3), project_far)
    parts = [group_move(v, k) for k, v in ((1, s1), (2, s2), (3, s3))]
    input_gradient = own + parts[0][:T].astype(f32) + parts[1][:T].astype(f32) + parts[2][:T].astype(f32)
    result = res0 + parts[0][T:].astype(f32) + parts[1][T:].astype(f32) + parts[2][T:].astype(f32)
    if fast:
        inner_mine, outer_mine, second_sums = call(
            middle_sum_kernel,
            (shape((R, D), f32), shape((R, D), bf16), shape((R, 1), f32)),
            [middle_mine, middle_last, second_rows],
            scalars=0,
            us=1,
        )
        pairs = []
        for a in range(GROUPS):
            for b in range(C):
                for z in range(fsdps):
                    pairs.append(((a * C + b) * fsdps + z, ((a ^ z) * C + b) * fsdps + z))
        outer_got = lax.ppermute(outer_mine, ("seq", "fsdp"), pairs)
        wide = 3 * CG + D + 128
        t1, t2, t3, tmine, extra, output_grad = call(
            project_plane_kernel,
            (shape((RR + 8, wide), bf16),) * 3
            + (shape((RR, wide), f32), shape((8, 3 * CG), f32), shape((RR, D), f32)),
            [ids, mine, more, extra, inner_mine, second_sums, first_rows],
            scratch=[
                pltpu.VMEM((4, RR, 3 * CG), f32),
                pltpu.VMEM((4, RR, D), f32),
                pltpu.VMEM((4, RR, 128), f32),
            ],
            us=1,
        )
        ts = [group_move(t, k) for k, t in ((1, t1), (2, t2), (3, t3))]
        where = jnp.stack([g, position * fsdps + f]).astype(jnp.int32)
        count = D // (seqs * fsdps)
        query_grad, key_grad, value_grad, inner_grad, first_grad, second_grad, table_grad, outer_grad = call(
            final_kernel,
            (shape((RR, D), f32),) * 3
            + (shape((RR, 4 * F0), f32), shape((1, count), f32), shape((1, count), f32), shape((H, 32), f32))
            + (shape((R, D), f32),),
            [where, tmine] + ts + [extra, outer_got, gains],
            scratch=[pltpu.VMEM((4, RR, wide), f32), pltpu.VMEM((D // count, count), f32)],
            us=1,
        )
        first_grad, second_grad = first_grad.reshape(count), second_grad.reshape(count)
        table_grad = table_grad.T
    else:
        FB = F0 // 8
        axes = ("seq", "fsdp")

        def product(left, right):
            return lax.optimization_barrier(mm(left, right, TN))

        def spread(whole, axis):
            blocks = []
            for z in range(4):
                for e in range(2):
                    block = lax.slice_in_dim(whole, (4 * e + z) * FB, (4 * e + z + 1) * FB, axis=axis)
                    blocks += [block * (b == (z ^ g)).astype(f32) for b in range(4)]
            return jnp.concatenate(blocks, axis=axis)

        inner_p = product(normed_ffn, ginner)
        inner_w = spread(inner_p, 1)
        outer_w = spread(product(active, cot_all.reshape(4 * T, D)), 0)
        out_w = jnp.zeros((4, CG, D), f32)
        for k in range(4):
            out_w = lax.dynamic_update_slice_in_dim(out_w, product(ctx_all[k], branch)[None], k, 0)
        joined_w = product(normed, joined)
        pairs_w = joined_w[:, : 2 * CG].reshape(D, HG, 2, DH)

        def whole(part):
            return lax.dynamic_update_slice(jnp.zeros((D, D), f32), part.reshape(D, CG), (0, g * CG))

        def scatter(part):
            return lax.psum_scatter(part, axes, scatter_dimension=0, tiled=True)

        query_grad = scatter(whole(joined_w[:, 2 * CG :]))
        key_grad = scatter(whole(pairs_w[:, :, 0]))
        value_grad = scatter(whole(pairs_w[:, :, 1]))
        output_grad = scatter(out_w.reshape(D, D))
        inner_grad = scatter(inner_w)
        outer_grad = scatter(outer_w)
        extra = lax.psum(extra, axes)
        order = f ^ jnp.arange(4)

        def by_plane(slots, low, high):
            return jnp.stack([v[low:high] for v in slots])[order].astype(f32)

        pair = jnp.stack([by_plane(ws, 0, RH), by_plane(wo, 0, RH)], axis=1).reshape(D, 3 * CG)
        first_vec = jnp.sum(pair * joined_w, axis=1)
        wide = jnp.concatenate([by_plane(v, R0, 2 * R0).reshape(D, F0 // 2) for v in (ms, mo)], axis=1)
        second_vec = jnp.sum(wide * inner_p, axis=1)
        first_vec = lax.psum(first_vec, axes) / gains[0]
        second_vec = lax.psum(second_vec, axes) / gains[1]
        at = position * fsdps + f
        count = D // (seqs * fsdps)
        second_grad = lax.dynamic_slice_in_dim(second_vec, at * count, count)
        first_grad = lax.dynamic_slice_in_dim(first_vec, at * count, count)
        table_grad = extra[0, : 32 * H].reshape(H, 32).T
    return (
        result[None],
        input_gradient[None],
        first_grad,
        query_grad,
        key_grad,
        value_grad,
        output_grad,
        table_grad,
        second_grad,
        inner_grad,
        outer_grad,
    )


def solution(mesh):
    return jax.shard_map(
        functools.partial(on_device, mesh.shape["seq"], mesh.shape["fsdp"]),
        mesh=mesh,
        in_specs=(
            P("fsdp", "seq", None),
            P("fsdp", "seq"),
            P("fsdp", "seq", None),
            P("fsdp"),
            P("fsdp", None),
            P("fsdp", None),
            P("fsdp", None),
            P("fsdp", None),
            P("fsdp", None),
            P("fsdp"),
            P("fsdp", None),
            P("fsdp", None),
        ),
        out_specs=(
            P("fsdp", "seq", None),
            P("fsdp", "seq", None),
            P(("seq", "fsdp")),
            P(("seq", "fsdp"), None),
            P(("seq", "fsdp"), None),
            P(("seq", "fsdp"), None),
            P(("seq", "fsdp"), None),
            P(),
            P(("seq", "fsdp")),
            P(("seq", "fsdp"), None),
            P(("seq", "fsdp"), None),
        ),
        check_vma=False,
    )
```

```python
import functools

import jax
import jax.numpy as jnp
from jax import lax
from jax.experimental import pallas as pl
from jax.experimental.pallas import tpu as pltpu
from jax.sharding import PartitionSpec as P

D = 768
H = 12
DH = 64
GROUPS = 4
HG = H // GROUPS
CG = HG * DH

epsilon = 1e-06
FORCE_GENERIC = False
SCALE = 10**6
neg_fill = -1e30
limits = (12, 16, 23, 32, 46, 64, 91)
root_half = 0.7071067811865476
inv_root_tau = 0.3989422804014327
bf16 = jnp.bfloat16
f32 = jnp.float32
NT = (((1,), (1,)), ((), ()))
TN = (((0,), (0,)), ((), ()))
NN = (((1,), (0,)), ((), ()))


def mm(a, b, dims=NN):
    return lax.dot_general(a, b, dims, preferred_element_type=f32)


def bucket_of(offset):
    distance = jnp.abs(offset)
    farther = jnp.zeros_like(offset) + 8
    for limit in limits:
        farther = farther + (distance >= limit).astype(jnp.int32)
    nearer = jnp.where(distance < 8, distance, farther)
    return nearer + jnp.where(offset > 0, 16, 0)


def call(kernel, outs, args, scalars=1, scratch=(), mib=12, us=2, far=()):
    vmem = pl.BlockSpec(memory_space=pltpu.VMEM)
    smem = pl.BlockSpec(memory_space=pltpu.SMEM)
    hbm = pl.BlockSpec(memory_space=pltpu.HBM)
    return pl.pallas_call(
        kernel,
        out_shape=outs,
        in_specs=[smem] * scalars + [hbm if n in far else vmem for n in range(scalars, len(args))],
        out_specs=jax.tree.map(lambda _: vmem, outs),
        scratch_shapes=scratch,
        compiler_params=pltpu.CompilerParams(vmem_limit_bytes=mib << 20),
        cost_estimate=pl.CostEstimate(flops=us * SCALE, bytes_accessed=1 << 10, transcendentals=0),
    )(*args)


def shape(dims, kind):
    return jax.ShapeDtypeStruct(dims, kind)


def project_kernel(T, fast, ids, *refs):
    half, f = ids[1], ids[2]
    ws, os = refs[0:4], refs[4:8]
    xs = [refs[8].at[k] for k in range(4)]
    if fast:
        xs += [refs[9].at[k] for k in range(4)]
    normed, kv, query, marks, gains, W, small = refs[-7:]
    rows = W.shape[2]
    for k in range(4):
        z = f ^ k
        W[z, half] = ws[k][:rows, :]
        W[z, 1 - half] = os[k][:rows, :]
        small[z] = ws[k][rows:, :].astype(f32)
    gain = jnp.concatenate([small[z, 0:1, 0 : D // 4] for z in range(4)], axis=1)
    gains[0:1, :] = gain
    gains[1:2, :] = jnp.concatenate([small[z, 1:2, 0 : D // 4] for z in range(4)], axis=1)
    weight = W[...].reshape(D, 3 * CG)
    count = len(xs)
    seg = [xs[k][T:, :].astype(f32)[0:1, :128] for k in range(count)]
    marks[...] = jnp.concatenate(seg + [jnp.zeros((8 - count, 128), f32)] * (count < 8), axis=0)
    for i in range(count // 2):
        parts = []
        for k in (2 * i, 2 * i + 1):
            x = xs[k][:T, :].astype(f32)
            s = lax.rsqrt(jnp.mean(x * x, axis=-1, keepdims=True) + epsilon)
            parts.append((x * s * gain).astype(bf16))
        n = jnp.concatenate(parts, axis=0)
        at = slice(2 * i * T, (2 * i + 2) * T)
        normed[at, :] = n
        out = mm(n, weight if i < 2 else weight[:, : 2 * CG])
        for h in range(HG):
            kv[h, at, :] = out[:, 128 * h : 128 * h + 128].astype(bf16)
        if i < 2:
            blank = jnp.zeros((2 * T, DH), f32)
            for h in range(HG):
                q = out[:, 2 * CG + DH * h : 2 * CG + DH * (h + 1)]
                query[h, at, :] = jnp.concatenate([q, blank], axis=1).astype(bf16)


def tiles_kernel(T, ids, w0, w1, w2, w3, tiles, small):
    g, f = ids[0], ids[2]
    rows = w0.shape[0] - 16
    for k, w in enumerate((w0, w1, w2, w3)):
        small[f ^ k] = w[rows:, :].astype(f32)
    table = jnp.concatenate([small[z, 8:16, 0:128] for z in range(4)], axis=0)
    lane = lax.broadcasted_iota(jnp.int32, (32, 128), 1)
    m = lax.broadcasted_iota(jnp.int32, (32, 2 * T), 1)
    label = lax.broadcasted_iota(jnp.int32, (32, 2 * T), 0)
    for h in range(HG):
        column = jnp.sum(jnp.where(lane == HG * g + h, table, 0.0), axis=1, keepdims=True)
        for d in range(5):
            if d in (0, 4):
                one = column[15 if d == 0 else 31 :][:1, :]
                tiles[h, d] = jnp.broadcast_to(one, (T, T))
                continue
            offset = T * (d - 2) - jnp.where(m < T, m, m - 2 * T)
            hot = jnp.where(bucket_of(offset) == label, column, 0.0)
            along = jnp.sum(hot, axis=0, keepdims=True)
            wide = jnp.broadcast_to(along, (T, 2 * T))
            tiles[h, d] = pltpu.roll(wide, 0, 1, stride=1, stride_axis=0)[:, :T]


def tile_of(key_at, query_at):
    return jnp.clip(key_at - query_at, -2, 2) + 2


def mark_columns(T, count, marks, columns):
    across = jnp.concatenate([marks[...], jnp.zeros((128 - marks.shape[0], 128), f32)], axis=0).T
    for t in range(count):
        columns[t] = jnp.broadcast_to(across[:, t : t + 1], (T, 128))


def masked_scores(T, scores, base, pair, h, q_at, k_at, seg_q, columns, tiles):
    pieces = []
    for t in range(8):
        kt = base + t
        bias = jnp.concatenate([tiles[h, tile_of(k_at[kt], q_at[2 * pair + j])] for j in range(2)], axis=1)
        column = jnp.concatenate([columns[kt], columns[kt]], axis=1)
        piece = scores[t * T : (t + 1) * T] + bias
        pieces.append(jnp.where(column == seg_q, piece, neg_fill))
    return jnp.concatenate(pieces, axis=0)


def pick_keys(blocks, i, h):
    if len(blocks[0].shape) == 3:
        return blocks[0][h]
    return jnp.concatenate([blocks[0][2 * i, h], blocks[0][2 * i + 1, h]], axis=0)


def forward_kernel(T, nb, fast, ids, q_at, k_at, query, seg_q, seg_k, tiles, *rest):
    blocks, (context, lse, columns) = rest[:-3], rest[-3:]
    mark_columns(T, nb * 4, seg_k, columns)

    def pair_step(pair, carry):
        at = slice(pair * 2 * T, (pair + 1) * 2 * T)
        seg = jnp.concatenate([seg_q[2 * pair + j : 2 * pair + j + 1, :] for j in range(2)], axis=1)
        out = []
        for h in range(HG):
            q = query[h, at, :]

            def chunk(i, state):
                peak, total, acc = state
                keys = pick_keys(blocks, i, h)
                s = masked_scores(T, mm(keys, q, NT), 8 * i, pair, h, q_at, k_at, seg, columns, tiles)
                top = jnp.maximum(peak, jnp.max(s, axis=0, keepdims=True))
                p = jnp.exp(s - top)
                fade = jnp.exp(peak - top)
                total = total * fade + jnp.sum(p, axis=0, keepdims=True)
                acc = acc * fade + mm(keys, p.astype(bf16), TN)
                return top, total, acc

            start = (
                jnp.full((1, 2 * T), neg_fill, f32),
                jnp.zeros((1, 2 * T), f32),
                jnp.zeros((128, 2 * T), f32),
            )
            if fast:
                peak, total, acc = chunk(0, start)
            else:
                peak, total, acc = lax.fori_loop(0, nb // 2, chunk, start)
            out.append(acc[DH:, :] / total)
            lse[pair, h : h + 1, :] = peak + jnp.log(total)
        joined = jnp.concatenate(out, axis=0)
        context[at, :] = joined.T.astype(bf16)
        return carry

    for pair in range(2):
        pair_step(pair, 0)


def backward_kernel(T, nb, fast, ids, q_at, k_at, query, seg_q, seg_k, tiles, lse, g0, g1, g2, g3, *rest):
    nin = 1
    blocks = rest[:nin]
    if fast:
        dquery, down, doth, sums, columns, dkv = rest[nin:]
    else:
        dquery, dkv, sums, columns = rest[nin:]
    mark_columns(T, nb * 4, seg_k, columns)
    sums[...] = jnp.zeros_like(sums)
    dkv[...] = jnp.zeros_like(dkv)

    def pair_step(pair, carry):
        at = pl.ds(pl.multiple_of(pair * 2 * T, 2 * T), 2 * T)
        seg = jnp.concatenate([seg_q[pl.ds(2 * pair + j, 1), :] for j in range(2)], axis=1)
        grad = g0[at, :].astype(f32) + g1[at, :].astype(f32) + g2[at, :].astype(f32) + g3[at, :].astype(f32)
        blank = jnp.zeros((2 * T, DH), f32)
        out = []
        for h in range(HG):
            q = query[h, at, :]
            do = jnp.concatenate([blank, grad[:, DH * h : DH * (h + 1)]], axis=1).astype(bf16)
            row = lse[pair, h : h + 1, :]

            def probs_of(i):
                keys = pick_keys(blocks, i, h)
                s = masked_scores(T, mm(keys, q, NT), 8 * i, pair, h, q_at, k_at, seg, columns, tiles)
                return keys, jnp.exp(s - row), mm(keys, do, NT)

            def finish(i, keys, p, dp, delta):
                ds = p * (dp - delta)
                for t in range(8):
                    for j in range(2):
                        index = tile_of(k_at[8 * i + t], q_at[2 * pair + j])
                        sums[h, index] += ds[t * T : (t + 1) * T, j * T : (j + 1) * T]
                ds = ds.astype(bf16)
                both = jnp.concatenate([ds, p.astype(bf16)], axis=1)
                piece = mm(both, jnp.concatenate([q, do], axis=0))
                if fast:
                    dkv[h] += piece
                else:
                    dkv[2 * i, h] += piece[: 4 * T]
                    dkv[2 * i + 1, h] += piece[4 * T :]
                return mm(keys, ds, TN)[:DH, :]

            if fast:
                keys, p, dp = probs_of(0)
                delta = jnp.sum(p * dp, axis=0, keepdims=True)
                dq = finish(0, keys, p, dp, delta)
            else:

                def first(i, delta):
                    keys, p, dp = probs_of(i)
                    return delta + jnp.sum(p * dp, axis=0, keepdims=True)

                delta = lax.fori_loop(0, nb // 2, first, jnp.zeros((1, 2 * T), f32))

                def second(i, dq):
                    keys, p, dp = probs_of(i)
                    return dq + finish(i, keys, p, dp, delta)

                dq = lax.fori_loop(0, nb // 2, second, jnp.zeros((DH, 2 * T), f32))
            out.append(dq)
        dquery[at, :] = jnp.concatenate(out, axis=0).T.astype(bf16)
        return carry

    lax.fori_loop(0, 2, pair_step, 0)
    if fast:
        for h in range(HG):
            down[h] = dkv[h, : 4 * T, :].astype(bf16)
            doth[h] = dkv[h, 4 * T :, :].astype(bf16)


def exact_mm(value, chosen):
    high = value.astype(bf16)
    low = (value - high.astype(f32)).astype(bf16)
    return mm(high, chosen) + mm(low, chosen)


def table_kernel(T, ids, sums, out):
    g = ids[0]
    row = lax.broadcasted_iota(jnp.int32, (T, T), 0)
    lane = lax.broadcasted_iota(jnp.int32, (T, T), 1)
    mirror = (row + lane == T - 1).astype(bf16)
    blank = jnp.zeros((T, T), f32)
    offset = lax.broadcasted_iota(jnp.int32, (2 * T, 128), 0) - (T - 1)
    label = lax.broadcasted_iota(jnp.int32, (2 * T, 128), 1)
    label8 = lax.broadcasted_iota(jnp.int32, (8, 128), 1)
    total = jnp.zeros((8, 128), f32)
    for d in range(5):
        lines = []
        for h in range(HG):
            if d in (0, 4):
                lines.append(jnp.sum(sums[h, d], axis=0, keepdims=True))
            else:
                moved = jnp.concatenate([exact_mm(sums[h, d], mirror), blank], axis=1)
                moved = pltpu.roll(moved, 0, 1, stride=1, stride_axis=0)
                lines.append(jnp.sum(moved, axis=0, keepdims=True))
        block = jnp.concatenate(lines + [jnp.zeros((8 - HG, lines[0].shape[1]), f32)], axis=0)
        if d in (0, 4):
            whole = jnp.sum(block, axis=1, keepdims=True)
            total = total + jnp.where(label8 == (15 if d == 0 else 31), whole, 0.0)
        else:
            total = total + exact_mm(block, (bucket_of(offset + T * (d - 2)) == label).astype(bf16))
    pieces = []
    for a in range(GROUPS):
        for h in range(HG):
            pieces.append(jnp.where(g == a, total[h : h + 1, :32], 0.0))
    out[...] = jnp.concatenate(pieces, axis=1)


def middle_kernel(T, ids, *refs):
    g, half, f = ids[0], ids[1], ids[2]
    x, ctx, gains = refs[0:3]
    cots, ws, others = refs[3:7], refs[7:11], refs[11:15]
    res0, sends, gcs = refs[15], refs[16:19], refs[19:23]
    grads, normed, active, ginner, branch, cot_all = refs[23:29]
    WO, W1, W2, held = refs[29:33]
    for k in range(4):
        cot_all[g ^ k] = cots[k][...]
    rows, low = WO.shape[2], WO.shape[2] // 2
    FH = W1.shape[3]
    for k in range(4):
        z = f ^ k
        for at, pieces in ((half, ws), (1 - half, others)):
            piece = pieces[k]
            WO[z, at] = piece[:rows]
            W1[at, z] = piece[rows : 2 * rows]
            W2[at, z, :, 0 : D // 2] = piece[2 * rows : 2 * rows + low]
            W2[at, z, :, D // 2 :] = piece[2 * rows + low :]
    gain = gains[1:2, :]

    def out_rows(a):
        return jnp.concatenate([WO[a, 0], WO[a, 1]], axis=1)

    for i in range(2):
        at = slice(2 * i * T, (2 * i + 2) * T)
        slots = (2 * i, 2 * i + 1)
        att = jnp.concatenate([x[m, :T, :] for m in slots], axis=0).astype(f32)
        cot = jnp.concatenate([cot_all[m] for m in slots], axis=0)
        for a in range(4):
            att = att + mm(ctx[a, at, :], out_rows(a))
        s = lax.rsqrt(jnp.mean(att * att, axis=-1, keepdims=True) + epsilon)
        n = (att * s * gain).astype(bf16)
        normed[at, :] = n
        result = None
        gn = None
        for c in range(2):
            columns = slice(c * FH, (c + 1) * FH)
            w1 = W1[c].reshape(D, FH)
            w2 = W2[c].reshape(FH, D)
            inner = mm(n, w1)
            cdf = 0.5 * (1.0 + lax.erf(inner * root_half))
            act = (inner * cdf).astype(bf16)
            slope = cdf + inner * jnp.exp(-0.5 * inner * inner) * inv_root_tau
            part = mm(act, w2)
            result = part if result is None else result + part
            ga = mm(cot, w2, NT).astype(bf16)
            gi = (ga.astype(f32) * slope).astype(bf16)
            part = mm(gi, w1, NT)
            gn = part if gn is None else gn + part
            active[at, columns] = act
            ginner[at, columns] = gi
        for index, m in enumerate(slots):
            share = (g == m).astype(f32)
            held[m] = result[index * T : (index + 1) * T] + share * att[index * T : (index + 1) * T]
        u = gn * gain
        grad = 0.25 * cot.astype(f32) + s * u - att * (s * s * s) * jnp.mean(u * att, axis=-1, keepdims=True)
        grads[at, :] = grad
        gb = grad.astype(bf16)
        branch[at, :] = gb
        for k in range(4):
            gcs[k][at, :] = mm(gb, out_rows(g ^ k), NT).astype(bf16)
    res0[...] = held[g]
    for k in (1, 2, 3):
        sends[k - 1][...] = held[g ^ k].astype(bf16)


def weight_kernel(T, ids, normed, active, ginner, branch, cot, ctx, keep, send, gi, go, gw):
    c = ids[3]
    R = D // 8
    gi[...] = mm(normed[...], ginner[...], TN).reshape(4, 2, R, D)
    go[...] = mm(active[...], cot[...].reshape(4 * T, D), TN).reshape(2, 4, R, D)
    gb = branch[...]
    for a in range(4):
        gw[a] = mm(ctx[a], gb, TN).reshape(2, R, D)
    for a in range(4):
        keep[0, a] = gi[a, c]
        keep[1, a] = go[c, a]
        keep[2, a] = gw[a, c]
        send[0, a] = gi[a, 1 - c].astype(bf16)
        send[1, a] = go[1 - c, a].astype(bf16)
        send[2, a] = gw[a, 1 - c].astype(bf16)


def tail_kernel(T, ids, x_all, dq, down, doth, grads, gains, *refs):
    g, half, f = ids[0], ids[1], ids[2]
    ws, os, rs = refs[0:4], refs[4:8], refs[8:11]
    own, s1, s2, s3, joined, W, held = refs[11:]
    rows = W.shape[2]
    sends = (s1, s2, s3)
    for k in range(4):
        z = f ^ k
        W[z, half] = ws[k][:rows, :]
        W[z, 1 - half] = os[k][:rows, :]
    weight = W[...].reshape(D, 3 * CG)
    gain = gains[0:1, :]
    for i in range(2):
        at = slice(2 * i * T, (2 * i + 2) * T)
        parts = [(down[h, at, :].astype(f32) + doth[h, at, :].astype(f32)).astype(bf16) for h in range(HG)]
        dqkv = jnp.concatenate(parts + [dq[at, :]], axis=1)
        joined[at, :] = dqkv
        gn = mm(dqkv, weight, NT)
        x = jnp.concatenate([x_all[m, :T, :] for m in (2 * i, 2 * i + 1)], axis=0).astype(f32)
        s = lax.rsqrt(jnp.mean(x * x, axis=-1, keepdims=True) + epsilon)
        u = gn * gain
        total = grads[at, :] + s * u - x * (s * s * s) * jnp.mean(u * x, axis=-1, keepdims=True)
        for index, m in enumerate((2 * i, 2 * i + 1)):
            held[m] = total[index * T : (index + 1) * T]
    own[...] = held[g]
    for k in (1, 2, 3):
        sends[k - 1][:T, :] = held[g ^ k].astype(bf16)
        sends[k - 1][T:, :] = rs[k - 1][...]


def split_rows(value):
    high = value.astype(bf16)
    return jnp.concatenate([high, (value - high.astype(f32)).astype(bf16)], axis=0)


def project_grad_kernel(T, ids, normed, dq, down, doth, keep, e0, e1, gw):
    c = ids[3]
    R = D // 8
    own = jnp.concatenate([down[h] for h in range(HG)], axis=1)
    other = jnp.concatenate([doth[h] for h in range(HG)], axis=1)
    pairs = mm(normed[...], jnp.concatenate([own, other], axis=0), TN)
    single = mm(normed[: 4 * T, :], dq[...], TN)
    gw[...] = jnp.concatenate([pairs, single], axis=1).reshape(4, 2, R, 3 * CG)
    for a in range(4):
        keep[a] = gw[a, c]
        (e0, e1)[a // 2][a % 2] = gw[a, 1 - c].astype(bf16)


def extra_kernel(table, block, send):
    rows = jnp.concatenate([table[...], jnp.zeros((1, 3 * CG - 32 * H), f32)], axis=1)
    rows = jnp.concatenate([rows, jnp.zeros((7, 3 * CG), f32)], axis=0)
    block[...] = rows
    send[...] = split_rows(rows)


def start_steps(T, C, ids, q, k, v, first, second, table, x, seg, out, x_out, small, held, gain1, gain2, rows8, marks, sems):
    place = lax.axis_index("seq")
    g = lax.div(place, C)
    side = lax.rem(place, C) if ids is None else ids[1]
    rows = out.shape[0] - 16
    at = pl.ds(pl.multiple_of(side * rows, rows), rows)
    lanes = pl.ds(pl.multiple_of(128 * (g + lax.div(g, 2)), 128), 256)
    pairs = [(w.at[at, lanes], held.at[n]) for n, w in enumerate((q, k, v))]
    pairs += [(first, gain1), (second, gain2), (table, rows8), (seg, marks), (x.at[0], x_out.at[:T])]
    copies = [pltpu.make_async_copy(a, b, sems.at[n]) for n, (a, b) in enumerate(pairs)]
    for copy in copies:
        copy.start()
    small[...] = jnp.zeros_like(small)
    yield
    for copy in copies:
        copy.wait()
    mark = jnp.concatenate([marks[...].astype(f32), jnp.zeros((15, T), f32)], axis=0)
    x_out[T:, :] = jnp.concatenate([mark, jnp.zeros((16, D - T), f32)], axis=1).astype(bf16)
    small[0:1, 0 : D // 4] = gain1[...].reshape(1, D // 4).astype(f32)
    small[1:2, 0 : D // 4] = gain2[...].reshape(1, D // 4).astype(f32)
    small[8:16, 0:H] = rows8[...].astype(f32)
    out[rows:, :] = small[...].astype(bf16)
    for odd in range(2):

        @pl.when(lax.rem(g, 2) == odd)
        def _():
            pieces = []
            for h in range(HG):
                here = slice(DH * (odd + h), DH * (odd + h + 1))
                pieces += [held[1, :, here], held[2, :, here]]
            pieces.append(held[0, :, DH * odd : DH * odd + CG])
            out[:rows, :] = jnp.concatenate(pieces, axis=1)


def middle_steps(C, ids, wo, inner, outer, out, held, block, sems):
    place, f = lax.axis_index("seq"), lax.axis_index("fsdp")
    g = lax.div(place, C)
    side = lax.rem(place, C) if ids is None else ids[1]
    R0, F0 = wo.shape[0], outer.shape[0]
    FB, low = F0 // 8, R0 // 2
    half = F0 // 2
    pairs = [
        (wo.at[:, pl.ds(pl.multiple_of(side * half, 128), half)], out.at[:R0]),
        (outer.at[pl.ds(pl.multiple_of(side * half + FB * (f ^ g), FB), FB)], block),
    ]
    for z in range(4):
        base = (2 * z + side) * half + 128 * lax.div(z ^ g, 2)
        pairs.append((inner.at[:, pl.ds(pl.multiple_of(base, 128), 256)], held.at[z]))
    copies = [pltpu.make_async_copy(a, b, sems.at[n]) for n, (a, b) in enumerate(pairs)]
    for copy in copies:
        copy.start()
    yield
    for copy in copies:
        copy.wait()
    for a in range(GROUPS):

        @pl.when(g == a)
        def _():
            starts = [FB * (z ^ a) - 128 * ((z ^ a) // 2) for z in range(4)]
            picked = jnp.concatenate([held[z, :, n : n + FB] for z, n in enumerate(starts)], axis=1)
            out[R0 : 2 * R0, :] = picked

    out[2 * R0 : 2 * R0 + low, :] = block[:, : D // 2]
    out[2 * R0 + low :, :] = block[:, D // 2 :]


def start_kernel(T, C, ids, *refs):
    inputs, outputs, scratch = refs[:11], refs[11:14], refs[14:]
    steps = [
        start_steps(T, C, ids, *inputs[:8], *outputs[:2], *scratch[:7]),
        middle_steps(C, ids, *inputs[8:], outputs[2], *scratch[7:]),
    ]
    for step in steps:
        next(step)
    for step in steps:
        next(step, None)


def added(refs):
    value = refs[0][...].astype(f32)
    for r in refs[1:]:
        value = value + r[...].astype(f32)
    return value


def join_kernel(ids, keep, more, far, near, p1, p2, p3, wown, total):
    g, f = ids[0], ids[2]
    R = D // 8
    total[...] = (keep[0] + more[0].astype(f32)).reshape(4, 4, R // 4, D)

    def toward(at):
        right = keep[1, at ^ g] + more[1, at ^ g].astype(f32)
        return [total[a, at] for a in range(4)] + [right]

    far[...] = jnp.concatenate(toward(f ^ 2) + toward(f ^ 3), axis=0).astype(bf16)
    near[...] = jnp.concatenate(toward(f) + toward(f ^ 1), axis=0)
    for k, out in enumerate((wown, p1, p2, p3)):
        out[...] = (keep[2, g ^ k] + more[2, g ^ k].astype(f32)).astype(out.dtype)


def middle_half_kernel(near, more, send, mine):
    value = near[...] + more[...].astype(f32)
    count = mine.shape[0]
    mine[...] = value[:count]
    send[...] = value[count:].astype(bf16)


def rows_kernel(ids, *refs):
    qs, ws, os = refs[0:4], refs[4:8], refs[8:12]
    first, second, narrow_rows, wide_rows = refs[12:16]
    half, f, c = ids[1], ids[2], ids[3]
    R = D // 8
    RR, R0 = R // 4, D // 4
    for k in range(4):
        narrow_rows[f ^ k] = qs[k][:R, :].astype(f32)
        for at, pieces in ((half, ws), (1 - half, os)):
            wide_rows[f ^ k, at] = pieces[k][R0 : 2 * R0, :].astype(f32)
    at = pl.ds(pl.multiple_of(RR * f, 8), RR)
    there = pl.ds(pl.multiple_of(R * c + RR * f, 8), RR)
    for a in range(4):
        first[a * RR : (a + 1) * RR, :] = narrow_rows[a, at, :]
        rows = jnp.concatenate([wide_rows[a, 0, there, :], wide_rows[a, 1, there, :]], axis=1)
        second[a * RR : (a + 1) * RR, :] = rows


def middle_sum_kernel(own, more, rows, inner, outer, sums):
    R = D // 8
    value = own[...] + more[...].astype(f32)
    inner[...] = value[:R]
    outer[...] = value[R:].astype(bf16)
    sums[...] = jnp.sum(rows[...] * value[:R], axis=1, keepdims=True)


def unsplit(block):
    return block[:8] + block[8:]


def narrow(block):
    wide = 3 * CG
    right = block[:, wide:]
    rows = block.shape[0] // 3
    folded = jnp.concatenate([right[n * rows : (n + 1) * rows] for n in range(3)], axis=1)
    return jnp.concatenate([block[:, :wide], folded], axis=0)


def widen(block):
    rows = D // 32
    folded = block[rows:]
    wide = D - 3 * CG
    right = jnp.concatenate([folded[:, n * wide : (n + 1) * wide] for n in range(3)], axis=0)
    return jnp.concatenate([block[:rows], right], axis=1)


def project_join_kernel(ids, keep, m0, m1, extra, extra_more, wown, p1, p2, p3, far, near, extra_out, total, out_total):
    f = ids[2]
    R = D // 8
    for a in range(4):
        total[a] = (keep[a] + (m0, m1)[a // 2][a % 2].astype(f32)).reshape(4, R // 4, 3 * CG)
    out_total[...] = added((wown, p1, p2, p3)).reshape(4, R // 4, D)
    ex = extra[...] + unsplit(extra_more[...].astype(f32))
    extra_out[...] = ex

    def toward(at):
        return [total[a, at] for a in range(4)]

    far[: 2 * R, :] = jnp.concatenate(toward(f ^ 1) + toward(f ^ 3), axis=0).astype(bf16)
    data = jnp.concatenate([narrow(out_total[f ^ 1]), narrow(out_total[f ^ 3])], axis=0).astype(bf16)
    far[2 * R : 2 * R + data.shape[0], :] = data
    far[2 * R + data.shape[0] :, :] = split_rows(ex)
    kept = [toward(at) + [narrow(out_total[at])] for at in (f, f ^ 2)]
    near[...] = jnp.concatenate(kept[0] + kept[1], axis=0)


def project_half_kernel(near, more, extra, send, mine, extra_out):
    R = D // 8
    got, tail = more[: 2 * R, :].astype(f32), more[2 * R :, :].astype(f32)
    count = mine.shape[0]
    low = count - R
    ex = extra[...] + unsplit(tail[2 * low :])
    extra_out[...] = ex
    mine[:R, :] = near[:R, :] + got[:R]
    mine[R:, :] = near[R:count, :] + tail[:low]
    send[:R, :] = (near[count : count + R, :] + got[R:]).astype(bf16)
    send[R:count, :] = (near[count + R :, :] + tail[low : 2 * low]).astype(bf16)
    send[count:, :] = split_rows(ex)


def project_plane_kernel(ids, own, more, extra, inner, second, rows, s1, s2, s3, mine, extra_out, output, total, held, sums):
    g = ids[0]
    R = D // 8
    RR = R // 4
    got = more[...].astype(f32)
    value = own[...] + got[: own.shape[0]]
    ex = extra[...] + unsplit(got[own.shape[0] :])
    extra_out[...] = ex
    output[...] = widen(value[R:])
    total[...] = value[:R].reshape(4, RR, 3 * CG)
    held[...] = inner[...].reshape(4, RR, D)
    products = jnp.sum(rows[...] * value[:R], axis=1, keepdims=True)
    lane = lax.broadcasted_iota(jnp.int32, (RR, 128), 1)
    for a in range(4):
        one = products[a * RR : (a + 1) * RR, :]
        two = second[a * RR : (a + 1) * RR, :]
        columns = jnp.zeros((RR, 128), f32)
        for n, part in enumerate((one, two)):
            high = part.astype(bf16).astype(f32)
            columns = jnp.where(lane == 2 * n, high, columns)
            columns = jnp.where(lane == 2 * n + 1, part - high, columns)
        sums[a] = columns
    high = ex.astype(bf16).astype(f32)
    low = ex - high
    width = 3 * CG + D + 128
    tail = jnp.concatenate([high[:, : D // 2], low[:, : D // 2], jnp.zeros((8, width - D), f32)], axis=1)
    for k, out in enumerate((mine, s1, s2, s3)):
        block = jnp.concatenate([total[g ^ k], held[g ^ k], sums[g ^ k]], axis=1)
        out[...] = block if k == 0 else jnp.concatenate([block, tail], axis=0).astype(bf16)


def final_kernel(where, own, r1, r2, r3, extra, outer_in, gains, query, key, value, inner, first, second, table, outer, slots, rows):
    g, at = where[0], where[1]
    RR = D // 32
    ex = extra[...][:, : D // 2]
    slots[g] = own[...]
    for k, r in ((1, r1), (2, r2), (3, r3)):
        got = r[...].astype(f32)
        slots[g ^ k] = got[:RR]
        ex = ex + got[RR:, : D // 2] + got[RR:, D // 2 : D]
    query[...] = jnp.concatenate([slots[a, :, 2 * CG : 3 * CG] for a in range(4)], axis=1)
    for part, out in enumerate((key, value)):
        starts = [128 * h + DH * part for h in range(HG)]
        out[...] = jnp.concatenate([slots[a, :, n : n + DH] for a in range(4) for n in starts], axis=1)
    base = 3 * CG
    for z in range(4):
        for e in range(2):
            n = base + (4 * e + z) * 4 * RR
            inner[:, (8 * z + 4 * e) * 4 * RR : (8 * z + 4 * e + 4) * 4 * RR] = jnp.concatenate(
                [slots[z ^ b, :, n : n + 4 * RR] for b in range(4)], axis=1
            )
    columns = slots[0, :, base + D :] + slots[1, :, base + D :] + slots[2, :, base + D :] + slots[3, :, base + D :]
    square = jnp.concatenate([columns, jnp.zeros((128 - RR, 128), f32)], axis=0).T
    for n, out in enumerate((first, second)):
        whole = gains[n : n + 1, :]
        rows[...] = jnp.concatenate([whole[:, RR * m : RR * (m + 1)] for m in range(D // RR)], axis=0)
        out[...] = (square[2 * n : 2 * n + 1, :RR] + square[2 * n + 1 : 2 * n + 2, :RR]) / rows[pl.ds(at, 1), :]
    table[...] = jnp.concatenate([ex[0:1, 32 * h : 32 * (h + 1)] for h in range(H)], axis=0)
    outer[...] = outer_in[...].astype(f32)


def on_device(seqs, fsdps, *args):
    (
        activations,
        segments,
        cotangent,
        attention_gain,
        query_weight,
        key_weight,
        value_weight,
        output_weight,
        bias_table,
        feedforward_gain,
        inner_weight,
        outer_weight,
    ) = args
    T = activations.shape[1]
    C = seqs // GROUPS
    fast = C == 2 and not FORCE_GENERIC
    position = lax.axis_index("seq")
    f = lax.axis_index("fsdp")
    g, c = position // C, position % C
    half = c if fast else 0
    ids = jnp.stack([g, half, f, c]).astype(jnp.int32)
    R0 = query_weight.shape[0]
    RH = R0 // 2
    F0 = outer_weight.shape[0]

    def group_move(value, k):
        pairs = [(a * C + b, (a ^ k) * C + b) for a in range(GROUPS) for b in range(C)]
        return lax.ppermute(value, "seq", pairs)

    def plane_move(value, k):
        return lax.ppermute(value, "fsdp", [(i, i ^ k) for i in range(fsdps)])

    def core_move(value):
        return lax.ppermute(value, "seq", [(i, i ^ 1) for i in range(seqs)])

    def from_group(value):
        return [value] + [group_move(value, k) for k in (1, 2, 3)]

    def from_planes(value):
        return [value] + [plane_move(value, k) for k in (1, 2, 3)]

    def ids_for(side):
        return jnp.stack([g, jnp.asarray(side, jnp.int32), f, c]).astype(jnp.int32)

    def start(side):
        own = fast and side is half
        kernel = functools.partial(start_kernel, T, C)
        return call(
            functools.partial(kernel, None) if own else kernel,
            (shape((RH + 16, 3 * CG), bf16), shape((T + 16, D), bf16), shape((3 * R0, D // 2), bf16)),
            ([] if own else [ids_for(side)])
            + [
                query_weight,
                key_weight,
                value_weight,
                attention_gain,
                feedforward_gain,
                bias_table,
                activations,
                segments,
                output_weight,
                inner_weight,
                outer_weight,
            ],
            scratch=[
                pltpu.VMEM((16, 3 * CG), f32),
                pltpu.VMEM((3, RH, 256), bf16),
                pltpu.VMEM((R0,), bf16),
                pltpu.VMEM((R0,), bf16),
                pltpu.VMEM(bias_table.shape, bf16),
                pltpu.VMEM((1, T), jnp.int32),
                pltpu.SemaphoreType.DMA((8,)),
                pltpu.VMEM((4, R0, 256), bf16),
                pltpu.VMEM((F0 // 8, D), bf16),
                pltpu.SemaphoreType.DMA((6,)),
            ],
            us=1,
            mib=60,
            scalars=0 if own else 1,
            far=range(12),
        )

    def after(values, *earlier):
        return lax.optimization_barrier((values, earlier))[0]

    def ring(value):
        return lax.ppermute(value, "fsdp", [(i, (i + 1) % fsdps) for i in range(fsdps)])

    token_groups = [[a * C + b for a in range(GROUPS)] for b in range(C)]

    def gather(value):
        return lax.all_gather(value, "seq", axis=0, axis_index_groups=token_groups)

    w_pack, x_pack, m_pack = start(half)
    ws = from_planes(w_pack)
    m1, m2 = plane_move(m_pack, 1), plane_move(m_pack, 2)
    x_all = gather(x_pack)
    if fast:
        xo = [core_move(after(x_all, *ws))]
        wo = [core_move(w) for w in ws]
    else:
        xo = []
        wo = from_planes(start(1)[0])

    tiles = call(
        functools.partial(tiles_kernel, T),
        shape((HG, 5, T, T), f32),
        [ids] + ws,
        scratch=[pltpu.VMEM((4, 16, 3 * CG), f32)],
        us=1,
    )
    m_other = core_move(m_pack) if fast else None
    x_all, tiles, m_other = after((x_all, tiles, m_other), tiles)
    wide_t = (8 if fast else 4) * T
    normed, kv, query, marks, gains = call(
        functools.partial(project_kernel, T, fast),
        (
            shape((wide_t, D), bf16),
            shape((HG, wide_t, 128), bf16),
            shape((HG, 4 * T, 128), bf16),
            shape((8, 128), f32),
            shape((8, D), f32),
        ),
        [ids] + ws + wo + [x_all] + xo,
        scratch=[pltpu.VMEM((4, 2, RH, 3 * CG), bf16), pltpu.VMEM((4, 16, 3 * CG), f32)],
        us=1,
    )

    cots = from_group(after(cotangent[0], kv))
    slot = jnp.arange(4, dtype=jnp.int32)
    q_at = slot * C + c
    seg_q = marks
    blocks = [kv]
    if fast:
        seg_k = marks
        k_at = jnp.concatenate([slot * C + c, slot * C + 1 - c])
    else:
        members = [[a * C + b for b in range(C)] for a in range(GROUPS)]
        blocks = [lax.all_gather(kv, "seq", axis=0, axis_index_groups=members)]
        seg_k = lax.all_gather(marks[:4].astype(bf16), "seq", axis=0, axis_index_groups=members)
        seg_k = seg_k.reshape(C * 4, T).astype(f32)
        k_at = (slot[None, :] * C + jnp.arange(C, dtype=jnp.int32)[:, None]).reshape(C * 4)
    context, lse = call(
        functools.partial(forward_kernel, T, C, fast),
        (shape((4 * T, CG), bf16), shape((2, 8, 2 * T), f32)),
        [ids, q_at, k_at, query, seg_q, seg_k, tiles] + blocks,
        scalars=3,
        scratch=[pltpu.VMEM((C * 4, T, 128), f32)],
        mib=16 if fast else 48,
        us=1,
    )
    if fast:
        context, m2, cots = after((context, m2, tuple(cots)), context)
        m3 = plane_move(m2, 1)
        ctx_all = gather(after(context, *cots))
        m1, m2, m3 = after((m1, m2, m3), ctx_all)
        mo = [m_other, core_move(m1), core_move(m2), core_move(m3)]
    else:
        ctx_all = gather(context)
        m3 = plane_move(m2, 1)
        mo = from_planes(start(1)[2])
    ms = (m_pack, m1, m2, m3)

    FH = F0 // 2
    outs = call(
        functools.partial(middle_kernel, T),
        (shape((T, D), f32),)
        + (shape((T, D), bf16),) * 3
        + (shape((4 * T, CG), bf16),) * 4
        + (shape((4 * T, D), f32),)
        + (shape((4 * T, D), bf16),) * 4
        + (shape((4, T, D), bf16),),
        [ids, x_all, ctx_all, gains] + list(cots) + list(ms) + mo,
        scratch=[
            pltpu.VMEM((4, 2, R0, D // 2), bf16),
            pltpu.VMEM((2, 4, R0, FH), bf16),
            pltpu.VMEM((2, 4, F0 // 8, D), bf16),
            pltpu.VMEM((4, T, D), f32),
        ],
        mib=24,
        us=10,
    )
    res0, res_send, gcs = outs[0], outs[1:4], outs[4:8]
    grads, normed_ffn, active, ginner, branch, cot_all = outs[8:14]
    got = [gcs[0]] + [group_move(gcs[k], k) for k in (1, 2, 3)]
    R = D // 8
    keep, send = call(
        functools.partial(weight_kernel, T),
        (shape((3, 4, R, D), f32), shape((3, 4, R, D), bf16)),
        [ids, normed_ffn, active, ginner, branch, cot_all, ctx_all],
        scratch=[
            pltpu.VMEM((4, 2, R, D), f32),
            pltpu.VMEM((2, 4, R, D), f32),
            pltpu.VMEM((4, 2, R, D), f32),
        ],
        mib=24,
        us=5,
    )

    RR = R // 4
    if fast:
        far, near, p1, p2, p3, wown = call(
            join_kernel,
            (shape((4 * R, D), bf16), shape((4 * R, D), f32)) + (shape((R, D), bf16),) * 3 + (shape((R, D), f32),),
            [ids, keep, core_move(send)],
            scratch=[pltpu.VMEM((4, 4, RR, D), f32)],
        )
        middle_more = plane_move(far, 2)
        first_rows, second_rows = call(
            rows_kernel,
            (shape((R, 3 * CG), f32), shape((R, D), f32)),
            [ids] + ws + list(ms) + mo,
            scratch=[pltpu.VMEM((4, R, 3 * CG), f32), pltpu.VMEM((4, 2, R0, F0 // 2), f32)],
            us=1,
        )
        got = list(after(tuple(got), far, p1, second_rows))
        ps = [group_move(p, k) for k, p in ((1, p1), (2, p2), (3, p3))]
    if fast:
        back_outs = (
            shape((4 * T, CG), bf16),
            shape((HG, 4 * T, 128), bf16),
            shape((HG, 4 * T, 128), bf16),
            shape((HG, 5, T, T), f32),
        )
        back_scratch = [pltpu.VMEM((C * 4, T, 128), f32), pltpu.VMEM((HG, 8 * T, 128), f32)]
    else:
        back_outs = (
            shape((4 * T, CG), bf16),
            shape((C, HG, 4 * T, 128), f32),
            shape((HG, 5, T, T), f32),
        )
        back_scratch = [pltpu.VMEM((C * 4, T, 128), f32)]
    back = call(
        functools.partial(backward_kernel, T, C, fast),
        back_outs,
        [ids, q_at, k_at, query, seg_q, seg_k, tiles, lse] + got + blocks,
        scalars=3,
        scratch=back_scratch,
        mib=20 if fast else 56,
        us=30000,
    )
    if fast:
        dq, down, doth, sums = back
        doth = after(doth, *ps)
        dmore = core_move(doth)
        keep_p, *send_p = call(
            functools.partial(project_grad_kernel, T),
            (shape((4, R, 3 * CG), f32),) + (shape((2, R, 3 * CG), bf16),) * 2,
            [ids, normed, dq, down, doth],
            scratch=[pltpu.VMEM((4, 2, R, 3 * CG), f32)],
        )
        RB = R + RR * D // (3 * CG)
        project_more = [core_move(v) for v in send_p]
    else:
        dq, dall, sums = back
        down = lax.psum_scatter(dall, "seq", scatter_dimension=0, axis_index_groups=members)
        down, dmore = down.astype(bf16), jnp.zeros((HG, 4 * T, 128), bf16)

    table_row = call(functools.partial(table_kernel, T), shape((1, 32 * H), f32), [ids, sums])
    small = shape((8, 3 * CG), f32), shape((16, 3 * CG), bf16)
    extra, extra_send = call(extra_kernel, small, [table_row], scalars=0, us=1)
    if fast:
        RB = R + RR * D // (3 * CG)
        project_far, project_near, extra = call(
            project_join_kernel,
            (shape((2 * RB + 16, 3 * CG), bf16),)
            + (shape((2 * RB, 3 * CG), f32), shape((8, 3 * CG), f32)),
            [ids, keep_p] + project_more + [extra, core_move(extra_send), wown] + ps,
            scratch=[pltpu.VMEM((4, 4, RR, 3 * CG), f32), pltpu.VMEM((4, RR, D), f32)],
            us=1,
        )
        dmore = after(dmore, project_far)
    own, s1, s2, s3, joined = call(
        functools.partial(tail_kernel, T),
        (shape((T, D), f32),)
        + (shape((2 * T, D), bf16),) * 3
        + (shape((4 * T, 3 * CG), bf16),),
        [ids, x_all, dq, down, dmore, grads, gains] + ws + wo + list(res_send),
        scratch=[pltpu.VMEM((4, 2, RH, 3 * CG), bf16), pltpu.VMEM((4, T, D), f32)],
    )
    if fast:
        middle_send, middle_mine = call(
            middle_half_kernel,
            (shape((2 * R, D), bf16), shape((2 * R, D), f32)),
            [near, middle_more],
            scalars=0,
            us=1,
        )
        project_more = plane_move(project_far, 1)
        middle_last = plane_move(middle_send, 1)
        send, mine, extra = call(
            project_half_kernel,
            (shape((RB + 16, 3 * CG), bf16), shape((RB, 3 * CG), f32), shape((8, 3 * CG), f32)),
            [after(project_near, middle_send), project_more, extra],
            scalars=0,
            us=1,
        )
        more = plane_move(send, 2)
        s1, s2, s3 = after((s1, s2, s3), project_far)
    parts = [group_move(v, k) for k, v in ((1, s1), (2, s2), (3, s3))]
    input_gradient = own + parts[0][:T].astype(f32) + parts[1][:T].astype(f32) + parts[2][:T].astype(f32)
    result = res0 + parts[0][T:].astype(f32) + parts[1][T:].astype(f32) + parts[2][T:].astype(f32)
    if fast:
        inner_mine, outer_mine, second_sums = call(
            middle_sum_kernel,
            (shape((R, D), f32), shape((R, D), bf16), shape((R, 1), f32)),
            [middle_mine, middle_last, second_rows],
            scalars=0,
            us=1,
        )
        pairs = []
        for a in range(GROUPS):
            for b in range(C):
                for z in range(fsdps):
                    pairs.append(((a * C + b) * fsdps + z, ((a ^ z) * C + b) * fsdps + z))
        outer_got = lax.ppermute(outer_mine, ("seq", "fsdp"), pairs)
        wide = 3 * CG + D + 128
        t1, t2, t3, tmine, extra, output_grad = call(
            project_plane_kernel,
            (shape((RR + 8, wide), bf16),) * 3
            + (shape((RR, wide), f32), shape((8, 3 * CG), f32), shape((RR, D), f32)),
            [ids, mine, more, extra, inner_mine, second_sums, first_rows],
            scratch=[
                pltpu.VMEM((4, RR, 3 * CG), f32),
                pltpu.VMEM((4, RR, D), f32),
                pltpu.VMEM((4, RR, 128), f32),
            ],
            us=1,
        )
        ts = [group_move(t, k) for k, t in ((1, t1), (2, t2), (3, t3))]
        where = jnp.stack([g, position * fsdps + f]).astype(jnp.int32)
        count = D // (seqs * fsdps)
        query_grad, key_grad, value_grad, inner_grad, first_grad, second_grad, table_grad, outer_grad = call(
            final_kernel,
            (shape((RR, D), f32),) * 3
            + (shape((RR, 4 * F0), f32), shape((1, count), f32), shape((1, count), f32), shape((H, 32), f32))
            + (shape((R, D), f32),),
            [where, tmine] + ts + [extra, outer_got, gains],
            scratch=[pltpu.VMEM((4, RR, wide), f32), pltpu.VMEM((D // count, count), f32)],
            us=1,
        )
        first_grad, second_grad = first_grad.reshape(count), second_grad.reshape(count)
        table_grad = table_grad.T
    else:
        FB = F0 // 8
        axes = ("seq", "fsdp")

        def product(left, right):
            return lax.optimization_barrier(mm(left, right, TN))

        def spread(whole, axis):
            blocks = []
            for z in range(4):
                for e in range(2):
                    block = lax.slice_in_dim(whole, (4 * e + z) * FB, (4 * e + z + 1) * FB, axis=axis)
                    blocks += [block * (b == (z ^ g)).astype(f32) for b in range(4)]
            return jnp.concatenate(blocks, axis=axis)

        inner_p = product(normed_ffn, ginner)
        inner_w = spread(inner_p, 1)
        outer_w = spread(product(active, cot_all.reshape(4 * T, D)), 0)
        out_w = jnp.zeros((4, CG, D), f32)
        for k in range(4):
            out_w = lax.dynamic_update_slice_in_dim(out_w, product(ctx_all[k], branch)[None], k, 0)
        joined_w = product(normed, joined)
        pairs_w = joined_w[:, : 2 * CG].reshape(D, HG, 2, DH)

        def whole(part):
            return lax.dynamic_update_slice(jnp.zeros((D, D), f32), part.reshape(D, CG), (0, g * CG))

        def scatter(part):
            return lax.psum_scatter(part, axes, scatter_dimension=0, tiled=True)

        query_grad = scatter(whole(joined_w[:, 2 * CG :]))
        key_grad = scatter(whole(pairs_w[:, :, 0]))
        value_grad = scatter(whole(pairs_w[:, :, 1]))
        output_grad = scatter(out_w.reshape(D, D))
        inner_grad = scatter(inner_w)
        outer_grad = scatter(outer_w)
        extra = lax.psum(extra, axes)
        order = f ^ jnp.arange(4)

        def by_plane(slots, low, high):
            return jnp.stack([v[low:high] for v in slots])[order].astype(f32)

        pair = jnp.stack([by_plane(ws, 0, RH), by_plane(wo, 0, RH)], axis=1).reshape(D, 3 * CG)
        first_vec = jnp.sum(pair * joined_w, axis=1)
        wide = jnp.concatenate([by_plane(v, R0, 2 * R0).reshape(D, F0 // 2) for v in (ms, mo)], axis=1)
        second_vec = jnp.sum(wide * inner_p, axis=1)
        first_vec = lax.psum(first_vec, axes) / gains[0]
        second_vec = lax.psum(second_vec, axes) / gains[1]
        at = position * fsdps + f
        count = D // (seqs * fsdps)
        second_grad = lax.dynamic_slice_in_dim(second_vec, at * count, count)
        first_grad = lax.dynamic_slice_in_dim(first_vec, at * count, count)
        table_grad = extra[0, : 32 * H].reshape(H, 32).T
    return (
        result[None],
        input_gradient[None],
        first_grad,
        query_grad,
        key_grad,
        value_grad,
        output_grad,
        table_grad,
        second_grad,
        inner_grad,
        outer_grad,
    )


def solution(mesh):
    return jax.shard_map(
        functools.partial(on_device, mesh.shape["seq"], mesh.shape["fsdp"]),
        mesh=mesh,
        in_specs=(
            P("fsdp", "seq", None),
            P("fsdp", "seq"),
            P("fsdp", "seq", None),
            P("fsdp"),
            P("fsdp", None),
            P("fsdp", None),
            P("fsdp", None),
            P("fsdp", None),
            P("fsdp", None),
            P("fsdp"),
            P("fsdp", None),
            P("fsdp", None),
        ),
        out_specs=(
            P("fsdp", "seq", None),
            P("fsdp", "seq", None),
            P(("seq", "fsdp")),
            P(("seq", "fsdp"), None),
            P(("seq", "fsdp"), None),
            P(("seq", "fsdp"), None),
            P(("seq", "fsdp"), None),
            P(),
            P(("seq", "fsdp")),
            P(("seq", "fsdp"), None),
            P(("seq", "fsdp"), None),
        ),
        check_vma=False,
    )
```
